256 devices in a mesh: wide: 16 (over x, y), narrow: 16 (over z, core).
Axes of the slice: x: 4, y: 4, z: 8, core: 2. Of those that a mesh axis runs over, the one named last changes fastest.
Arguments:
- features: bfloat16 [512, 16, 256, 128], P(('wide', 'narrow'))
- out_cotangent: bfloat16 [512, 16, 256, 128], P(('wide', 'narrow'))
- occupancy: int32 [512, 16, 16], P(('wide', 'narrow')), may hold values from 0 to 65535, as said below
- live_slots: int32 [16, 16], P('wide'), may hold values from 0 to 31, as said below
- neighbours: int32 [256, 27], P('wide'), may hold values from -1 to 255, as said below
- timestep: int32 [1], replicated, may hold values from 0 to 999
- norm_gain: float32 [128], replicated, may hold values from 0.1 to 1.9
- norm_bias: float32 [128], replicated, may hold values from -3 to 3
- film_weight: float32 [256, 256], replicated, may hold values from -0.375 to 0.375
- conv_weight: bfloat16 [27, 128, 128], replicated, may hold values from -0.15625 to 0.15625
- conv_bias: float32 [128], replicated, may hold values from -3 to 3
Outputs:
- mixed: bfloat16 [512, 16, 256, 128], P(('wide', 'narrow'))
- feature_grad: bfloat16 [512, 16, 256, 128], P(('wide', 'narrow'))
- weight_step: float32 [27, 128, 128], replicated
The draws below stay inside these ranges and needn't reach their ends.
Inputs may be any that keep to these rules, and one draw needn't show every extreme that they name: `live_slots`: each row lists 16 distinct slots in rising order; slots not listed have all occupancy words zero. `occupancy`: bit x of a word marks voxel x of that row; every listed block has its centre voxel occupied. `neighbours`: entry 9 (dz + 1) + 3 (dy + 1) + (dx + 1) of a row is the live number of the live block at that block offset, or -1 where no live block lies there; entry 13 is the block itself; the relation is symmetric; the coarse group of a block is its x coordinate among blocks: entries with dx = -1 or dx = 1 name blocks of coarse group w - 1 or w + 1, all other entries name blocks of the same coarse group.
All inputs are finite; a program needn't handle non-finite values.
Results may differ from the reference program's by a relative error of at most 0.0029.
Values may be sent and summed in bfloat16 or wider, within the bound.
No kernel may reach another device: no remote copies, remote signals or barrier semaphores. Data moves between devices by JAX's collectives and lax.ppermute only.
A program may use at most 256 MiB of HBM per device.

```python
import jax
import jax.numpy as jnp
from jax import lax

C = 128
G = 32
TEMB = 256
EDGE = 16
SLOTS = 2
GROUP_LIVE = 16
BLOCKS = 512
N_WIDE = 16
N_NARROW = 16


def rising_scales(key_rows, length):
    ramp = 3.0 ** (jnp.arange(length).astype(jnp.float32) / length)
    spread = jnp.exp(jax.random.uniform(key_rows, (length,), minval=jnp.log(0.5), maxval=jnp.log(2.0)))
    return ramp * spread


def channel_scales(key_chans):
    return jnp.exp(jax.random.uniform(key_chans, (C,), minval=jnp.log(0.5), maxval=jnp.log(2.0)))


def pick_slots(key):
    slot_key = jax.random.fold_in(key, 101)
    group_keys = jax.random.split(slot_key, N_WIDE)

    def one_group(group_key):
        return jnp.sort(jax.random.permutation(group_key, SLOTS * N_NARROW)[:GROUP_LIVE]).astype(jnp.int32)
    return jax.vmap(one_group)(group_keys)


def draw_features(key, part):
    key = jax.random.fold_in(key, 11)
    split_keys = jax.random.split(key, 3)
    row_scale = rising_scales(split_keys[0], BLOCKS)
    chan_scale = channel_scales(split_keys[1])
    shape = (BLOCKS, EDGE, EDGE * EDGE, C)
    base = jax.random.normal(split_keys[2], shape)
    return (base * row_scale[:, None, None, None] * chan_scale).astype(jnp.bfloat16)


def draw_out_cotangent(key, part):
    key = jax.random.fold_in(key, 13)
    split_keys = jax.random.split(key, 3)
    row_scale = rising_scales(split_keys[0], BLOCKS)
    chan_scale = channel_scales(split_keys[1])
    shape = (BLOCKS, EDGE, EDGE * EDGE, C)
    base = jax.random.normal(split_keys[2], shape)
    return (base * row_scale[:, None, None, None] * chan_scale).astype(jnp.bfloat16)


def draw_live_slots(key, part):
    chosen = pick_slots(key)
    return chosen


def draw_occupancy(key, part):
    chosen = pick_slots(key)
    key = jax.random.fold_in(key, 19)
    packed = jax.random.randint(key, (BLOCKS, EDGE, EDGE), 0, 2 ** EDGE)
    middle = EDGE // 2
    centre = (jnp.arange(EDGE)[:, None] == middle) & (jnp.arange(EDGE)[None, :] == middle)
    packed = jnp.where(centre, jnp.bitwise_or(packed, 2 ** middle), packed)
    group_slots = SLOTS * N_NARROW
    global_rows = (chosen + group_slots * jnp.arange(N_WIDE)[:, None]).reshape(-1)
    alive = jnp.zeros((BLOCKS,), jnp.int32).at[global_rows].set(1)
    return (packed * alive[:, None, None]).astype(jnp.int32)


def draw_neighbours(key, part):
    key = jax.random.fold_in(key, 23)
    group_keys = jax.random.split(key, N_WIDE)
    cells = 2 * GROUP_LIVE
    depth_cells = GROUP_LIVE // 2

    def one_group(group_key):
        return jnp.sort(jax.random.permutation(group_key, cells)[:GROUP_LIVE]).astype(jnp.int32)
    chosen = jax.vmap(one_group)(group_keys)
    group_ids = jnp.arange(N_WIDE).astype(jnp.int32)[:, None]
    live_ids = jnp.arange(GROUP_LIVE).astype(jnp.int32)[None, :] + group_ids * GROUP_LIVE
    ordinal = jnp.full((N_WIDE, cells), -1, jnp.int32).at[group_ids, chosen].set(live_ids)
    cell_y = chosen % 4
    cell_z = chosen // 4
    columns = []
    for offset in range(27):
        off_z, off_y, off_x = (offset // 9 - 1, offset // 3 % 3 - 1, offset % 3 - 1)
        near_group = group_ids + off_x + 0 * chosen
        near_y = cell_y + off_y
        near_z = cell_z + off_z
        inside = (near_group >= 0) & (near_group < N_WIDE) & (near_y >= 0) & (near_y < 4) & (near_z >= 0) & (near_z < depth_cells)
        found = ordinal[jnp.clip(near_group, 0, N_WIDE - 1), jnp.clip(near_z * 4 + near_y, 0, cells - 1)]
        columns.append(jnp.where(inside, found, -1))
    return jnp.stack(columns, axis=-1).reshape(N_WIDE * GROUP_LIVE, 27).astype(jnp.int32)


def noise(rng, shape, scale, reach, kind=jnp.bfloat16):
    return jnp.clip(scale * jax.random.normal(rng, shape, jnp.float32), -reach, reach).astype(kind)


def setup_inputs(seed: int = 0) -> dict:
    streams_of = jax.random.split(jax.random.key(seed), 12)
    features = draw_features(jax.random.fold_in(streams_of[11], 71), 0)
    out_cotangent = draw_out_cotangent(jax.random.fold_in(streams_of[11], 71), 0)
    occupancy = draw_occupancy(jax.random.fold_in(streams_of[11], 71), 0)
    live_slots = draw_live_slots(jax.random.fold_in(streams_of[11], 71), 0)
    neighbours = draw_neighbours(jax.random.fold_in(streams_of[11], 71), 0)
    timestep = jax.random.randint(streams_of[5], (1,), 0, 1000).astype(jnp.int32)
    norm_gain = jnp.clip(1.0 + 0.18 * jax.random.normal(streams_of[6], (C,), jnp.float32), 0.1, 1.9)
    norm_bias = noise(streams_of[7], (C,), 0.5, 3.0, jnp.float32)
    film_weight = noise(streams_of[8], (TEMB, 2 * C), TEMB ** -0.5, 0.375, jnp.float32)
    conv_weight = noise(streams_of[9], (27, C, C), (27 * C // 2) ** -0.5, 0.15625)
    conv_bias = noise(streams_of[10], (C,), 0.5, 3.0, jnp.float32)
    return {"features": features, "out_cotangent": out_cotangent, "occupancy": occupancy, "live_slots": live_slots, "neighbours": neighbours, "timestep": timestep, "norm_gain": norm_gain, "norm_bias": norm_bias, "film_weight": film_weight, "conv_weight": conv_weight, "conv_bias": conv_bias}


norm_eps = 1e-05
step_eps = 1e-06

def film_terms(timestep, film_weight):
    half_width = film_weight.shape[0] // 2
    channels = film_weight.shape[1] // 2
    frequencies = jnp.exp(-jnp.log(10000.0) * jnp.arange(half_width).astype(jnp.float32) / half_width)
    angles = timestep.astype(jnp.float32)[0] * frequencies
    embedding = jax.nn.silu(jnp.concatenate([jnp.cos(angles), jnp.sin(angles)]))
    film_out = jnp.dot(embedding[None, :], film_weight, precision=lax.Precision.HIGHEST)[0]
    return (film_out[:channels], film_out[channels:])

def unpack_mask(packed):
    bit_width = packed.shape[-1]
    shifts = jnp.arange(bit_width).astype(jnp.int32)
    bit_values = jnp.bitwise_and(jnp.right_shift(packed[..., None], shifts), 1)
    return bit_values.reshape(packed.shape[:-1] + (bit_width * bit_width, 1)).astype(jnp.float32)

def gather_block(lookup, wanted):
    usable = wanted >= 0
    picked = lookup[jnp.clip(wanted, 0, lookup.shape[0] - 1)]
    picked = jnp.where(usable[:, None, None, None], picked, jnp.zeros_like(picked))
    channels = picked.shape[-1]
    arranged = picked.reshape(3, 3, 3, EDGE, EDGE, EDGE, channels).transpose(0, 3, 1, 4, 2, 5, 6)
    arranged = arranged.reshape(3 * EDGE, 3 * EDGE, 3 * EDGE, channels)
    return arranged[EDGE - 1:2 * EDGE + 1, EDGE - 1:2 * EDGE + 1, EDGE - 1:2 * EDGE + 1]

def tap_offsets(offset, flipped):
    off_z, off_y, off_x = (offset // 9, offset // 3 % 3, offset % 3)
    if flipped:
        return (2 - off_z, 2 - off_y, 2 - off_x)
    return (off_z, off_y, off_x)

def apply_taps(padded, weight, flipped):
    channels = padded.shape[-1]
    running = jnp.zeros((EDGE ** 3, weight.shape[-1]), jnp.float32)
    for offset in range(27):
        off_z, off_y, off_x = tap_offsets(offset, flipped)
        tap_rows = padded[off_z:off_z + EDGE, off_y:off_y + EDGE, off_x:off_x + EDGE].reshape(-1, channels)
        kernel = weight[offset].T if flipped else weight[offset]
        running = running + jnp.dot(tap_rows, kernel, preferred_element_type=jnp.float32)
    return running

def tap_grads(padded, upstream_rows):
    channels = padded.shape[-1]
    grads = []
    for offset in range(27):
        off_z, off_y, off_x = tap_offsets(offset, False)
        tap_rows = padded[off_z:off_z + EDGE, off_y:off_y + EDGE, off_x:off_x + EDGE].reshape(-1, channels)
        grads.append(lax.dot_general(tap_rows, upstream_rows, (((0,), (0,)), ((), ())), preferred_element_type=jnp.float32))
    return jnp.stack(grads)

def reference(features, out_cotangent, occupancy, live_slots, neighbours, timestep, norm_gain, norm_bias, film_weight, conv_weight, conv_bias):
    group_slots = SLOTS * N_NARROW
    live_rows = (live_slots + group_slots * jnp.arange(N_WIDE).astype(jnp.int32)[:, None]).reshape(-1)
    blocks = features[live_rows]
    cotan = out_cotangent[live_rows]
    occupied = unpack_mask(occupancy[live_rows])
    group_width = C // G
    masked = blocks.astype(jnp.float32) * occupied
    first_sums = lax.optimization_barrier(jnp.sum(masked.reshape(-1, G, group_width), axis=(0, 2)))
    squares = lax.optimization_barrier(jnp.sum((masked * blocks.astype(jnp.float32)).reshape(-1, G, group_width), axis=(0, 2)))
    voxel_count = jnp.sum(occupied) * group_width
    group_mean = first_sums / voxel_count
    group_rstd = lax.rsqrt(squares / voxel_count - group_mean * group_mean + norm_eps)
    mean_chan = jnp.repeat(group_mean, group_width)
    rstd_chan = jnp.repeat(group_rstd, group_width)
    film_scale, film_shift = film_terms(timestep, film_weight)

    def pre_terms(block):
        normed = (block.astype(jnp.float32) - mean_chan) * rstd_chan
        return (normed, (normed * norm_gain + norm_bias) * (1.0 + film_scale) + film_shift)

    def activate(pieces):
        block, block_mask = pieces
        return (jax.nn.silu(pre_terms(block)[1]) * block_mask).astype(jnp.bfloat16)
    hidden = lax.map(activate, (blocks, occupied))
    upstream = (cotan.astype(jnp.float32) * occupied).astype(jnp.bfloat16)

    def forward_step(running, pieces):
        block, block_mask, wanted, grad_rows = pieces
        padded = gather_block(hidden, wanted)
        conv_out = apply_taps(padded, conv_weight, False).reshape(block.shape)
        mixed_block = (block.astype(jnp.float32) + (conv_out + conv_bias) * block_mask).astype(jnp.bfloat16)
        running = running + tap_grads(padded, grad_rows.reshape(-1, C))
        return (running, mixed_block)
    weight_total, mixed_live = lax.scan(forward_step, jnp.zeros((27, C, C), jnp.float32), (blocks, occupied, neighbours, upstream))
    weight_step = weight_total * lax.rsqrt(jnp.mean(weight_total * weight_total) + step_eps)

    def back_step(pieces):
        block, block_mask, wanted = pieces
        padded = gather_block(upstream, wanted)
        back_grad = apply_taps(padded, conv_weight, True).reshape(block.shape)
        normed, pre_act = pre_terms(block)
        gate_sig = jax.nn.sigmoid(pre_act)
        grad_hat = back_grad * block_mask * gate_sig * (1.0 + pre_act * (1.0 - gate_sig)) * (1.0 + film_scale) * norm_gain
        return grad_hat
    grad_hat = lax.map(back_step, (blocks, occupied, neighbours))

    def group_terms(pieces):
        block, grad_block = pieces
        normed = pre_terms(block)[0]
        return (lax.optimization_barrier(jnp.sum(grad_block.reshape(-1, G, group_width), axis=(0, 2))), lax.optimization_barrier(jnp.sum((grad_block * normed).reshape(-1, G, group_width), axis=(0, 2))))
    first_parts, second_parts = lax.map(group_terms, (blocks, grad_hat))
    first_chan = jnp.repeat(lax.optimization_barrier(jnp.sum(first_parts, axis=0)), group_width)
    second_chan = jnp.repeat(lax.optimization_barrier(jnp.sum(second_parts, axis=0)), group_width)

    def finish(pieces):
        block, grad_block, block_mask, cot_block = pieces
        normed = pre_terms(block)[0]
        correction = rstd_chan * (grad_block - first_chan / voxel_count - normed * second_chan / voxel_count) * block_mask
        return (cot_block.astype(jnp.float32) + correction).astype(jnp.bfloat16)
    grad_live = lax.map(finish, (blocks, grad_hat, occupied, cotan))
    mixed = features.at[live_rows].set(mixed_live)
    feature_grad = out_cotangent.at[live_rows].set(grad_live)
    return (mixed, feature_grad, weight_step)
```

```python
import functools

import jax
import jax.numpy as jnp
from jax import lax
from jax.experimental import pallas as pl
from jax.experimental.pallas import tpu as pltpu
from jax.sharding import PartitionSpec as P

G = 32
norm_eps = 1e-05
step_eps = 1e-06
MIB = 1 << 20
f32 = jnp.float32
bf16 = jnp.bfloat16

SMEM = pl.BlockSpec(memory_space=pltpu.SMEM)
VMEM = pl.BlockSpec(memory_space=pltpu.VMEM)


def params(limit, semantics=None):
    return pltpu.CompilerParams(vmem_limit_bytes=limit * MIB, dimension_semantics=semantics)


def cost(flops, size):
    return pl.CostEstimate(flops=flops, bytes_accessed=size, transcendentals=0)


def film_terms(timestep, film_weight):
    half_width = film_weight.shape[0] // 2
    channels = film_weight.shape[1] // 2
    frequencies = jnp.exp(
        -jnp.log(10000.0) * jnp.arange(half_width).astype(jnp.float32) / half_width
    )
    angles = timestep.astype(jnp.float32)[0] * frequencies
    embedding = jax.nn.silu(jnp.concatenate([jnp.cos(angles), jnp.sin(angles)]))
    film_out = jnp.dot(embedding[None, :], film_weight, precision=lax.Precision.HIGHEST)[0]
    return (film_out[:channels], film_out[channels:])


def plane_mask(occ_ref, slot, z, edge, channels):
    bit = lax.broadcasted_iota(jnp.int32, (edge, channels), 0)
    rows = [
        jnp.bitwise_and(jnp.right_shift(jnp.full((edge, channels), occ_ref[slot, z, y], jnp.int32), bit), 1)
        for y in range(edge)
    ]
    return jnp.concatenate(rows, axis=0) != 0


def planes_mask(occ_ref, slot, z, count, edge, channels):
    return jnp.concatenate([plane_mask(occ_ref, slot, z + i, edge, channels) for i in range(count)], axis=0)


def x_row(rows, edge, channels):
    return lax.rem(lax.broadcasted_iota(jnp.int32, (rows, channels), 0), edge)


def pieces(value, count):
    found = []
    for _ in range(count):
        part = value.astype(bf16).astype(f32)
        found.append(part)
        value = value - part
    return found


def surface_kernel(edge, with_stats, fill, occ_ref, v_ref, out_ref, plane_s, edge_s, stat_s):
    channels = v_ref.shape[-1]
    last = edge - 1
    slot = pl.program_id(0)

    @pl.when(slot == 0)
    def _():
        stat_s[...] = jnp.zeros_like(stat_s)
        edge_s[...] = jnp.zeros_like(edge_s)

    def coded(z):
        mask = plane_mask(occ_ref, slot, z, edge, channels)
        values = v_ref[0, z].astype(f32)
        return (mask, values, jnp.where(mask, values, fill))

    def step(z, carry):
        mask, values, shown = coded(z)
        plane_s[...] = shown
        for side in range(2):
            row = side * last
            out_ref[z, 4 + 2 * slot + side] = shown[row * edge : (row + 1) * edge].astype(bf16)
            out_ref[z, 8 + 2 * slot + side] = plane_s[pl.ds(row, edge, stride=edge), :].astype(bf16)
        if not with_stats:
            return carry
        total, squares, count = carry
        masked = jnp.where(mask, values, 0.0)
        total = total + jnp.sum(masked, axis=0, keepdims=True)
        squares = squares + jnp.sum(masked * values, axis=0, keepdims=True)
        count = count + jnp.sum(mask.astype(f32), axis=0, keepdims=True)
        return (total, squares, count)

    zero = jnp.zeros((1, channels), f32)
    found = lax.fori_loop(0, edge, step, (zero, zero, zero) if with_stats else 0)
    if with_stats:
        for index in range(3):
            stat_s[index : index + 1, :] = stat_s[index : index + 1, :] + found[index]
    for z_side in range(2):
        _, _, shown = coded(z_side * last)
        for hub in range(edge):
            out_ref[hub, 2 * slot + z_side] = shown[hub * edge : (hub + 1) * edge].astype(bf16)
        for y_side in range(2):
            for hub in range(edge):
                first = y_side * last * edge + hub
                for place in range(2):

                    @pl.when(slot == place)
                    def _():
                        row = 4 * place + 2 * z_side + y_side
                        edge_s[hub, row : row + 1, :] = shown[first : first + 1]

    @pl.when(slot == 1)
    def _():
        if with_stats:
            parts = pieces(stat_s[0:1, :], 3) + pieces(stat_s[1:2, :], 3) + pieces(stat_s[2:3, :], 2)
            for hub in range(edge):
                for row, part in enumerate(parts):
                    edge_s[hub, 8 + row : 9 + row, :] = part
        for hub in range(edge):
            for tile in range(16 // edge):
                out_ref[hub, 12 + tile] = edge_s[hub, tile * edge : (tile + 1) * edge].astype(bf16)


def surface(occupancy, values, fill, with_stats):
    edge, cells, channels = values.shape[1:]
    tiles = 12 + 16 // edge
    return pl.pallas_call(
        functools.partial(surface_kernel, edge, with_stats, fill),
        grid=(2,),
        out_shape=jax.ShapeDtypeStruct((edge, tiles, edge, channels), bf16),
        in_specs=[SMEM, pl.BlockSpec((1, edge, cells, channels), lambda s: (s, 0, 0, 0))],
        out_specs=pl.BlockSpec((edge, tiles, edge, channels), lambda s: (0, 0, 0, 0)),
        scratch_shapes=[
            pltpu.VMEM((cells, channels), f32),
            pltpu.VMEM((edge, 16, channels), f32),
            pltpu.VMEM((8, channels), f32),
        ],
        compiler_params=params(24, ("arbitrary",)),
        cost_estimate=cost(0, 3 * MIB),
        name="surface",
    )(occupancy, values)


def trade_kernel(edge, live_ref, got_ref, left_ref, right_ref, stat_ref, ends_s):
    live_count = live_ref.shape[1]
    for k in range(live_count):
        slot = live_ref[0, k]
        owner, local = slot // 2, lax.rem(slot, 2)
        for side, out in ((0, left_ref), (1, right_ref)):
            out[k] = got_ref[owner, 8 + 2 * local + side]
            for z_side in range(2):
                tile = got_ref[owner, 2 * local + z_side].astype(f32)
                row = 2 * k + z_side
                x = side * (edge - 1)
                ends_s[side, row : row + 1, :] = tile[x : x + 1]
    for side, out in ((0, left_ref), (1, right_ref)):
        for tile in range(2 * live_count // edge):
            out[live_count + tile] = ends_s[side, tile * edge : (tile + 1) * edge].astype(bf16)
    rows = []
    for tile in range(8 // edge if edge < 16 else 0, 16 // edge):
        total = got_ref[0, 12 + tile].astype(f32)
        for source in range(1, edge):
            total = total + got_ref[source, 12 + tile].astype(f32)
        rows.append(total)
    rows = jnp.concatenate(rows, axis=0)
    if edge == 16:
        rows = rows[8:]
    stat_ref[...] = jnp.zeros_like(stat_ref)
    stat_ref[0:1, :] = rows[0:1] + rows[1:2] + rows[2:3]
    stat_ref[1:2, :] = rows[3:4] + rows[4:5] + rows[5:6]
    stat_ref[2:3, :] = rows[6:7] + rows[7:8]


def trade(live_slots, got):
    edge, channels = got.shape[2], got.shape[-1]
    live_count = live_slots.shape[1]
    tiles = live_count + 2 * live_count // edge
    payload = jax.ShapeDtypeStruct((tiles, edge, channels), bf16)
    return pl.pallas_call(
        functools.partial(trade_kernel, edge),
        out_shape=(payload, payload, jax.ShapeDtypeStruct((8, channels), f32)),
        in_specs=[SMEM, VMEM],
        out_specs=(VMEM, VMEM, VMEM),
        scratch_shapes=[pltpu.VMEM((2, 2 * live_count, channels), f32)],
        compiler_params=params(16),
        cost_estimate=cost(0, 2 * MIB),
        name="trade",
    )(live_slots, got)


def hub_kernel(edge, fill, place_ref, live_ref, near_ref, got_ref, lower_ref, upper_ref, out_ref, wide_s, rows_s):
    live_count = live_ref.shape[1]
    last = edge - 1
    hub, group = place_ref[0], place_ref[1]
    x_refs = (lower_ref, upper_ref)
    for side in range(2):
        wide_s[side] = x_refs[side][...].astype(f32)

    def entry(k, dz, dy, dx):
        number = near_ref[k, 9 * (dz + 1) + 3 * (dy + 1) + (dx + 1)]
        index = jnp.clip(number - (group + dx) * live_count, 0, live_count - 1)
        return (number >= 0, index)

    def own(k, dz, dy):
        there, index = entry(k, dz, dy, 0)
        slot = live_ref[0, index]
        return (there, slot // 2, lax.rem(slot, 2))

    def step(k, carry):
        slot = live_ref[0, k]
        owner, local = slot // 2, lax.rem(slot, 2)

        def put(tile, there, values):
            out_ref[owner, local, tile] = jnp.where(there, values, fill).astype(bf16)

        def put_row(row, there, values):
            rows_s[row : row + 1, :] = jnp.where(there, values, fill)

        for side in range(2):
            step_to = 2 * side - 1
            there, source, place = own(k, step_to, 0)
            put(side, there, got_ref[source, 2 * place + 1 - side].astype(f32))
            there, source, place = own(k, 0, step_to)
            put(2 + side, there, got_ref[source, 4 + 2 * place + 1 - side].astype(f32))
            there, index = entry(k, 0, 0, step_to)
            put(4 + side, there, wide_s[side, index])
        dz_corner = jnp.where(hub == last, -1, 1)
        for a in range(2):
            for b in range(2):
                there, source, place = own(k, 2 * a - 1, 2 * b - 1)
                row = 4 * place + 2 * (1 - a) + (1 - b)
                tile = got_ref[source, 12 + row // edge].astype(f32)
                picked = lax.broadcasted_iota(jnp.int32, tile.shape, 0) == lax.rem(row, edge)
                put_row(2 * a + b, there, jnp.sum(jnp.where(picked, tile, 0.0), axis=0, keepdims=True))
                there, index = entry(k, 2 * a - 1, 0, 2 * b - 1)
                row = 2 * index + (1 - a)
                tile = wide_s[b, live_count + row // edge]
                picked = lax.broadcasted_iota(jnp.int32, tile.shape, 0) == lax.rem(row, edge)
                put_row(4 + 2 * a + b, there, jnp.sum(jnp.where(picked, tile, 0.0), axis=0, keepdims=True))
                row = last if a == 0 else 0
                there, index = entry(k, 0, 2 * a - 1, 2 * b - 1)
                put_row(8 + 2 * a + b, there, wide_s[b, index, row : row + 1, :])
                there, index = entry(k, dz_corner, 2 * a - 1, 2 * b - 1)
                put_row(12 + 2 * a + b, there, wide_s[b, index, row : row + 1, :])
        for tile in range(16 // edge):
            out_ref[owner, local, 6 + tile] = rows_s[tile * edge : (tile + 1) * edge].astype(bf16)
        return carry

    lax.fori_loop(0, live_count, step, 0)


def hub_rows(place, live_slots, neighbours, got, lower, upper, fill):
    edge, channels = got.shape[2], got.shape[-1]
    return pl.pallas_call(
        functools.partial(hub_kernel, edge, fill),
        out_shape=jax.ShapeDtypeStruct((edge, 2, 6 + 16 // edge, edge, channels), bf16),
        in_specs=[SMEM, SMEM, SMEM, VMEM, VMEM, VMEM],
        out_specs=VMEM,
        scratch_shapes=[
            pltpu.VMEM((2,) + lower.shape, f32),
            pltpu.VMEM((16, channels), f32),
        ],
        compiler_params=params(16),
        cost_estimate=cost(0, 8 * MIB),
        name="hub_rows",
    )(place, live_slots, neighbours, got, lower, upper)


def exchange(values, axis):
    return lax.all_to_all(values, axis, split_axis=0, concat_axis=0, tiled=True)


def hub_stage(place, live_slots, neighbours, got, fill):
    to_left, to_right, stats = trade(live_slots, got)
    count = lax.axis_size("wide")
    lower = lax.ppermute(to_right, "wide", [(i, i + 1) for i in range(count - 1)])
    upper = lax.ppermute(to_left, "wide", [(i + 1, i) for i in range(count - 1)])
    return (hub_rows(place, live_slots, neighbours, got, lower, upper, fill), stats)


def coefficients(coef_ref):
    return [coef_ref[i : i + 1, :] for i in range(5)]


def set_halo(edge, rim_ref, pad_ref, pad_lead, shift_ref, shift_lead, xh_s, edge_s, change):
    last = edge - 1
    for hub in range(edge):
        tiles = [change(rim_ref[hub, 0, tile].astype(f32)) for tile in range(6 + 16 // edge)]
        for side in range(2):
            pad_ref[pad_lead + (side * (edge + 1), hub + 1)] = tiles[side].astype(bf16)
            pad_ref[pad_lead + (hub + 1, side * (edge + 1))] = tiles[2 + side].astype(bf16)
            xh_s[side, hub + 1, 8 : 8 + edge, :] = tiles[4 + side]

        def row(index):
            tile = tiles[6 + index // edge]
            return tile[index % edge : index % edge + 1]

        for a in range(2):
            for b in range(2):
                edge_s[2 * a + b, hub : hub + 1, :] = row(2 * a + b)
                xh_s[b, a * (edge + 1), 8 + hub : 9 + hub, :] = row(4 + 2 * a + b)
                y = 8 + edge if a else 7
                xh_s[b, hub + 1, y : y + 1, :] = row(8 + 2 * a + b)
                if hub == last:
                    xh_s[b, 0, y : y + 1, :] = row(12 + 2 * a + b)
                if hub == 0:
                    xh_s[b, edge + 1, y : y + 1, :] = row(12 + 2 * a + b)
    for a in range(2):
        for b in range(2):
            pad_ref[pad_lead + (a * (edge + 1), b * (edge + 1))] = edge_s[2 * a + b].astype(bf16)
    for side in range(2):
        for z in range(edge + 2):
            for y in range(3):
                shift_ref[shift_lead + (side, y, z)] = xh_s[side, z, 7 + y : 7 + y + edge, :].astype(bf16)


def hidden_plane(feats, mask, coef):
    mean, rstd, scale, shift = coef[:4]
    pre = (feats - mean) * rstd * scale + shift
    return jnp.where(mask, pre * jax.nn.sigmoid(pre), 0.0)


def weight_kernel(edge, occ_ref, live_ref, f_ref, g_ref, rim_ref, coef_ref, grad_ref, pad_ref, shift_ref,
                  hid_ref, acc_s, even_s, odd_s, xh_s, edge_s, plane_s, face_s):
    channels = f_ref.shape[-1]
    cells = edge * edge
    slot = pl.program_id(0)
    coef = coefficients(coef_ref)
    depth = min(4, edge // 2)
    chunks = edge // depth

    @pl.when(slot == 0)
    def _():
        acc_s[...] = jnp.zeros_like(acc_s)

    @pl.when(live_ref[slot] != 0)
    def _():
        set_halo(edge, rim_ref, pad_ref, (0,), shift_ref, (0,), xh_s, edge_s, lambda v: v)
        lane_x = lax.rem(lax.broadcasted_iota(jnp.int32, (channels, cells), 1), edge)

        def fill(z, carry):
            mask = plane_mask(occ_ref, slot, z, edge, channels)
            ups = jnp.where(mask, g_ref[0, z].astype(f32), 0.0).astype(bf16)
            pad_ref[0, z + 1, 1 : edge + 1] = ups.reshape(edge, edge, channels)
            return carry

        lax.fori_loop(0, edge, fill, 0)

        def prepare(chunk, flip_s):
            for part in range(depth):
                z = chunk * depth + part
                mask = plane_mask(occ_ref, slot, z, edge, channels)
                hidden = hidden_plane(f_ref[0, z].astype(f32), mask, coef).astype(bf16)
                hid_ref[0, z] = hidden
                hidden = hidden.astype(f32)
                plane_s[part] = hidden
                for side in range(2):
                    face_s[side, pl.ds(z * edge, edge), :] = plane_s[
                        part, pl.ds(side * (edge - 1), edge, stride=edge), :
                    ]
                flat = hidden.T
                before = jnp.where(lane_x == edge - 1, 0.0, pltpu.roll(flat, cells - 1, 1))
                after = jnp.where(lane_x == 0, 0.0, pltpu.roll(flat, 1, 1))
                columns = slice(part * cells, (part + 1) * cells)
                flip_s[0:channels, columns] = before.astype(bf16)
                flip_s[channels : 2 * channels, columns] = flat.astype(bf16)
                flip_s[2 * channels : 3 * channels, columns] = after.astype(bf16)

        def add(tap, px, values):
            pz, py = tap // 3, tap % 3
            offset = 9 * (2 - pz) + 3 * (2 - py) + (2 - px)
            acc_s[offset] = acc_s[offset] + values

        pairs = [(0, 1), (2, 3), (4, 5), (6, 7), (8,)]

        def multiply(chunk, flip_s):
            z0 = chunk * depth
            left = flip_s[...]
            for pair in pairs:
                right = [
                    pad_ref[0, pl.ds(z0 + tap // 3, depth), tap % 3 : tap % 3 + edge].reshape(
                        depth * cells, channels
                    )
                    for tap in pair
                ]
                right = right[0] if len(right) == 1 else jnp.concatenate(right, axis=1)
                found = jnp.dot(left, right, preferred_element_type=f32)
                for place, tap in enumerate(pair):
                    for px in range(3):
                        add(
                            tap,
                            px,
                            found[
                                px * channels : (px + 1) * channels,
                                place * channels : (place + 1) * channels,
                            ],
                        )

        prepare(0, even_s)

        def two(i, carry):
            prepare(2 * i + 1, odd_s)
            multiply(2 * i, even_s)
            prepare(jnp.minimum(2 * i + 2, chunks - 1), even_s)
            multiply(2 * i + 1, odd_s)
            return carry

        lax.fori_loop(0, chunks // 2, two, 0)
        for side in range(2):
            left = face_s[side].T.astype(bf16)
            for tap in range(9):
                right = shift_ref[0, side, tap % 3, tap // 3 : tap // 3 + edge].reshape(cells, channels)
                add(tap, 2 * side, jnp.dot(left, right, preferred_element_type=f32))

    @pl.when(slot == 1)
    def _():
        grad_ref[...] = acc_s[...]


def weight_grad(occupancy, live, features, cotangent, rim, coef):
    edge, channels = features.shape[1], features.shape[-1]
    cells = edge * edge
    wide = edge + 2
    whole = pl.BlockSpec((1, edge, cells, channels), lambda s: (s, 0, 0, 0))
    return pl.pallas_call(
        functools.partial(weight_kernel, edge),
        grid=(2,),
        out_shape=(
            jax.ShapeDtypeStruct((27, channels, channels), f32),
            jax.ShapeDtypeStruct((2, wide, wide, edge, channels), bf16),
            jax.ShapeDtypeStruct((2, 2, 3, wide, edge, channels), bf16),
            jax.ShapeDtypeStruct(features.shape, bf16),
        ),
        in_specs=[
            SMEM,
            SMEM,
            whole,
            whole,
            pl.BlockSpec((edge, 1) + rim.shape[2:], lambda s: (0, s, 0, 0, 0)),
            pl.BlockSpec((8, channels), lambda s: (0, 0)),
        ],
        out_specs=(
            pl.BlockSpec((27, channels, channels), lambda s: (0, 0, 0)),
            pl.BlockSpec((1, wide, wide, edge, channels), lambda s: (s, 0, 0, 0, 0)),
            pl.BlockSpec((1, 2, 3, wide, edge, channels), lambda s: (s, 0, 0, 0, 0, 0)),
            whole,
        ),
        scratch_shapes=[
            pltpu.VMEM((27, channels, channels), f32),
            pltpu.VMEM((3 * channels, min(4, edge // 2) * cells), bf16),
            pltpu.VMEM((3 * channels, min(4, edge // 2) * cells), bf16),
            pltpu.VMEM((2, wide, 8 * ((edge + 16) // 8), channels), f32),
            pltpu.VMEM((4, edge, channels), f32),
            pltpu.VMEM((min(4, edge // 2), cells, channels), f32),
            pltpu.VMEM((2, cells, channels), f32),
        ],
        compiler_params=params(48, ("arbitrary",)),
        cost_estimate=cost(20 * 10**9, 8 * MIB),
        name="weight_grad",
    )(occupancy, live, features, cotangent, rim, coef)


def side_rows(edge, shift_ref, shift_lead, w_ref, side_s):
    cells = edge * edge
    channels = w_ref.shape[0] // 9
    for side in range(2):
        rows = jnp.concatenate(
            [
                shift_ref[shift_lead + (side, tap % 3, slice(tap // 3, tap // 3 + edge))].reshape(cells, channels)
                for tap in range(9)
            ],
            axis=1,
        )
        first = 2 * side * channels
        side_s[side] = jnp.dot(rows, w_ref[:, first : first + channels], preferred_element_type=f32)


DEPTH = 2


def conv_planes(edge, z, pad_ref, pad_lead, w_ref, side_s, x_at):
    cells = edge * edge
    rows = DEPTH * cells
    channels = w_ref.shape[0] // 9
    found = jnp.dot(
        jnp.concatenate(
            [
                pad_ref[pad_lead + (pl.ds(z + tap // 3, DEPTH), slice(tap % 3, tap % 3 + edge))].reshape(
                    rows, channels
                )
                for tap in range(9)
            ],
            axis=1,
        ),
        w_ref[...],
        preferred_element_type=f32,
    )

    def beside(side):
        line = side_s[side, pl.ds(pl.multiple_of(z * edge, edge), DEPTH * edge), :]
        return jnp.broadcast_to(line[:, None, :], (DEPTH * edge, edge, channels)).reshape(rows, channels)

    before = jnp.where(x_at == 0, beside(0), pltpu.roll(found[:, :channels], 1, 0))
    after = jnp.where(x_at == edge - 1, beside(1), pltpu.roll(found[:, 2 * channels :], rows - 1, 0))
    return found[:, channels : 2 * channels] + before + after


def back_kernel(edge, occ_ref, live_ref, f_ref, pad_ref, shift_ref, w_ref, coef_ref, hat_ref, sum_ref, side_s):
    channels = f_ref.shape[-1]
    slot = pl.program_id(0)
    coef = coefficients(coef_ref)
    mean, rstd, scale, shift = coef[:4]

    @pl.when(slot == 0)
    def _():
        sum_ref[...] = jnp.zeros_like(sum_ref)

    @pl.when(live_ref[slot] != 0)
    def _():
        side_rows(edge, shift_ref, (0,), w_ref, side_s)
        rows = DEPTH * edge * edge
        x_at = x_row(rows, edge, channels)

        def planes(z, first, second):
            back = conv_planes(edge, z, pad_ref, (0,), w_ref, side_s, x_at)
            mask = planes_mask(occ_ref, slot, z, DEPTH, edge, channels)
            feats = f_ref[0, pl.ds(z, DEPTH)].reshape(rows, channels).astype(f32)
            normed = (feats - mean) * rstd
            pre = normed * scale + shift
            gate = jax.nn.sigmoid(pre)
            hat = jnp.where(mask, back * (gate * (1.0 + pre * (1.0 - gate))) * scale, 0.0)
            hat_ref[0, pl.ds(z, DEPTH)] = hat.reshape(DEPTH, edge * edge, channels)
            first = first + jnp.sum(hat, axis=0, keepdims=True)
            second = second + jnp.sum(hat * normed, axis=0, keepdims=True)
            return (first, second)

        def step(i, carry):
            for part in range(2):
                carry = planes((2 * i + part) * DEPTH, *carry)
            return carry

        zero = jnp.zeros((1, channels), f32)
        first, second = lax.fori_loop(0, edge // (2 * DEPTH), step, (zero, zero))
        sum_ref[0:1, :] = sum_ref[0:1, :] + first
        sum_ref[1:2, :] = sum_ref[1:2, :] + second


def back_conv(occupancy, live, features, padded, shifted, weight, coef):
    edge, channels = features.shape[1], features.shape[-1]
    cells = edge * edge
    whole = pl.BlockSpec((1, edge, cells, channels), lambda s: (s, 0, 0, 0))
    return pl.pallas_call(
        functools.partial(back_kernel, edge),
        grid=(2,),
        out_shape=(
            jax.ShapeDtypeStruct((2, edge, cells, channels), f32),
            jax.ShapeDtypeStruct((8, channels), f32),
        ),
        in_specs=[
            SMEM,
            SMEM,
            whole,
            pl.BlockSpec((1,) + padded.shape[1:], lambda s: (s, 0, 0, 0, 0)),
            pl.BlockSpec((1,) + shifted.shape[1:], lambda s: (s, 0, 0, 0, 0, 0)),
            pl.BlockSpec(weight.shape, lambda s: (0, 0)),
            pl.BlockSpec((8, channels), lambda s: (0, 0)),
        ],
        out_specs=(whole, pl.BlockSpec((8, channels), lambda s: (0, 0))),
        scratch_shapes=[pltpu.VMEM((2, cells, channels), f32)],
        compiler_params=params(48, ("arbitrary",)),
        cost_estimate=cost(20 * 10**9, 8 * MIB),
        name="back_conv",
    )(occupancy, live, features, padded, shifted, weight, coef)


def forward_kernel(edge, slot, occ_ref, live_ref, f_ref, hid_ref, rim_ref, w_ref, coef_ref, bias_ref, *refs):
    out_ref, pad_s, shift_s, xh_s, edge_s, side_s = refs[-6:]
    channels = f_ref.shape[-1]
    coef = coefficients(coef_ref)

    @pl.when(live_ref[slot] == 0)
    def _():
        out_ref[...] = f_ref[...]

    @pl.when(live_ref[slot] != 0)
    def _():
        def activate(coded):
            return hidden_plane(coded, coded < jnp.inf, coef)

        set_halo(edge, rim_ref, pad_s, (), shift_s, (), xh_s, edge_s, activate)
        for z in range(edge):
            pad_s[z + 1, 1 : edge + 1] = hid_ref[0, z].reshape(edge, edge, channels)
        side_rows(edge, shift_s, (), w_ref, side_s)
        rows = DEPTH * edge * edge
        x_at = x_row(rows, edge, channels)

        def step(i, carry):
            for part in range(2):
                z = (2 * i + part) * DEPTH
                conv = conv_planes(edge, z, pad_s, (), w_ref, side_s, x_at)
                mask = planes_mask(occ_ref, slot, z, DEPTH, edge, channels)
                feats = f_ref[0, pl.ds(z, DEPTH)].reshape(rows, channels).astype(f32)
                mixed = (feats + jnp.where(mask, conv + bias_ref[...], 0.0)).astype(bf16)
                out_ref[0, pl.ds(z, DEPTH)] = mixed.reshape(DEPTH, edge * edge, channels)
            return carry

        lax.fori_loop(0, edge // (2 * DEPTH), step, 0)


def forward_conv(slot, occupancy, live, features, hidden, rim, weight, coef, bias, base=None):
    edge, channels = features.shape[1], features.shape[-1]
    cells = edge * edge
    wide = edge + 2
    whole = pl.BlockSpec((1, edge, cells, channels), lambda s: (slot, 0, 0, 0))
    extra = [] if base is None else [base]
    return pl.pallas_call(
        functools.partial(forward_kernel, edge, slot),
        grid=(1,),
        out_shape=jax.ShapeDtypeStruct(features.shape, bf16),
        in_specs=[
            SMEM,
            SMEM,
            whole,
            whole,
            pl.BlockSpec((edge, 1) + rim.shape[2:], lambda s: (0, slot, 0, 0, 0)),
            pl.BlockSpec(weight.shape, lambda s: (0, 0)),
            pl.BlockSpec((8, channels), lambda s: (0, 0)),
            pl.BlockSpec((1, channels), lambda s: (0, 0)),
        ]
        + [pl.BlockSpec(memory_space=pl.ANY)] * len(extra),
        out_specs=whole,
        scratch_shapes=[
            pltpu.VMEM((wide, wide, edge, channels), bf16),
            pltpu.VMEM((2, 3, wide, edge, channels), bf16),
            pltpu.VMEM((2, wide, 8 * ((edge + 16) // 8), channels), f32),
            pltpu.VMEM((4, edge, channels), f32),
            pltpu.VMEM((2, cells, channels), f32),
        ],
        input_output_aliases={8: 0} if extra else {},
        compiler_params=params(48, ("arbitrary",)),
        cost_estimate=cost(10 * 10**9, 4 * MIB),
        name="forward_conv",
    )(occupancy, live, features, hidden, rim, weight, coef, bias, *extra)


def finish_kernel(edge, occ_ref, live_ref, f_ref, g_ref, hat_ref, coef_ref, out_ref):
    channels = f_ref.shape[-1]
    slot = pl.program_id(0)
    mean, rstd = coef_ref[0:1, :], coef_ref[1:2, :]
    first, second = coef_ref[2:3, :], coef_ref[3:4, :]

    @pl.when(live_ref[slot] == 0)
    def _():
        out_ref[...] = g_ref[...]

    @pl.when(live_ref[slot] != 0)
    def _():
        def plane(z, carry):
            mask = plane_mask(occ_ref, slot, z, edge, channels)
            normed = (f_ref[0, z].astype(f32) - mean) * rstd
            change = rstd * (hat_ref[0, z] - first - normed * second)
            out_ref[0, z] = (g_ref[0, z].astype(f32) + jnp.where(mask, change, 0.0)).astype(bf16)
            return carry

        lax.fori_loop(0, edge, plane, 0)


def finish(occupancy, live, features, cotangent, hat, coef):
    edge, channels = features.shape[1], features.shape[-1]
    whole = pl.BlockSpec((1, edge, edge * edge, channels), lambda s: (s, 0, 0, 0))
    return pl.pallas_call(
        functools.partial(finish_kernel, edge),
        grid=(2,),
        out_shape=jax.ShapeDtypeStruct(features.shape, bf16),
        in_specs=[SMEM, SMEM, whole, whole, whole, pl.BlockSpec((8, channels), lambda s: (0, 0))],
        out_specs=whole,
        compiler_params=params(32, ("arbitrary",)),
        cost_estimate=cost(0, 12 * MIB),
        name="finish",
    )(occupancy, live, features, cotangent, hat, coef)


def wide_sum(values):
    count = lax.axis_size("wide")
    step = 1
    while step < count:
        values = values + lax.ppermute(values, "wide", [(i, i ^ step) for i in range(count)])
        step *= 2
    return values


def group_sums(rows, channels):
    width = channels // G
    which = jnp.arange(channels) // width
    same = (which[:, None] == which[None, :]).astype(f32)
    return jnp.dot(rows, same, precision=lax.Precision.HIGHEST)


def scale_kernel(parts_ref, out_ref):
    total = jnp.zeros((1, parts_ref.shape[-1]), f32)
    for part in range(parts_ref.shape[0]):
        values = parts_ref[part].astype(f32)
        total = total + jnp.sum(values * values, axis=0, keepdims=True)
    mean = jnp.sum(total, axis=1, keepdims=True) / out_ref.size
    factor = lax.rsqrt(mean + step_eps)
    for part in range(parts_ref.shape[0]):
        out_ref[part] = parts_ref[part].astype(f32) * factor


def reduce_weights(grads, sums, tie):
    shape = grads.shape
    wide, narrow = lax.axis_size("wide"), lax.axis_size("narrow")
    rows = shape[0] * shape[1] // wide
    mine = jnp.sum(exchange(grads.reshape(wide, rows, shape[2]), "wide"), axis=0)
    deep = -(-rows // (8 * narrow)) * 8
    mine = jnp.pad(mine, ((0, deep * narrow - rows), (0, 0))).reshape(narrow, deep, shape[2])
    sums = jnp.broadcast_to(sums[None], (narrow,) + sums.shape)
    mine = jnp.sum(exchange(jnp.concatenate([mine, sums], axis=1), "narrow"), axis=0)
    mine, sums = mine[:deep], mine[deep:]
    mine, sums, tie = lax.optimization_barrier((mine, sums, tie))
    mine = exchange(jnp.broadcast_to(mine.astype(bf16)[None], (narrow, deep, shape[2])), "narrow")
    mine = mine.reshape(narrow * deep, shape[2])[:rows]
    parts = exchange(jnp.broadcast_to(mine[None], (wide,) + mine.shape), "wide")
    step = pl.pallas_call(
        scale_kernel,
        out_shape=jax.ShapeDtypeStruct(parts.shape, f32),
        in_specs=[VMEM],
        out_specs=VMEM,
        compiler_params=params(16),
        cost_estimate=cost(0, 3 * MIB),
        name="scale",
    )(parts)
    return (step.reshape(shape), sums, tie)


def local(
    features,
    out_cotangent,
    occupancy,
    live_slots,
    neighbours,
    timestep,
    norm_gain,
    norm_bias,
    film_weight,
    conv_weight,
    conv_bias,
):
    channels = features.shape[-1]
    group_width = channels // G
    hub = lax.axis_index("narrow").astype(jnp.int32)
    place = jnp.stack([hub, lax.axis_index("wide").astype(jnp.int32)])
    mine = 2 * hub + jnp.arange(2, dtype=jnp.int32)
    live = jnp.any(live_slots[0][None, :] == mine[:, None], axis=1).astype(jnp.int32)

    taps = conv_weight.reshape(9, 3, channels, channels)
    forward_weight = taps.transpose(0, 2, 1, 3).reshape(9 * channels, 3 * channels)
    flipped = conv_weight[::-1].reshape(9, 3, channels, channels)
    back_weight = flipped.transpose(0, 3, 1, 2).reshape(9 * channels, 3 * channels)
    film_scale, film_shift = film_terms(timestep, film_weight)
    scale = norm_gain * (1.0 + film_scale)
    shift = norm_bias * (1.0 + film_scale) + film_shift

    up_got = exchange(surface(occupancy, out_cotangent, 0.0, False), "narrow")
    feat_message = surface(occupancy, features, float("inf"), True)
    feat_message, up_got, forward_weight, back_weight, scale, shift = lax.optimization_barrier(
        (feat_message, up_got, forward_weight, back_weight, scale, shift)
    )
    feat_got = exchange(feat_message, "narrow")
    up_rows, _ = hub_stage(place, live_slots, neighbours, up_got, 0.0)
    up_rows, feat_got = lax.optimization_barrier((up_rows, feat_got))
    up_rim = exchange(up_rows, "narrow")
    feat_rows, stats = hub_stage(place, live_slots, neighbours, feat_got, float("inf"))
    stats = wide_sum(stats)
    feat_rows, up_rim = lax.optimization_barrier((feat_rows, up_rim))
    feat_rim = exchange(feat_rows, "narrow")

    voxel_count = stats[2, 0] * group_width
    sums = group_sums(stats[:2], channels)
    mean = sums[0] / voxel_count
    rstd = lax.rsqrt(sums[1] / voxel_count - mean * mean + norm_eps)
    blank = jnp.zeros((channels,), f32)
    coef = jnp.stack([mean, rstd, scale, shift, blank, blank, blank, blank])

    grads, padded, shifted, hidden = weight_grad(occupancy, live, features, out_cotangent, up_rim, coef)
    grads, feat_rim = lax.optimization_barrier((grads, feat_rim))
    hat, grad_sums = back_conv(occupancy, live, features, padded, shifted, back_weight, coef)
    forward = (occupancy, live, features, hidden, feat_rim, forward_weight, coef, conv_bias[None, :])
    mixed = forward_conv(0, *forward)
    weight_step, grad_sums, mixed = reduce_weights(grads, grad_sums, mixed)
    grad_sums, mixed = lax.optimization_barrier((wide_sum(grad_sums), mixed))
    grad_sums = group_sums(grad_sums[:2], channels) / voxel_count
    mixed = forward_conv(1, *forward, base=mixed)
    grad_coef = jnp.stack([mean, rstd, grad_sums[0], grad_sums[1], blank, blank, blank, blank])
    feature_grad = finish(occupancy, live, features, out_cotangent, hat, grad_coef)
    return (mixed, feature_grad, weight_step)


def solution(mesh):
    return jax.shard_map(
        local,
        mesh=mesh,
        in_specs=(
            P(("wide", "narrow"), None, None, None),
            P(("wide", "narrow"), None, None, None),
            P(("wide", "narrow"), None, None),
            P("wide", None),
            P("wide", None),
            P(),
            P(),
            P(),
            P(),
            P(),
            P(),
        ),
        out_specs=(
            P(("wide", "narrow"), None, None, None),
            P(("wide", "narrow"), None, None, None),
            P(),
        ),
        check_vma=False,
    )
```

```python
import functools

import jax
import jax.numpy as jnp
from jax import lax
from jax.experimental import pallas as pl
from jax.experimental.pallas import tpu as pltpu
from jax.sharding import PartitionSpec as P

G = 32
norm_eps = 1e-05
step_eps = 1e-06
MIB = 1 << 20
f32 = jnp.float32
bf16 = jnp.bfloat16

SMEM = pl.BlockSpec(memory_space=pltpu.SMEM)
VMEM = pl.BlockSpec(memory_space=pltpu.VMEM)


def params(limit, semantics=None):
    return pltpu.CompilerParams(vmem_limit_bytes=limit * MIB, dimension_semantics=semantics)


def cost(flops, size):
    return pl.CostEstimate(flops=flops, bytes_accessed=size, transcendentals=0)


def film_terms(timestep, film_weight):
    half_width = film_weight.shape[0] // 2
    channels = film_weight.shape[1] // 2
    frequencies = jnp.exp(
        -jnp.log(10000.0) * jnp.arange(half_width).astype(jnp.float32) / half_width
    )
    angles = timestep.astype(jnp.float32)[0] * frequencies
    embedding = jax.nn.silu(jnp.concatenate([jnp.cos(angles), jnp.sin(angles)]))
    film_out = jnp.dot(embedding[None, :], film_weight, precision=lax.Precision.HIGHEST)[0]
    return (film_out[:channels], film_out[channels:])


def plane_mask(occ_ref, slot, z, edge, channels):
    bit = lax.broadcasted_iota(jnp.int32, (edge, channels), 0)
    rows = [
        jnp.bitwise_and(jnp.right_shift(jnp.full((edge, channels), occ_ref[slot, z, y], jnp.int32), bit), 1)
        for y in range(edge)
    ]
    return jnp.concatenate(rows, axis=0) != 0


def x_row(rows, edge, channels):
    return lax.rem(lax.broadcasted_iota(jnp.int32, (rows, channels), 0), edge)


def pieces(value, count):
    found = []
    for _ in range(count):
        part = value.astype(bf16).astype(f32)
        found.append(part)
        value = value - part
    return found


def surface_kernel(edge, with_stats, fill, occ_ref, v_ref, out_ref, plane_s, edge_s, stat_s):
    channels = v_ref.shape[-1]
    last = edge - 1
    slot = pl.program_id(0)

    @pl.when(slot == 0)
    def _():
        stat_s[...] = jnp.zeros_like(stat_s)
        edge_s[...] = jnp.zeros_like(edge_s)

    def coded(z):
        mask = plane_mask(occ_ref, slot, z, edge, channels)
        values = v_ref[0, z].astype(f32)
        return (mask, values, jnp.where(mask, values, fill))

    def step(z, carry):
        mask, values, shown = coded(z)
        plane_s[...] = shown
        for side in range(2):
            row = side * last
            out_ref[z, 4 + 2 * slot + side] = shown[row * edge : (row + 1) * edge].astype(bf16)
            out_ref[z, 8 + 2 * slot + side] = plane_s[pl.ds(row, edge, stride=edge), :].astype(bf16)
        if not with_stats:
            return carry
        total, squares, count = carry
        masked = jnp.where(mask, values, 0.0)
        total = total + jnp.sum(masked, axis=0, keepdims=True)
        squares = squares + jnp.sum(masked * values, axis=0, keepdims=True)
        count = count + jnp.sum(mask.astype(f32), axis=0, keepdims=True)
        return (total, squares, count)

    zero = jnp.zeros((1, channels), f32)
    found = lax.fori_loop(0, edge, step, (zero, zero, zero) if with_stats else 0)
    if with_stats:
        for index in range(3):
            stat_s[index : index + 1, :] = stat_s[index : index + 1, :] + found[index]
    for z_side in range(2):
        _, _, shown = coded(z_side * last)
        for hub in range(edge):
            out_ref[hub, 2 * slot + z_side] = shown[hub * edge : (hub + 1) * edge].astype(bf16)
        for y_side in range(2):
            for hub in range(edge):
                first = y_side * last * edge + hub
                for place in range(2):

                    @pl.when(slot == place)
                    def _():
                        row = 4 * place + 2 * z_side + y_side
                        edge_s[hub, row : row + 1, :] = shown[first : first + 1]

    @pl.when(slot == 1)
    def _():
        if with_stats:
            parts = pieces(stat_s[0:1, :], 3) + pieces(stat_s[1:2, :], 3) + pieces(stat_s[2:3, :], 2)
            for hub in range(edge):
                for row, part in enumerate(parts):
                    edge_s[hub, 8 + row : 9 + row, :] = part
        for hub in range(edge):
            for tile in range(16 // edge):
                out_ref[hub, 12 + tile] = edge_s[hub, tile * edge : (tile + 1) * edge].astype(bf16)


def surface(occupancy, values, fill, with_stats):
    edge, cells, channels = values.shape[1:]
    tiles = 12 + 16 // edge
    return pl.pallas_call(
        functools.partial(surface_kernel, edge, with_stats, fill),
        grid=(2,),
        out_shape=jax.ShapeDtypeStruct((edge, tiles, edge, channels), bf16),
        in_specs=[SMEM, pl.BlockSpec((1, edge, cells, channels), lambda s: (s, 0, 0, 0))],
        out_specs=pl.BlockSpec((edge, tiles, edge, channels), lambda s: (0, 0, 0, 0)),
        scratch_shapes=[
            pltpu.VMEM((cells, channels), f32),
            pltpu.VMEM((edge, 16, channels), f32),
            pltpu.VMEM((8, channels), f32),
        ],
        compiler_params=params(60, ("arbitrary",)),
        cost_estimate=cost(0, 3 * MIB),
        name="surface",
    )(occupancy, values)


def trade_kernel(edge, live_ref, got_ref, left_ref, right_ref, stat_ref, ends_s):
    live_count = live_ref.shape[1]
    for k in range(live_count):
        slot = live_ref[0, k]
        owner, local = slot // 2, lax.rem(slot, 2)
        for side, out in ((0, left_ref), (1, right_ref)):
            out[k] = got_ref[owner, 8 + 2 * local + side]
            for z_side in range(2):
                tile = got_ref[owner, 2 * local + z_side].astype(f32)
                row = 2 * k + z_side
                x = side * (edge - 1)
                ends_s[side, row : row + 1, :] = tile[x : x + 1]
    for side, out in ((0, left_ref), (1, right_ref)):
        for tile in range(2 * live_count // edge):
            out[live_count + tile] = ends_s[side, tile * edge : (tile + 1) * edge].astype(bf16)
    rows = []
    for tile in range(8 // edge if edge < 16 else 0, 16 // edge):
        total = got_ref[0, 12 + tile].astype(f32)
        for source in range(1, edge):
            total = total + got_ref[source, 12 + tile].astype(f32)
        rows.append(total)
    rows = jnp.concatenate(rows, axis=0)
    if edge == 16:
        rows = rows[8:]
    stat_ref[...] = jnp.zeros_like(stat_ref)
    stat_ref[0:1, :] = rows[0:1] + rows[1:2] + rows[2:3]
    stat_ref[1:2, :] = rows[3:4] + rows[4:5] + rows[5:6]
    stat_ref[2:3, :] = rows[6:7] + rows[7:8]


def trade(live_slots, got):
    edge, channels = got.shape[2], got.shape[-1]
    live_count = live_slots.shape[1]
    tiles = live_count + 2 * live_count // edge
    payload = jax.ShapeDtypeStruct((tiles, edge, channels), bf16)
    return pl.pallas_call(
        functools.partial(trade_kernel, edge),
        out_shape=(payload, payload, jax.ShapeDtypeStruct((8, channels), f32)),
        in_specs=[SMEM, VMEM],
        out_specs=(VMEM, VMEM, VMEM),
        scratch_shapes=[pltpu.VMEM((2, 2 * live_count, channels), f32)],
        compiler_params=params(16),
        cost_estimate=cost(0, 2 * MIB),
        name="trade",
    )(live_slots, got)


def hub_kernel(edge, fill, place_ref, live_ref, near_ref, got_ref, lower_ref, upper_ref, out_ref, wide_s, rows_s):
    live_count = live_ref.shape[1]
    last = edge - 1
    hub, group = place_ref[0], place_ref[1]
    x_refs = (lower_ref, upper_ref)
    for side in range(2):
        wide_s[side] = x_refs[side][...].astype(f32)

    def entry(k, dz, dy, dx):
        number = near_ref[k, 9 * (dz + 1) + 3 * (dy + 1) + (dx + 1)]
        index = jnp.clip(number - (group + dx) * live_count, 0, live_count - 1)
        return (number >= 0, index)

    def own(k, dz, dy):
        there, index = entry(k, dz, dy, 0)
        slot = live_ref[0, index]
        return (there, slot // 2, lax.rem(slot, 2))

    def step(k, carry):
        slot = live_ref[0, k]
        owner, local = slot // 2, lax.rem(slot, 2)

        def put(tile, there, values):
            out_ref[owner, local, tile] = jnp.where(there, values, fill).astype(bf16)

        def put_row(row, there, values):
            rows_s[row : row + 1, :] = jnp.where(there, values, fill)

        for side in range(2):
            step_to = 2 * side - 1
            there, source, place = own(k, step_to, 0)
            put(side, there, got_ref[source, 2 * place + 1 - side].astype(f32))
            there, source, place = own(k, 0, step_to)
            put(2 + side, there, got_ref[source, 4 + 2 * place + 1 - side].astype(f32))
            there, index = entry(k, 0, 0, step_to)
            put(4 + side, there, wide_s[side, index])
        dz_corner = jnp.where(hub == last, -1, 1)
        for a in range(2):
            for b in range(2):
                there, source, place = own(k, 2 * a - 1, 2 * b - 1)
                row = 4 * place + 2 * (1 - a) + (1 - b)
                tile = got_ref[source, 12 + row // edge].astype(f32)
                picked = lax.broadcasted_iota(jnp.int32, tile.shape, 0) == lax.rem(row, edge)
                put_row(2 * a + b, there, jnp.sum(jnp.where(picked, tile, 0.0), axis=0, keepdims=True))
                there, index = entry(k, 2 * a - 1, 0, 2 * b - 1)
                row = 2 * index + (1 - a)
                tile = wide_s[b, live_count + row // edge]
                picked = lax.broadcasted_iota(jnp.int32, tile.shape, 0) == lax.rem(row, edge)
                put_row(4 + 2 * a + b, there, jnp.sum(jnp.where(picked, tile, 0.0), axis=0, keepdims=True))
                row = last if a == 0 else 0
                there, index = entry(k, 0, 2 * a - 1, 2 * b - 1)
                put_row(8 + 2 * a + b, there, wide_s[b, index, row : row + 1, :])
                there, index = entry(k, dz_corner, 2 * a - 1, 2 * b - 1)
                put_row(12 + 2 * a + b, there, wide_s[b, index, row : row + 1, :])
        for tile in range(16 // edge):
            out_ref[owner, local, 6 + tile] = rows_s[tile * edge : (tile + 1) * edge].astype(bf16)
        return carry

    lax.fori_loop(0, live_count, step, 0)


def hub_rows(place, live_slots, neighbours, got, lower, upper, fill):
    edge, channels = got.shape[2], got.shape[-1]
    return pl.pallas_call(
        functools.partial(hub_kernel, edge, fill),
        out_shape=jax.ShapeDtypeStruct((edge, 2, 6 + 16 // edge, edge, channels), bf16),
        in_specs=[SMEM, SMEM, SMEM, VMEM, VMEM, VMEM],
        out_specs=VMEM,
        scratch_shapes=[
            pltpu.VMEM((2,) + lower.shape, f32),
            pltpu.VMEM((16, channels), f32),
        ],
        compiler_params=params(16),
        cost_estimate=cost(0, 8 * MIB),
        name="hub_rows",
    )(place, live_slots, neighbours, got, lower, upper)


def exchange(values, axis):
    return lax.all_to_all(values, axis, split_axis=0, concat_axis=0, tiled=True)


def hub_stage(place, live_slots, neighbours, got, fill, with_stats=False):
    to_left, to_right, stats = trade(live_slots, got)
    count = lax.axis_size("wide")
    lower = lax.ppermute(to_right, "wide", [(i, i + 1) for i in range(count - 1)])
    upper = lax.ppermute(to_left, "wide", [(i + 1, i) for i in range(count - 1)])
    if with_stats:
        stats, lower, upper = lax.optimization_barrier((stats, lower, upper))
        stats = wide_round(stats, 1)
    return (hub_rows(place, live_slots, neighbours, got, lower, upper, fill), stats)


def coefficients(coef_ref):
    return [coef_ref[i : i + 1, :] for i in range(5)]


def set_halo(edge, rim_ref, pad_ref, pad_lead, shift_ref, shift_lead, xh_s, edge_s, change):
    last = edge - 1
    for hub in range(edge):
        tiles = [change(rim_ref[hub, 0, tile].astype(f32)) for tile in range(6 + 16 // edge)]
        for side in range(2):
            pad_ref[pad_lead + (side * (edge + 1), hub + 1)] = tiles[side].astype(bf16)
            pad_ref[pad_lead + (hub + 1, side * (edge + 1))] = tiles[2 + side].astype(bf16)
            xh_s[side, hub + 1, 8 : 8 + edge, :] = tiles[4 + side]

        def row(index):
            tile = tiles[6 + index // edge]
            return tile[index % edge : index % edge + 1]

        for a in range(2):
            for b in range(2):
                edge_s[2 * a + b, hub : hub + 1, :] = row(2 * a + b)
                xh_s[b, a * (edge + 1), 8 + hub : 9 + hub, :] = row(4 + 2 * a + b)
                y = 8 + edge if a else 7
                xh_s[b, hub + 1, y : y + 1, :] = row(8 + 2 * a + b)
                if hub == last:
                    xh_s[b, 0, y : y + 1, :] = row(12 + 2 * a + b)
                if hub == 0:
                    xh_s[b, edge + 1, y : y + 1, :] = row(12 + 2 * a + b)
    for a in range(2):
        for b in range(2):
            pad_ref[pad_lead + (a * (edge + 1), b * (edge + 1))] = edge_s[2 * a + b].astype(bf16)
    for side in range(2):
        for z in range(edge + 2):
            for y in range(3):
                shift_ref[shift_lead + (side, y, z)] = xh_s[side, z, 7 + y : 7 + y + edge, :].astype(bf16)


def hidden_plane(feats, mask, coef):
    mean, rstd, scale, shift = coef[:4]
    pre = (feats - mean) * rstd * scale + shift
    return jnp.where(mask, pre * jax.nn.sigmoid(pre), 0.0)


def weight_kernel(edge, occ_ref, live_ref, f_ref, g_ref, rim_ref, coef_ref, grad_ref, pad_ref, shift_ref,
                  hid_ref, acc_s, even_s, odd_s, xh_s, edge_s, plane_s, face_s):
    channels = f_ref.shape[-1]
    cells = edge * edge
    slot = pl.program_id(0)
    coef = coefficients(coef_ref)
    depth = min(4, edge // 2)
    chunks = edge // depth

    @pl.when(slot == 0)
    def _():
        acc_s[...] = jnp.zeros_like(acc_s)

    @pl.when(live_ref[slot] != 0)
    def _():
        set_halo(edge, rim_ref, pad_ref, (0,), shift_ref, (0,), xh_s, edge_s, lambda v: v)
        lane_x = lax.rem(lax.broadcasted_iota(jnp.int32, (channels, cells), 1), edge)

        def fill(z, carry):
            mask = plane_mask(occ_ref, slot, z, edge, channels)
            ups = jnp.where(mask, g_ref[0, z].astype(f32), 0.0).astype(bf16)
            pad_ref[0, z + 1, 1 : edge + 1] = ups.reshape(edge, edge, channels)
            return carry

        lax.fori_loop(0, edge, fill, 0)

        def prepare(chunk, flip_s, part):
            if part < depth:
                z = chunk * depth + part
                mask = plane_mask(occ_ref, slot, z, edge, channels)
                hidden = hidden_plane(f_ref[0, z].astype(f32), mask, coef).astype(bf16)
                hid_ref[0, z] = hidden
                hidden = hidden.astype(f32)
                plane_s[part] = hidden
                for side in range(2):
                    face_s[side, pl.ds(z * edge, edge), :] = plane_s[
                        part, pl.ds(side * (edge - 1), edge, stride=edge), :
                    ]
                flat = hidden.T
                before = jnp.where(lane_x == edge - 1, 0.0, pltpu.roll(flat, cells - 1, 1))
                after = jnp.where(lane_x == 0, 0.0, pltpu.roll(flat, 1, 1))
                columns = slice(part * cells, (part + 1) * cells)
                flip_s[0:channels, columns] = before.astype(bf16)
                flip_s[channels : 2 * channels, columns] = flat.astype(bf16)
                flip_s[2 * channels : 3 * channels, columns] = after.astype(bf16)

        def add(tap, px, values):
            pz, py = tap // 3, tap % 3
            offset = 9 * (2 - pz) + 3 * (2 - py) + (2 - px)
            acc_s[offset] = acc_s[offset] + values

        pairs = [(0, 1), (2, 3), (4, 5), (6, 7), (8,)]

        def multiply(chunk, flip_s, beside):
            z0 = chunk * depth
            left = flip_s[...]
            for turn, pair in enumerate(pairs):
                right = [
                    pad_ref[0, pl.ds(z0 + tap // 3, depth), tap % 3 : tap % 3 + edge].reshape(
                        depth * cells, channels
                    )
                    for tap in pair
                ]
                right = right[0] if len(right) == 1 else jnp.concatenate(right, axis=1)
                found = jnp.dot(left, right, preferred_element_type=f32)
                for place, tap in enumerate(pair):
                    for px in range(3):
                        add(
                            tap,
                            px,
                            found[
                                px * channels : (px + 1) * channels,
                                place * channels : (place + 1) * channels,
                            ],
                        )
                beside(turn)

        def two(i, carry):
            multiply(2 * i, even_s, functools.partial(prepare, 2 * i + 1, odd_s))
            multiply(2 * i + 1, odd_s, functools.partial(prepare, 2 * i + 2, even_s))
            return carry

        for part in range(depth):
            prepare(0, even_s, part)
        lax.fori_loop(0, chunks // 2 - 1, two, 0)
        multiply(chunks - 2, even_s, functools.partial(prepare, chunks - 1, odd_s))
        multiply(chunks - 1, odd_s, lambda turn: None)
        for side in range(2):
            left = face_s[side].T.astype(bf16)
            for tap in range(9):
                right = shift_ref[0, side, tap % 3, tap // 3 : tap // 3 + edge].reshape(cells, channels)
                add(tap, 2 * side, jnp.dot(left, right, preferred_element_type=f32))

    @pl.when(slot == 1)
    def _():
        grad_ref[...] = acc_s[...]


def weight_grad(occupancy, live, features, cotangent, rim, coef):
    edge, channels = features.shape[1], features.shape[-1]
    cells = edge * edge
    wide = edge + 2
    whole = pl.BlockSpec((1, edge, cells, channels), lambda s: (s, 0, 0, 0))
    return pl.pallas_call(
        functools.partial(weight_kernel, edge),
        grid=(2,),
        out_shape=(
            jax.ShapeDtypeStruct((27, channels, channels), f32),
            jax.ShapeDtypeStruct((2, wide, wide, edge, channels), bf16),
            jax.ShapeDtypeStruct((2, 2, 3, wide, edge, channels), bf16),
            jax.ShapeDtypeStruct(features.shape, bf16),
        ),
        in_specs=[
            SMEM,
            SMEM,
            whole,
            whole,
            pl.BlockSpec((edge, 1) + rim.shape[2:], lambda s: (0, s, 0, 0, 0)),
            pl.BlockSpec((8, channels), lambda s: (0, 0)),
        ],
        out_specs=(
            pl.BlockSpec((27, channels, channels), lambda s: (0, 0, 0)),
            pl.BlockSpec((1, wide, wide, edge, channels), lambda s: (s, 0, 0, 0, 0)),
            pl.BlockSpec((1, 2, 3, wide, edge, channels), lambda s: (s, 0, 0, 0, 0, 0)),
            whole,
        ),
        scratch_shapes=[
            pltpu.VMEM((27, channels, channels), f32),
            pltpu.VMEM((3 * channels, min(4, edge // 2) * cells), bf16),
            pltpu.VMEM((3 * channels, min(4, edge // 2) * cells), bf16),
            pltpu.VMEM((2, wide, 8 * ((edge + 16) // 8), channels), f32),
            pltpu.VMEM((4, edge, channels), f32),
            pltpu.VMEM((min(4, edge // 2), cells, channels), f32),
            pltpu.VMEM((2, cells, channels), f32),
        ],
        compiler_params=params(60, ("arbitrary",)),
        cost_estimate=cost(20 * 10**9, 8 * MIB),
        name="weight_grad",
    )(occupancy, live, features, cotangent, rim, coef)


def side_rows(edge, shift_ref, shift_lead, w_ref, side_s):
    cells = edge * edge
    channels = w_ref.shape[0] // 9
    for side in range(2):
        rows = jnp.concatenate(
            [
                shift_ref[shift_lead + (side, tap % 3, slice(tap // 3, tap // 3 + edge))].reshape(cells, channels)
                for tap in range(9)
            ],
            axis=1,
        )
        first = 2 * side * channels
        side_s[side] = jnp.dot(rows, w_ref[:, first : first + channels], preferred_element_type=f32)


DEPTH = 2


def conv_pipeline(edge, pad_ref, pad_lead, w_ref, side_s, found_s, finish_plane, carry):
    cells = edge * edge
    rows = DEPTH * cells
    channels = w_ref.shape[0] // 9
    groups = edge // DEPTH
    x_at = x_row(cells, edge, channels)
    spans = [slice(0, 2 * channels), slice(2 * channels, 3 * channels)]

    def multiply(group, buffer, span):
        z = group * DEPTH
        lines = jnp.concatenate(
            [
                pad_ref[pad_lead + (pl.ds(z + tap // 3, DEPTH), slice(tap % 3, tap % 3 + edge))].reshape(
                    rows, channels
                )
                for tap in range(9)
            ],
            axis=1,
        )
        found_s[buffer, :, span] = jnp.dot(lines, w_ref[:, span], preferred_element_type=f32)

    def combine(group, buffer, part, carry):
        z = group * DEPTH + part
        found = found_s[buffer, part * cells : (part + 1) * cells]

        def beside(side):
            line = side_s[side, pl.ds(pl.multiple_of(z * edge, edge), edge), :]
            return jnp.broadcast_to(line[:, None, :], (edge, edge, channels)).reshape(cells, channels)

        before = jnp.where(x_at == 0, beside(0), pltpu.roll(found[:, :channels], 1, 0))
        after = jnp.where(x_at == edge - 1, beside(1), pltpu.roll(found[:, 2 * channels :], cells - 1, 0))
        return finish_plane(z, found[:, channels : 2 * channels] + before + after, carry)

    def advance(group, buffer, carry):
        for part in range(DEPTH):
            multiply(group + 1, 1 - buffer, spans[part])
            carry = combine(group, buffer, part, carry)
        return carry

    def step(i, carry):
        return advance(2 * i + 1, 1, advance(2 * i, 0, carry))

    for span in spans:
        multiply(0, 0, span)
    carry = lax.fori_loop(0, groups // 2 - 1, step, carry)
    carry = advance(groups - 2, 0, carry)
    for part in range(DEPTH):
        carry = combine(groups - 1, 1, part, carry)
    return carry


def back_kernel(edge, occ_ref, live_ref, f_ref, pad_ref, shift_ref, w_ref, coef_ref, hat_ref, sum_ref, side_s, found_s):
    channels = f_ref.shape[-1]
    slot = pl.program_id(0)
    coef = coefficients(coef_ref)
    mean, rstd, scale, shift = coef[:4]

    @pl.when(slot == 0)
    def _():
        sum_ref[...] = jnp.zeros_like(sum_ref)

    @pl.when(live_ref[slot] != 0)
    def _():
        side_rows(edge, shift_ref, (0,), w_ref, side_s)

        def plane(z, back, carry):
            first, second = carry
            mask = plane_mask(occ_ref, slot, z, edge, channels)
            normed = (f_ref[0, z].astype(f32) - mean) * rstd
            pre = normed * scale + shift
            gate = jax.nn.sigmoid(pre)
            hat = jnp.where(mask, back * (gate * (1.0 + pre * (1.0 - gate))) * scale, 0.0)
            hat_ref[0, z] = hat
            first = first + jnp.sum(hat, axis=0, keepdims=True)
            second = second + jnp.sum(hat * normed, axis=0, keepdims=True)
            return (first, second)

        zero = jnp.zeros((1, channels), f32)
        first, second = conv_pipeline(edge, pad_ref, (0,), w_ref, side_s, found_s, plane, (zero, zero))
        sum_ref[0:1, :] = sum_ref[0:1, :] + first
        sum_ref[1:2, :] = sum_ref[1:2, :] + second


def back_conv(occupancy, live, features, padded, shifted, weight, coef):
    edge, channels = features.shape[1], features.shape[-1]
    cells = edge * edge
    whole = pl.BlockSpec((1, edge, cells, channels), lambda s: (s, 0, 0, 0))
    return pl.pallas_call(
        functools.partial(back_kernel, edge),
        grid=(2,),
        out_shape=(
            jax.ShapeDtypeStruct((2, edge, cells, channels), f32),
            jax.ShapeDtypeStruct((8, channels), f32),
        ),
        in_specs=[
            SMEM,
            SMEM,
            whole,
            pl.BlockSpec((1,) + padded.shape[1:], lambda s: (s, 0, 0, 0, 0)),
            pl.BlockSpec((1,) + shifted.shape[1:], lambda s: (s, 0, 0, 0, 0, 0)),
            pl.BlockSpec(weight.shape, lambda s: (0, 0)),
            pl.BlockSpec((8, channels), lambda s: (0, 0)),
        ],
        out_specs=(whole, pl.BlockSpec((8, channels), lambda s: (0, 0))),
        scratch_shapes=[
            pltpu.VMEM((2, cells, channels), f32),
            pltpu.VMEM((2, DEPTH * cells, 3 * channels), f32),
        ],
        compiler_params=params(60, ("arbitrary",)),
        cost_estimate=cost(20 * 10**9, 8 * MIB),
        name="back_conv",
    )(occupancy, live, features, padded, shifted, weight, coef)


def forward_kernel(edge, slot, occ_ref, live_ref, f_ref, hid_ref, rim_ref, w_ref, coef_ref, bias_ref, *refs):
    out_ref, pad_s, shift_s, xh_s, edge_s, side_s, found_s = refs[-7:]
    channels = f_ref.shape[-1]
    coef = coefficients(coef_ref)

    @pl.when(live_ref[slot] == 0)
    def _():
        out_ref[...] = f_ref[...]

    @pl.when(live_ref[slot] != 0)
    def _():
        def activate(coded):
            return hidden_plane(coded, coded < jnp.inf, coef)

        set_halo(edge, rim_ref, pad_s, (), shift_s, (), xh_s, edge_s, activate)
        for z in range(edge):
            pad_s[z + 1, 1 : edge + 1] = hid_ref[0, z].reshape(edge, edge, channels)
        side_rows(edge, shift_s, (), w_ref, side_s)

        def plane(z, conv, carry):
            mask = plane_mask(occ_ref, slot, z, edge, channels)
            feats = f_ref[0, z].astype(f32)
            out_ref[0, z] = (feats + jnp.where(mask, conv + bias_ref[...], 0.0)).astype(bf16)
            return carry

        conv_pipeline(edge, pad_s, (), w_ref, side_s, found_s, plane, 0)


def forward_conv(slot, occupancy, live, features, hidden, rim, weight, coef, bias, base=None):
    edge, channels = features.shape[1], features.shape[-1]
    cells = edge * edge
    wide = edge + 2
    whole = pl.BlockSpec((1, edge, cells, channels), lambda s: (slot, 0, 0, 0))
    extra = [] if base is None else [base]
    return pl.pallas_call(
        functools.partial(forward_kernel, edge, slot),
        grid=(1,),
        out_shape=jax.ShapeDtypeStruct(features.shape, bf16),
        in_specs=[
            SMEM,
            SMEM,
            whole,
            whole,
            pl.BlockSpec((edge, 1) + rim.shape[2:], lambda s: (0, slot, 0, 0, 0)),
            pl.BlockSpec(weight.shape, lambda s: (0, 0)),
            pl.BlockSpec((8, channels), lambda s: (0, 0)),
            pl.BlockSpec((1, channels), lambda s: (0, 0)),
        ]
        + [pl.BlockSpec(memory_space=pl.ANY)] * len(extra),
        out_specs=whole,
        scratch_shapes=[
            pltpu.VMEM((wide, wide, edge, channels), bf16),
            pltpu.VMEM((2, 3, wide, edge, channels), bf16),
            pltpu.VMEM((2, wide, 8 * ((edge + 16) // 8), channels), f32),
            pltpu.VMEM((4, edge, channels), f32),
            pltpu.VMEM((2, cells, channels), f32),
            pltpu.VMEM((2, DEPTH * cells, 3 * channels), f32),
        ],
        input_output_aliases={8: 0} if extra else {},
        compiler_params=params(60, ("arbitrary",)),
        cost_estimate=cost(10 * 10**9, 4 * MIB),
        name="forward_conv",
    )(occupancy, live, features, hidden, rim, weight, coef, bias, *extra)


def finish_kernel(edge, occ_ref, live_ref, f_ref, g_ref, hat_ref, coef_ref, sums_ref, out_ref):
    channels = f_ref.shape[-1]
    slot = pl.program_id(0)
    first_plane = pl.program_id(1) * f_ref.shape[1]
    mean, rstd = coef_ref[0:1, :], coef_ref[1:2, :]
    first, second = sums_ref[0:1, :], sums_ref[1:2, :]

    @pl.when(live_ref[slot] == 0)
    def _():
        out_ref[...] = g_ref[...]

    @pl.when(live_ref[slot] != 0)
    def _():
        for z in range(f_ref.shape[1]):
            mask = plane_mask(occ_ref, slot, first_plane + z, edge, channels)
            normed = (f_ref[0, z].astype(f32) - mean) * rstd
            change = rstd * (hat_ref[0, z] - first - normed * second)
            out_ref[0, z] = (g_ref[0, z].astype(f32) + jnp.where(mask, change, 0.0)).astype(bf16)


def finish(occupancy, live, features, cotangent, hat, coef, sums):
    edge, channels = features.shape[1], features.shape[-1]
    few = pl.BlockSpec((1, edge // 4, edge * edge, channels), lambda s, z: (s, z, 0, 0))
    return pl.pallas_call(
        functools.partial(finish_kernel, edge),
        grid=(2, 4),
        out_shape=jax.ShapeDtypeStruct(features.shape, bf16),
        in_specs=[SMEM, SMEM, few, few, few] + [pl.BlockSpec((8, channels), lambda s, z: (0, 0))] * 2,
        out_specs=few,
        compiler_params=params(60, ("arbitrary", "arbitrary")),
        cost_estimate=cost(0, 12 * MIB),
        name="finish",
    )(occupancy, live, features, cotangent, hat, coef, sums)


def wide_round(values, step):
    count = lax.axis_size("wide")
    terms = [values]
    for turn in range(1, 4):
        route = [(i, i ^ (turn * step)) for i in range(count)]
        terms.append(lax.ppermute(values, "wide", route))
    return (terms[0] + terms[1]) + (terms[2] + terms[3])


def group_sums(rows, channels):
    width = channels // G
    which = jnp.arange(channels) // width
    same = (which[:, None] == which[None, :]).astype(f32)
    return jnp.dot(rows, same, precision=lax.Precision.HIGHEST)


def scale_kernel(rows, parts_ref, coef_ref, out_ref, sums_ref):
    channels = parts_ref.shape[-1]
    tail = jnp.zeros((parts_ref.shape[1] - rows, channels), f32)
    total = jnp.zeros((1, channels), f32)
    for part in range(parts_ref.shape[0]):
        values = parts_ref[part, 0:rows].astype(f32)
        total = total + jnp.sum(values * values, axis=0, keepdims=True)
        tail = tail + parts_ref[part, rows:].astype(f32)
    mean = jnp.sum(total, axis=1, keepdims=True) / out_ref.size
    factor = lax.rsqrt(mean + step_eps)
    for part in range(parts_ref.shape[0]):
        out_ref[part] = parts_ref[part, 0:rows].astype(f32) * factor
    first = tail[0:1] + tail[1:2] + tail[2:3]
    second = tail[3:4] + tail[4:5] + tail[5:6]
    both = jnp.concatenate([first, second] + [jnp.zeros_like(first)] * 6, axis=0)
    row = lax.broadcasted_iota(jnp.int32, (channels, channels), 0) // (channels // G)
    column = lax.broadcasted_iota(jnp.int32, (channels, channels), 1) // (channels // G)
    same = (row == column).astype(f32)
    grouped = jnp.dot(both, same, precision=lax.Precision.HIGHEST, preferred_element_type=f32)
    sums_ref[...] = grouped / coef_ref[4:5, :]


def reduce_weights(grads, sums, coef, tie):
    shape = grads.shape
    channels = shape[2]
    wide, narrow = lax.axis_size("wide"), lax.axis_size("narrow")
    rows = shape[0] * shape[1] // wide
    mine = jnp.sum(exchange(grads.reshape(wide, rows, channels), "wide"), axis=0)
    deep = -(-rows // (8 * narrow)) * 8
    mine = jnp.pad(mine, ((0, deep * narrow - rows), (0, 0))).reshape(narrow, deep, channels)
    sums = jnp.broadcast_to(sums[None], (narrow,) + sums.shape)
    mine, tie = lax.optimization_barrier((mine, tie))
    mine = jnp.sum(exchange(jnp.concatenate([mine, sums], axis=1), "narrow"), axis=0)
    mine, sums = mine[:deep], mine[deep : deep + 2]
    mine = exchange(jnp.broadcast_to(mine.astype(bf16)[None], (narrow, deep, channels)), "narrow")
    high = lax.reduce_precision(sums, 8, 7)
    middle = lax.reduce_precision(sums - high, 8, 7)
    low = (sums - high) - middle
    tail = jnp.stack([high, middle, low], axis=1).reshape(6, channels).astype(bf16)
    mine = mine.reshape(narrow * deep, channels)[:rows]
    mine, tie = lax.optimization_barrier((mine, tie))
    mine = jnp.concatenate([mine, tail, jnp.zeros((2, channels), bf16)], axis=0)
    parts = exchange(jnp.broadcast_to(mine[None], (wide,) + mine.shape), "wide")
    step, sums = pl.pallas_call(
        functools.partial(scale_kernel, rows),
        out_shape=(
            jax.ShapeDtypeStruct((wide, rows, channels), f32),
            jax.ShapeDtypeStruct((8, channels), f32),
        ),
        in_specs=[VMEM, VMEM],
        out_specs=(VMEM, VMEM),
        compiler_params=params(16),
        cost_estimate=cost(0, 3 * MIB),
        name="scale",
    )(parts, coef)
    return (step.reshape(shape), sums, tie)


def local(
    features,
    out_cotangent,
    occupancy,
    live_slots,
    neighbours,
    timestep,
    norm_gain,
    norm_bias,
    film_weight,
    conv_weight,
    conv_bias,
):
    channels = features.shape[-1]
    group_width = channels // G
    hub = lax.axis_index("narrow").astype(jnp.int32)
    place = jnp.stack([hub, lax.axis_index("wide").astype(jnp.int32)])
    mine = 2 * hub + jnp.arange(2, dtype=jnp.int32)
    live = jnp.any(live_slots[0][None, :] == mine[:, None], axis=1).astype(jnp.int32)

    taps = conv_weight.reshape(9, 3, channels, channels)
    forward_weight = taps.transpose(0, 2, 1, 3).reshape(9 * channels, 3 * channels)
    flipped = conv_weight[::-1].reshape(9, 3, channels, channels)
    back_weight = flipped.transpose(0, 3, 1, 2).reshape(9 * channels, 3 * channels)
    film_scale, film_shift = film_terms(timestep, film_weight)
    scale = norm_gain * (1.0 + film_scale)
    shift = norm_bias * (1.0 + film_scale) + film_shift

    up_got = exchange(surface(occupancy, out_cotangent, 0.0, False), "narrow")
    feat_message = surface(occupancy, features, float("inf"), True)
    feat_message, up_got, forward_weight, back_weight, scale, shift = lax.optimization_barrier(
        (feat_message, up_got, forward_weight, back_weight, scale, shift)
    )
    feat_got = exchange(feat_message, "narrow")
    up_rows, _ = hub_stage(place, live_slots, neighbours, up_got, 0.0)
    up_rows, feat_got = lax.optimization_barrier((up_rows, feat_got))
    up_rim = exchange(up_rows, "narrow")
    feat_rows, stats = hub_stage(place, live_slots, neighbours, feat_got, float("inf"), True)
    feat_rows, up_rim, stats = lax.optimization_barrier((feat_rows, up_rim, stats))
    step = 4
    while step < lax.axis_size("wide"):
        stats = wide_round(stats, step)
        step *= 4
    feat_rim = exchange(feat_rows, "narrow")

    voxel_count = stats[2, 0] * group_width
    sums = group_sums(stats[:2], channels)
    mean = sums[0] / voxel_count
    rstd = lax.rsqrt(sums[1] / voxel_count - mean * mean + norm_eps)
    blank = jnp.zeros((channels,), f32)
    coef = jnp.stack([mean, rstd, scale, shift, blank + voxel_count, blank, blank, blank])

    grads, padded, shifted, hidden = weight_grad(occupancy, live, features, out_cotangent, up_rim, coef)
    grads, feat_rim = lax.optimization_barrier((grads, feat_rim))
    hat, grad_sums = back_conv(occupancy, live, features, padded, shifted, back_weight, coef)
    forward = (occupancy, live, features, hidden, feat_rim, forward_weight, coef, conv_bias[None, :])
    mixed = forward_conv(0, *forward)
    weight_step, grad_sums, mixed = reduce_weights(grads, grad_sums, coef, mixed)
    mixed = forward_conv(1, *forward, base=mixed)
    feature_grad = finish(occupancy, live, features, out_cotangent, hat, coef, grad_sums)
    return (mixed, feature_grad, weight_step)


def solution(mesh):
    return jax.shard_map(
        local,
        mesh=mesh,
        in_specs=(
            P(("wide", "narrow"), None, None, None),
            P(("wide", "narrow"), None, None, None),
            P(("wide", "narrow"), None, None),
            P("wide", None),
            P("wide", None),
            P(),
            P(),
            P(),
            P(),
            P(),
            P(),
        ),
        out_specs=(
            P(("wide", "narrow"), None, None, None),
            P(("wide", "narrow"), None, None, None),
            P(),
        ),
        check_vma=False,
    )
```

```python
import functools

import jax
import jax.numpy as jnp
from jax import lax
from jax.experimental import pallas as pl
from jax.experimental.pallas import tpu as pltpu
from jax.sharding import PartitionSpec as P

G = 32
norm_eps = 1e-05
step_eps = 1e-06
MIB = 1 << 20
f32 = jnp.float32
bf16 = jnp.bfloat16

SMEM = pl.BlockSpec(memory_space=pltpu.SMEM)
VMEM = pl.BlockSpec(memory_space=pltpu.VMEM)


def params(limit, semantics=None):
    return pltpu.CompilerParams(vmem_limit_bytes=limit * MIB, dimension_semantics=semantics)


def cost(flops, size):
    return pl.CostEstimate(flops=flops, bytes_accessed=size, transcendentals=0)


def film_terms(timestep, film_weight):
    half_width = film_weight.shape[0] // 2
    channels = film_weight.shape[1] // 2
    frequencies = jnp.exp(
        -jnp.log(10000.0) * jnp.arange(half_width).astype(jnp.float32) / half_width
    )
    angles = timestep.astype(jnp.float32)[0] * frequencies
    embedding = jax.nn.silu(jnp.concatenate([jnp.cos(angles), jnp.sin(angles)]))
    film_out = jnp.dot(embedding[None, :], film_weight, precision=lax.Precision.HIGHEST)[0]
    return (film_out[:channels], film_out[channels:])


def plane_mask(occ_ref, slot, z, edge, channels):
    bit = lax.broadcasted_iota(jnp.int32, (edge, channels), 0)
    rows = [
        jnp.bitwise_and(jnp.right_shift(jnp.full((edge, channels), occ_ref[slot, z, y], jnp.int32), bit), 1)
        for y in range(edge)
    ]
    return jnp.concatenate(rows, axis=0) != 0


def x_row(rows, edge, channels):
    return lax.rem(lax.broadcasted_iota(jnp.int32, (rows, channels), 0), edge)


def pieces(value, count):
    found = []
    for _ in range(count):
        part = value.astype(bf16).astype(f32)
        found.append(part)
        value = value - part
    return found


def surface_kernel(edge, with_stats, fill, occ_ref, v_ref, out_ref, plane_s, edge_s, stat_s):
    channels = v_ref.shape[-1]
    last = edge - 1
    slot = pl.program_id(0)

    @pl.when(slot == 0)
    def _():
        stat_s[...] = jnp.zeros_like(stat_s)
        edge_s[...] = jnp.zeros_like(edge_s)

    def coded(z):
        mask = plane_mask(occ_ref, slot, z, edge, channels)
        values = v_ref[0, z].astype(f32)
        return (mask, values, jnp.where(mask, values, fill))

    def step(z, carry):
        mask, values, shown = coded(z)
        plane_s[...] = shown
        for side in range(2):
            row = side * last
            out_ref[z, 4 + 2 * slot + side] = shown[row * edge : (row + 1) * edge].astype(bf16)
            out_ref[z, 8 + 2 * slot + side] = plane_s[pl.ds(row, edge, stride=edge), :].astype(bf16)
        if not with_stats:
            return carry
        total, squares, count = carry
        masked = jnp.where(mask, values, 0.0)
        total = total + jnp.sum(masked, axis=0, keepdims=True)
        squares = squares + jnp.sum(masked * values, axis=0, keepdims=True)
        count = count + jnp.sum(mask.astype(f32), axis=0, keepdims=True)
        return (total, squares, count)

    zero = jnp.zeros((1, channels), f32)
    found = lax.fori_loop(0, edge, step, (zero, zero, zero) if with_stats else 0)
    if with_stats:
        for index in range(3):
            stat_s[index : index + 1, :] = stat_s[index : index + 1, :] + found[index]
    for z_side in range(2):
        _, _, shown = coded(z_side * last)
        for hub in range(edge):
            out_ref[hub, 2 * slot + z_side] = shown[hub * edge : (hub + 1) * edge].astype(bf16)
        for y_side in range(2):
            for hub in range(edge):
                first = y_side * last * edge + hub
                for place in range(2):

                    @pl.when(slot == place)
                    def _():
                        row = 4 * place + 2 * z_side + y_side
                        edge_s[hub, row : row + 1, :] = shown[first : first + 1]

    @pl.when(slot == 1)
    def _():
        if with_stats:
            parts = pieces(stat_s[0:1, :], 3) + pieces(stat_s[1:2, :], 3) + pieces(stat_s[2:3, :], 2)
            for hub in range(edge):
                for row, part in enumerate(parts):
                    edge_s[hub, 8 + row : 9 + row, :] = part
        for hub in range(edge):
            for tile in range(16 // edge):
                out_ref[hub, 12 + tile] = edge_s[hub, tile * edge : (tile + 1) * edge].astype(bf16)


def surface(occupancy, values, fill, with_stats):
    edge, cells, channels = values.shape[1:]
    tiles = 12 + 16 // edge
    return pl.pallas_call(
        functools.partial(surface_kernel, edge, with_stats, fill),
        grid=(2,),
        out_shape=jax.ShapeDtypeStruct((edge, tiles, edge, channels), bf16),
        in_specs=[SMEM, pl.BlockSpec((1, edge, cells, channels), lambda s: (s, 0, 0, 0))],
        out_specs=pl.BlockSpec((edge, tiles, edge, channels), lambda s: (0, 0, 0, 0)),
        scratch_shapes=[
            pltpu.VMEM((cells, channels), f32),
            pltpu.VMEM((edge, 16, channels), f32),
            pltpu.VMEM((8, channels), f32),
        ],
        compiler_params=params(60, ("arbitrary",)),
        cost_estimate=cost(0, 3 * MIB),
        name="surface",
    )(occupancy, values)


def trade_kernel(edge, live_ref, got_ref, left_ref, right_ref, stat_ref, ends_s):
    live_count = live_ref.shape[1]
    for k in range(live_count):
        slot = live_ref[0, k]
        owner, local = slot // 2, lax.rem(slot, 2)
        for side, out in ((0, left_ref), (1, right_ref)):
            out[k] = got_ref[owner, 8 + 2 * local + side]
            for z_side in range(2):
                tile = got_ref[owner, 2 * local + z_side].astype(f32)
                row = 2 * k + z_side
                x = side * (edge - 1)
                ends_s[side, row : row + 1, :] = tile[x : x + 1]
    for side, out in ((0, left_ref), (1, right_ref)):
        for tile in range(2 * live_count // edge):
            out[live_count + tile] = ends_s[side, tile * edge : (tile + 1) * edge].astype(bf16)
    rows = []
    for tile in range(8 // edge if edge < 16 else 0, 16 // edge):
        total = got_ref[0, 12 + tile].astype(f32)
        for source in range(1, edge):
            total = total + got_ref[source, 12 + tile].astype(f32)
        rows.append(total)
    rows = jnp.concatenate(rows, axis=0)
    if edge == 16:
        rows = rows[8:]
    stat_ref[...] = jnp.zeros_like(stat_ref)
    stat_ref[0:1, :] = rows[0:1] + rows[1:2] + rows[2:3]
    stat_ref[1:2, :] = rows[3:4] + rows[4:5] + rows[5:6]
    stat_ref[2:3, :] = rows[6:7] + rows[7:8]


def trade(live_slots, got):
    edge, channels = got.shape[2], got.shape[-1]
    live_count = live_slots.shape[1]
    tiles = live_count + 2 * live_count // edge
    payload = jax.ShapeDtypeStruct((tiles, edge, channels), bf16)
    return pl.pallas_call(
        functools.partial(trade_kernel, edge),
        out_shape=(payload, payload, jax.ShapeDtypeStruct((8, channels), f32)),
        in_specs=[SMEM, VMEM],
        out_specs=(VMEM, VMEM, VMEM),
        scratch_shapes=[pltpu.VMEM((2, 2 * live_count, channels), f32)],
        compiler_params=params(16),
        cost_estimate=cost(0, 2 * MIB),
        name="trade",
    )(live_slots, got)


def hub_kernel(edge, fill, place_ref, live_ref, near_ref, got_ref, lower_ref, upper_ref, out_ref, wide_s, rows_s):
    live_count = live_ref.shape[1]
    last = edge - 1
    hub, group = place_ref[0], place_ref[1]
    x_refs = (lower_ref, upper_ref)
    for side in range(2):
        wide_s[side] = x_refs[side][...].astype(f32)

    def entry(k, dz, dy, dx):
        number = near_ref[k, 9 * (dz + 1) + 3 * (dy + 1) + (dx + 1)]
        index = jnp.clip(number - (group + dx) * live_count, 0, live_count - 1)
        return (number >= 0, index)

    def own(k, dz, dy):
        there, index = entry(k, dz, dy, 0)
        slot = live_ref[0, index]
        return (there, slot // 2, lax.rem(slot, 2))

    def step(k, carry):
        slot = live_ref[0, k]
        owner, local = slot // 2, lax.rem(slot, 2)

        def put(tile, there, values):
            out_ref[owner, local, tile] = jnp.where(there, values, fill).astype(bf16)

        def put_row(row, there, values):
            rows_s[row : row + 1, :] = jnp.where(there, values, fill)

        for side in range(2):
            step_to = 2 * side - 1
            there, source, place = own(k, step_to, 0)
            put(side, there, got_ref[source, 2 * place + 1 - side].astype(f32))
            there, source, place = own(k, 0, step_to)
            put(2 + side, there, got_ref[source, 4 + 2 * place + 1 - side].astype(f32))
            there, index = entry(k, 0, 0, step_to)
            put(4 + side, there, wide_s[side, index])
        dz_corner = jnp.where(hub == last, -1, 1)
        for a in range(2):
            for b in range(2):
                there, source, place = own(k, 2 * a - 1, 2 * b - 1)
                row = 4 * place + 2 * (1 - a) + (1 - b)
                tile = got_ref[source, 12 + row // edge].astype(f32)
                picked = lax.broadcasted_iota(jnp.int32, tile.shape, 0) == lax.rem(row, edge)
                put_row(2 * a + b, there, jnp.sum(jnp.where(picked, tile, 0.0), axis=0, keepdims=True))
                there, index = entry(k, 2 * a - 1, 0, 2 * b - 1)
                row = 2 * index + (1 - a)
                tile = wide_s[b, live_count + row // edge]
                picked = lax.broadcasted_iota(jnp.int32, tile.shape, 0) == lax.rem(row, edge)
                put_row(4 + 2 * a + b, there, jnp.sum(jnp.where(picked, tile, 0.0), axis=0, keepdims=True))
                row = last if a == 0 else 0
                there, index = entry(k, 0, 2 * a - 1, 2 * b - 1)
                put_row(8 + 2 * a + b, there, wide_s[b, index, row : row + 1, :])
                there, index = entry(k, dz_corner, 2 * a - 1, 2 * b - 1)
                put_row(12 + 2 * a + b, there, wide_s[b, index, row : row + 1, :])
        for tile in range(16 // edge):
            out_ref[owner, local, 6 + tile] = rows_s[tile * edge : (tile + 1) * edge].astype(bf16)
        return carry

    lax.fori_loop(0, live_count, step, 0)


def hub_rows(place, live_slots, neighbours, got, lower, upper, fill):
    edge, channels = got.shape[2], got.shape[-1]
    return pl.pallas_call(
        functools.partial(hub_kernel, edge, fill),
        out_shape=jax.ShapeDtypeStruct((edge, 2, 6 + 16 // edge, edge, channels), bf16),
        in_specs=[SMEM, SMEM, SMEM, VMEM, VMEM, VMEM],
        out_specs=VMEM,
        scratch_shapes=[
            pltpu.VMEM((2,) + lower.shape, f32),
            pltpu.VMEM((16, channels), f32),
        ],
        compiler_params=params(16),
        cost_estimate=cost(0, 8 * MIB),
        name="hub_rows",
    )(place, live_slots, neighbours, got, lower, upper)


def exchange(values, axis):
    return lax.all_to_all(values, axis, split_axis=0, concat_axis=0, tiled=True)


def hub_stage(place, live_slots, neighbours, got, fill, with_stats=False):
    to_left, to_right, stats = trade(live_slots, got)
    count = lax.axis_size("wide")
    lower = lax.ppermute(to_right, "wide", [(i, i + 1) for i in range(count - 1)])
    upper = lax.ppermute(to_left, "wide", [(i + 1, i) for i in range(count - 1)])
    if with_stats:
        stats, lower, upper = lax.optimization_barrier((wide_round(stats, 1), lower, upper))
        stats = wide_round(stats, 4)
    return (hub_rows(place, live_slots, neighbours, got, lower, upper, fill), stats)


def coefficients(coef_ref):
    return [coef_ref[i : i + 1, :] for i in range(5)]


def set_halo(edge, rim_ref, pad_ref, pad_lead, shift_ref, shift_lead, xh_s, edge_s, change):
    last = edge - 1
    for hub in range(edge):
        tiles = [change(rim_ref[hub, 0, tile].astype(f32)) for tile in range(6 + 16 // edge)]
        for side in range(2):
            pad_ref[pad_lead + (side * (edge + 1), hub + 1)] = tiles[side].astype(bf16)
            pad_ref[pad_lead + (hub + 1, side * (edge + 1))] = tiles[2 + side].astype(bf16)
            xh_s[side, hub + 1, 8 : 8 + edge, :] = tiles[4 + side]

        def row(index):
            tile = tiles[6 + index // edge]
            return tile[index % edge : index % edge + 1]

        for a in range(2):
            for b in range(2):
                edge_s[2 * a + b, hub : hub + 1, :] = row(2 * a + b)
                xh_s[b, a * (edge + 1), 8 + hub : 9 + hub, :] = row(4 + 2 * a + b)
                y = 8 + edge if a else 7
                xh_s[b, hub + 1, y : y + 1, :] = row(8 + 2 * a + b)
                if hub == last:
                    xh_s[b, 0, y : y + 1, :] = row(12 + 2 * a + b)
                if hub == 0:
                    xh_s[b, edge + 1, y : y + 1, :] = row(12 + 2 * a + b)
    for a in range(2):
        for b in range(2):
            pad_ref[pad_lead + (a * (edge + 1), b * (edge + 1))] = edge_s[2 * a + b].astype(bf16)
    for side in range(2):
        for z in range(edge + 2):
            for y in range(3):
                shift_ref[shift_lead + (side, y, z)] = xh_s[side, z, 7 + y : 7 + y + edge, :].astype(bf16)


def hidden_plane(feats, mask, coef):
    mean, rstd, scale, shift = coef[:4]
    pre = (feats - mean) * rstd * scale + shift
    return jnp.where(mask, pre * jax.nn.sigmoid(pre), 0.0)


def weight_kernel(edge, occ_ref, live_ref, f_ref, g_ref, rim_ref, coef_ref, grad_ref, pad_ref, shift_ref,
                  hid_ref, acc_s, even_s, odd_s, xh_s, edge_s, plane_s, face_s):
    channels = f_ref.shape[-1]
    cells = edge * edge
    slot = pl.program_id(0)
    coef = coefficients(coef_ref)
    depth = min(4, edge // 2)
    chunks = edge // depth

    @pl.when(slot == 0)
    def _():
        acc_s[...] = jnp.zeros_like(acc_s)

    @pl.when(live_ref[slot] != 0)
    def _():
        set_halo(edge, rim_ref, pad_ref, (0,), shift_ref, (0,), xh_s, edge_s, lambda v: v)
        lane_x = lax.rem(lax.broadcasted_iota(jnp.int32, (channels, cells), 1), edge)

        def fill(z, carry):
            mask = plane_mask(occ_ref, slot, z, edge, channels)
            ups = jnp.where(mask, g_ref[0, z].astype(f32), 0.0).astype(bf16)
            pad_ref[0, z + 1, 1 : edge + 1] = ups.reshape(edge, edge, channels)
            return carry

        lax.fori_loop(0, edge, fill, 0)

        def prepare(chunk, flip_s, part):
            if part < depth:
                z = chunk * depth + part
                mask = plane_mask(occ_ref, slot, z, edge, channels)
                hidden = hidden_plane(f_ref[0, z].astype(f32), mask, coef).astype(bf16)
                hid_ref[0, z] = hidden
                hidden = hidden.astype(f32)
                plane_s[part] = hidden
                for side in range(2):
                    face_s[side, pl.ds(z * edge, edge), :] = plane_s[
                        part, pl.ds(side * (edge - 1), edge, stride=edge), :
                    ]
                flat = hidden.T
                before = jnp.where(lane_x == edge - 1, 0.0, pltpu.roll(flat, cells - 1, 1))
                after = jnp.where(lane_x == 0, 0.0, pltpu.roll(flat, 1, 1))
                columns = slice(part * cells, (part + 1) * cells)
                flip_s[0:channels, columns] = before.astype(bf16)
                flip_s[channels : 2 * channels, columns] = flat.astype(bf16)
                flip_s[2 * channels : 3 * channels, columns] = after.astype(bf16)

        def add(tap, px, values):
            pz, py = tap // 3, tap % 3
            offset = 9 * (2 - pz) + 3 * (2 - py) + (2 - px)
            acc_s[offset] = acc_s[offset] + values

        pairs = [(0, 1), (2, 3), (4, 5), (6, 7), (8,)]

        def multiply(chunk, flip_s, beside):
            z0 = chunk * depth
            left = flip_s[...]
            for turn, pair in enumerate(pairs):
                right = [
                    pad_ref[0, pl.ds(z0 + tap // 3, depth), tap % 3 : tap % 3 + edge].reshape(
                        depth * cells, channels
                    )
                    for tap in pair
                ]
                right = right[0] if len(right) == 1 else jnp.concatenate(right, axis=1)
                found = jnp.dot(left, right, preferred_element_type=f32)
                for place, tap in enumerate(pair):
                    for px in range(3):
                        add(
                            tap,
                            px,
                            found[
                                px * channels : (px + 1) * channels,
                                place * channels : (place + 1) * channels,
                            ],
                        )
                beside(turn)

        def two(i, carry):
            multiply(2 * i, even_s, functools.partial(prepare, 2 * i + 1, odd_s))
            multiply(2 * i + 1, odd_s, functools.partial(prepare, 2 * i + 2, even_s))
            return carry

        for part in range(depth):
            prepare(0, even_s, part)
        lax.fori_loop(0, chunks // 2 - 1, two, 0)
        multiply(chunks - 2, even_s, functools.partial(prepare, chunks - 1, odd_s))
        multiply(chunks - 1, odd_s, lambda turn: None)
        for side in range(2):
            left = face_s[side].T.astype(bf16)
            for tap in range(9):
                right = shift_ref[0, side, tap % 3, tap // 3 : tap // 3 + edge].reshape(cells, channels)
                add(tap, 2 * side, jnp.dot(left, right, preferred_element_type=f32))

    @pl.when(slot == 1)
    def _():
        grad_ref[...] = acc_s[...]


def weight_grad(occupancy, live, features, cotangent, rim, coef):
    edge, channels = features.shape[1], features.shape[-1]
    cells = edge * edge
    wide = edge + 2
    whole = pl.BlockSpec((1, edge, cells, channels), lambda s: (s, 0, 0, 0))
    return pl.pallas_call(
        functools.partial(weight_kernel, edge),
        grid=(2,),
        out_shape=(
            jax.ShapeDtypeStruct((27, channels, channels), f32),
            jax.ShapeDtypeStruct((2, wide, wide, edge, channels), bf16),
            jax.ShapeDtypeStruct((2, 2, 3, wide, edge, channels), bf16),
            jax.ShapeDtypeStruct(features.shape, bf16),
        ),
        in_specs=[
            SMEM,
            SMEM,
            whole,
            whole,
            pl.BlockSpec((edge, 1) + rim.shape[2:], lambda s: (0, s, 0, 0, 0)),
            pl.BlockSpec((8, channels), lambda s: (0, 0)),
        ],
        out_specs=(
            pl.BlockSpec((27, channels, channels), lambda s: (0, 0, 0)),
            pl.BlockSpec((1, wide, wide, edge, channels), lambda s: (s, 0, 0, 0, 0)),
            pl.BlockSpec((1, 2, 3, wide, edge, channels), lambda s: (s, 0, 0, 0, 0, 0)),
            whole,
        ),
        scratch_shapes=[
            pltpu.VMEM((27, channels, channels), f32),
            pltpu.VMEM((3 * channels, min(4, edge // 2) * cells), bf16),
            pltpu.VMEM((3 * channels, min(4, edge // 2) * cells), bf16),
            pltpu.VMEM((2, wide, 8 * ((edge + 16) // 8), channels), f32),
            pltpu.VMEM((4, edge, channels), f32),
            pltpu.VMEM((min(4, edge // 2), cells, channels), f32),
            pltpu.VMEM((2, cells, channels), f32),
        ],
        compiler_params=params(60, ("arbitrary",)),
        cost_estimate=cost(20 * 10**9, 8 * MIB),
        name="weight_grad",
    )(occupancy, live, features, cotangent, rim, coef)


def side_rows(edge, shift_ref, shift_lead, w_ref, side_s):
    cells = edge * edge
    channels = w_ref.shape[0] // 9
    for side in range(2):
        rows = jnp.concatenate(
            [
                shift_ref[shift_lead + (side, tap % 3, slice(tap // 3, tap // 3 + edge))].reshape(cells, channels)
                for tap in range(9)
            ],
            axis=1,
        )
        first = 2 * side * channels
        side_s[side] = jnp.dot(rows, w_ref[:, first : first + channels], preferred_element_type=f32)


DEPTH = 4


def conv_pipeline(edge, pad_ref, pad_lead, w_ref, side_s, found_s, finish_plane, carry):
    cells = edge * edge
    rows = DEPTH * cells
    channels = w_ref.shape[0] // 9
    groups = edge // DEPTH
    x_at = x_row(cells, edge, channels)
    spans = [slice(0, 2 * channels), slice(2 * channels, 3 * channels)]

    def multiply(group, buffer, span):
        z = group * DEPTH
        lines = jnp.concatenate(
            [
                pad_ref[pad_lead + (pl.ds(z + tap // 3, DEPTH), slice(tap % 3, tap % 3 + edge))].reshape(
                    rows, channels
                )
                for tap in range(9)
            ],
            axis=1,
        )
        found_s[buffer, :, span] = jnp.dot(lines, w_ref[:, span], preferred_element_type=f32)

    def combine(group, buffer, part, carry):
        z = group * DEPTH + part
        found = found_s[buffer, part * cells : (part + 1) * cells]

        def beside(side):
            line = side_s[side, pl.ds(pl.multiple_of(z * edge, edge), edge), :]
            return jnp.broadcast_to(line[:, None, :], (edge, edge, channels)).reshape(cells, channels)

        before = jnp.where(x_at == 0, beside(0), pltpu.roll(found[:, :channels], 1, 0))
        after = jnp.where(x_at == edge - 1, beside(1), pltpu.roll(found[:, 2 * channels :], cells - 1, 0))
        return finish_plane(z, found[:, channels : 2 * channels] + before + after, carry)

    def advance(group, buffer, carry):
        for part in range(DEPTH):
            if part % (DEPTH // 2) == 0:
                multiply(group + 1, 1 - buffer, spans[2 * part // DEPTH])
            carry = combine(group, buffer, part, carry)
        return carry

    def step(i, carry):
        return advance(2 * i + 1, 1, advance(2 * i, 0, carry))

    for span in spans:
        multiply(0, 0, span)
    carry = lax.fori_loop(0, groups // 2 - 1, step, carry)
    carry = advance(groups - 2, 0, carry)
    for part in range(DEPTH):
        carry = combine(groups - 1, 1, part, carry)
    return carry


def forward_block(edge, slot, occ_ref, f_ref, hid_ref, rim_ref, w_ref, coef, bias_ref, out_ref,
                  pad_s, shift_s, xh_s, edge_s, side_s, found_s):
    channels = f_ref.shape[-1]

    def activate(coded):
        return hidden_plane(coded, coded < jnp.inf, coef)

    set_halo(edge, rim_ref, pad_s, (), shift_s, (), xh_s, edge_s, activate)
    for z in range(edge):
        pad_s[z + 1, 1 : edge + 1] = hid_ref[0, z].reshape(edge, edge, channels)
    side_rows(edge, shift_s, (), w_ref, side_s)

    def plane(z, conv, carry):
        mask = plane_mask(occ_ref, slot, z, edge, channels)
        feats = f_ref[0, z].astype(f32)
        out_ref[0, z] = (feats + jnp.where(mask, conv + bias_ref[...], 0.0)).astype(bf16)
        return carry

    conv_pipeline(edge, pad_s, (), w_ref, side_s, found_s, plane, 0)


def convs_kernel(edge, occ_ref, live_ref, f_ref, pad_ref, shift_ref, back_ref, coef_ref, bias_ref,
                 hid_hbm, rim_hbm, forward_hbm, hat_hbm, sum_ref, out_ref,
                 side_s, found_s, hat_s, hid_s, rim_s, forward_s, pad_s, shift_s, xh_s, edge_s, sems):
    channels = f_ref.shape[-1]
    turn = pl.program_id(0)
    coef = coefficients(coef_ref)
    mean, rstd, scale, shift = coef[:4]
    fetches = [
        pltpu.make_async_copy(hid_hbm.at[pl.ds(0, 1)], hid_s, sems.at[0]),
        pltpu.make_async_copy(rim_hbm.at[:, pl.ds(0, 1)], rim_s, sems.at[1]),
        pltpu.make_async_copy(forward_hbm, forward_s, sems.at[2]),
    ]
    stores = [pltpu.make_async_copy(hat_s.at[slot], hat_hbm.at[slot], sems.at[3 + slot]) for slot in range(2)]

    @pl.when(turn == 0)
    def _():
        for fetch in fetches:
            fetch.start()
        sum_ref[...] = jnp.zeros_like(sum_ref)

    @pl.when(jnp.logical_and(turn < 2, live_ref[jnp.minimum(turn, 1)] != 0))
    def _():
        side_rows(edge, shift_ref, (0,), back_ref, side_s)

        def plane(z, back, carry):
            first, second = carry
            mask = plane_mask(occ_ref, turn, z, edge, channels)
            normed = (f_ref[0, z].astype(f32) - mean) * rstd
            pre = normed * scale + shift
            gate = jax.nn.sigmoid(pre)
            hat = jnp.where(mask, back * (gate * (1.0 + pre * (1.0 - gate))) * scale, 0.0)
            hat_s[turn, z] = hat
            first = first + jnp.sum(hat, axis=0, keepdims=True)
            second = second + jnp.sum(hat * normed, axis=0, keepdims=True)
            return (first, second)

        zero = jnp.zeros((1, channels), f32)
        first, second = conv_pipeline(edge, pad_ref, (0,), back_ref, side_s, found_s, plane, (zero, zero))
        sum_ref[0:1, :] = sum_ref[0:1, :] + first
        sum_ref[1:2, :] = sum_ref[1:2, :] + second

    for slot in range(2):

        @pl.when(turn == slot)
        def _():
            stores[slot].start()

    @pl.when(turn == 2)
    def _():
        for fetch in fetches:
            fetch.wait()

        @pl.when(live_ref[0] == 0)
        def _():
            out_ref[...] = f_ref[...]

        @pl.when(live_ref[0] != 0)
        def _():
            forward_block(edge, 0, occ_ref, f_ref, hid_s, rim_s, forward_s, coef, bias_ref, out_ref,
                          pad_s, shift_s, xh_s, edge_s, side_s, found_s)

        for store in stores:
            store.wait()


def forward_scratch(edge, channels):
    wide, cells = edge + 2, edge * edge
    return [
        pltpu.VMEM((wide, wide, edge, channels), bf16),
        pltpu.VMEM((2, 3, wide, edge, channels), bf16),
        pltpu.VMEM((2, wide, 8 * ((edge + 16) // 8), channels), f32),
        pltpu.VMEM((4, edge, channels), f32),
    ]


def conv_scratch(edge, channels):
    cells = edge * edge
    return [
        pltpu.VMEM((2, cells, channels), f32),
        pltpu.VMEM((2, DEPTH * cells, 3 * channels), f32),
    ]


def convs(occupancy, live, features, padded, shifted, back_weight, coef, bias, hidden, rim, forward_weight):
    edge, channels = features.shape[1], features.shape[-1]
    cells = edge * edge
    block = (1, edge, cells, channels)
    any_space = pl.BlockSpec(memory_space=pl.ANY)

    def small(rows):
        return pl.BlockSpec((rows, channels), lambda t: (0, 0))

    return pl.pallas_call(
        functools.partial(convs_kernel, edge),
        grid=(3,),
        out_shape=(
            jax.ShapeDtypeStruct((2, edge, cells, channels), f32),
            jax.ShapeDtypeStruct((8, channels), f32),
            jax.ShapeDtypeStruct(features.shape, bf16),
        ),
        in_specs=[
            SMEM,
            SMEM,
            pl.BlockSpec(block, lambda t: (t % 2, 0, 0, 0)),
            pl.BlockSpec((1,) + padded.shape[1:], lambda t: (jnp.minimum(t, 1), 0, 0, 0, 0)),
            pl.BlockSpec((1,) + shifted.shape[1:], lambda t: (jnp.minimum(t, 1), 0, 0, 0, 0, 0)),
            pl.BlockSpec(back_weight.shape, lambda t: (0, 0)),
            small(8),
            small(1),
            any_space,
            any_space,
            any_space,
        ],
        out_specs=(any_space, small(8), pl.BlockSpec(block, lambda t: (0, 0, 0, 0))),
        scratch_shapes=conv_scratch(edge, channels)
        + [
            pltpu.VMEM((2, edge, cells, channels), f32),
            pltpu.VMEM(block, bf16),
            pltpu.VMEM((edge, 1) + rim.shape[2:], bf16),
            pltpu.VMEM(forward_weight.shape, bf16),
        ]
        + forward_scratch(edge, channels)
        + [pltpu.SemaphoreType.DMA((5,))],
        compiler_params=params(60, ("arbitrary",)),
        cost_estimate=cost(30 * 10**9, 16 * MIB),
        name="convs",
    )(occupancy, live, features, padded, shifted, back_weight, coef, bias, hidden, rim, forward_weight)


def forward_kernel(edge, slot, occ_ref, live_ref, f_ref, hid_ref, rim_ref, w_ref, coef_ref, bias_ref, base_ref,
                   out_ref, side_s, found_s, *scratch):
    @pl.when(live_ref[slot] == 0)
    def _():
        out_ref[...] = f_ref[...]

    @pl.when(live_ref[slot] != 0)
    def _():
        forward_block(edge, slot, occ_ref, f_ref, hid_ref, rim_ref, w_ref, coefficients(coef_ref), bias_ref,
                      out_ref, *scratch, side_s, found_s)


def forward_conv(slot, occupancy, live, features, hidden, rim, weight, coef, bias, base):
    edge, channels = features.shape[1], features.shape[-1]
    whole = pl.BlockSpec((1, edge, edge * edge, channels), lambda s: (slot, 0, 0, 0))
    return pl.pallas_call(
        functools.partial(forward_kernel, edge, slot),
        grid=(1,),
        out_shape=jax.ShapeDtypeStruct(features.shape, bf16),
        in_specs=[
            SMEM,
            SMEM,
            whole,
            whole,
            pl.BlockSpec((edge, 1) + rim.shape[2:], lambda s: (0, slot, 0, 0, 0)),
            pl.BlockSpec(weight.shape, lambda s: (0, 0)),
            pl.BlockSpec((8, channels), lambda s: (0, 0)),
            pl.BlockSpec((1, channels), lambda s: (0, 0)),
            pl.BlockSpec(memory_space=pl.ANY),
        ],
        out_specs=whole,
        scratch_shapes=conv_scratch(edge, channels) + forward_scratch(edge, channels),
        input_output_aliases={8: 0},
        compiler_params=params(60, ("arbitrary",)),
        cost_estimate=cost(10 * 10**9, 4 * MIB),
        name="forward_conv",
    )(occupancy, live, features, hidden, rim, weight, coef, bias, base)


def finish_kernel(edge, occ_ref, live_ref, f_ref, g_ref, hat_ref, coef_ref, sums_ref, out_ref):
    channels = f_ref.shape[-1]
    slot = pl.program_id(0)
    mean, rstd = coef_ref[0:1, :], coef_ref[1:2, :]
    first, second = sums_ref[0:1, :], sums_ref[1:2, :]

    @pl.when(live_ref[slot] == 0)
    def _():
        out_ref[...] = g_ref[...]

    @pl.when(live_ref[slot] != 0)
    def _():
        def plane(z, carry):
            mask = plane_mask(occ_ref, slot, z, edge, channels)
            normed = (f_ref[0, z].astype(f32) - mean) * rstd
            change = rstd * (hat_ref[0, z] - first - normed * second)
            out_ref[0, z] = (g_ref[0, z].astype(f32) + jnp.where(mask, change, 0.0)).astype(bf16)
            return carry

        lax.fori_loop(0, edge, plane, 0)


def finish(occupancy, live, features, cotangent, hat, coef, sums):
    edge, channels = features.shape[1], features.shape[-1]
    few = pl.BlockSpec((1, edge, edge * edge, channels), lambda s: (s, 0, 0, 0))
    return pl.pallas_call(
        functools.partial(finish_kernel, edge),
        grid=(2,),
        out_shape=jax.ShapeDtypeStruct(features.shape, bf16),
        in_specs=[SMEM, SMEM, few, few, few] + [pl.BlockSpec((8, channels), lambda s: (0, 0))] * 2,
        out_specs=few,
        compiler_params=params(60, ("arbitrary",)),
        cost_estimate=cost(0, 12 * MIB),
        name="finish",
    )(occupancy, live, features, cotangent, hat, coef, sums)


def wide_round(values, step):
    count = lax.axis_size("wide")
    terms = [values]
    for turn in range(1, 4):
        route = [(i, i ^ (turn * step)) for i in range(count)]
        terms.append(lax.ppermute(values, "wide", route))
    return (terms[0] + terms[1]) + (terms[2] + terms[3])


def group_sums(rows, channels):
    width = channels // G
    which = jnp.arange(channels) // width
    same = (which[:, None] == which[None, :]).astype(f32)
    return jnp.dot(rows, same, precision=lax.Precision.HIGHEST)


def scale_kernel(rows, parts_ref, coef_ref, out_ref, sums_ref):
    channels = parts_ref.shape[-1]
    tail = jnp.zeros((parts_ref.shape[1] - rows, channels), f32)
    total = jnp.zeros((1, channels), f32)
    for part in range(parts_ref.shape[0]):
        values = parts_ref[part, 0:rows].astype(f32)
        total = total + jnp.sum(values * values, axis=0, keepdims=True)
        tail = tail + parts_ref[part, rows:].astype(f32)
    mean = jnp.sum(total, axis=1, keepdims=True) / out_ref.size
    factor = lax.rsqrt(mean + step_eps)
    for part in range(parts_ref.shape[0]):
        out_ref[part] = parts_ref[part, 0:rows].astype(f32) * factor
    first = tail[0:1] + tail[1:2] + tail[2:3]
    second = tail[3:4] + tail[4:5] + tail[5:6]
    both = jnp.concatenate([first, second] + [jnp.zeros_like(first)] * 6, axis=0)
    row = lax.broadcasted_iota(jnp.int32, (channels, channels), 0) // (channels // G)
    column = lax.broadcasted_iota(jnp.int32, (channels, channels), 1) // (channels // G)
    same = (row == column).astype(f32)
    grouped = jnp.dot(both, same, precision=lax.Precision.HIGHEST, preferred_element_type=f32)
    sums_ref[...] = grouped / coef_ref[4:5, :]


def reduce_weights(grads, sums, coef, tie):
    shape = grads.shape
    channels = shape[2]
    wide, narrow = lax.axis_size("wide"), lax.axis_size("narrow")
    rows = shape[0] * shape[1] // wide
    mine = lax.psum_scatter(grads.reshape(wide * rows, channels), "wide", scatter_dimension=0, tiled=True)
    deep = -(-rows // (8 * narrow)) * 8
    mine = jnp.pad(mine, ((0, deep * narrow - rows), (0, 0))).reshape(narrow, deep, channels)
    sums = jnp.broadcast_to(sums[None], (narrow,) + sums.shape)
    mine, tie = lax.optimization_barrier((mine, tie))
    mine = jnp.sum(exchange(jnp.concatenate([mine, sums], axis=1), "narrow"), axis=0)
    mine, sums = mine[:deep], mine[deep : deep + 2]
    mine = exchange(jnp.broadcast_to(mine.astype(bf16)[None], (narrow, deep, channels)), "narrow")
    high = lax.reduce_precision(sums, 8, 7)
    middle = lax.reduce_precision(sums - high, 8, 7)
    low = (sums - high) - middle
    tail = jnp.stack([high, middle, low], axis=1).reshape(6, channels).astype(bf16)
    mine = mine.reshape(narrow * deep, channels)[:rows]
    mine, tie = lax.optimization_barrier((mine, tie))
    mine = jnp.concatenate([mine, tail, jnp.zeros((2, channels), bf16)], axis=0)
    parts = lax.all_gather(mine, "wide")
    step, sums = pl.pallas_call(
        functools.partial(scale_kernel, rows),
        out_shape=(
            jax.ShapeDtypeStruct((wide, rows, channels), f32),
            jax.ShapeDtypeStruct((8, channels), f32),
        ),
        in_specs=[VMEM, VMEM],
        out_specs=(VMEM, VMEM),
        compiler_params=params(16),
        cost_estimate=cost(0, 3 * MIB),
        name="scale",
    )(parts, coef)
    return (step.reshape(shape), sums, tie)


def local(
    features,
    out_cotangent,
    occupancy,
    live_slots,
    neighbours,
    timestep,
    norm_gain,
    norm_bias,
    film_weight,
    conv_weight,
    conv_bias,
):
    channels = features.shape[-1]
    group_width = channels // G
    hub = lax.axis_index("narrow").astype(jnp.int32)
    place = jnp.stack([hub, lax.axis_index("wide").astype(jnp.int32)])
    mine = 2 * hub + jnp.arange(2, dtype=jnp.int32)
    live = jnp.any(live_slots[0][None, :] == mine[:, None], axis=1).astype(jnp.int32)

    taps = conv_weight.reshape(9, 3, channels, channels)
    forward_weight = taps.transpose(0, 2, 1, 3).reshape(9 * channels, 3 * channels)
    flipped = conv_weight[::-1].reshape(9, 3, channels, channels)
    back_weight = flipped.transpose(0, 3, 1, 2).reshape(9 * channels, 3 * channels)
    film_scale, film_shift = film_terms(timestep, film_weight)
    scale = norm_gain * (1.0 + film_scale)
    shift = norm_bias * (1.0 + film_scale) + film_shift

    up_got = exchange(surface(occupancy, out_cotangent, 0.0, False), "narrow")
    feat_message = surface(occupancy, features, float("inf"), True)
    feat_message, up_got, forward_weight, back_weight, scale, shift = lax.optimization_barrier(
        (feat_message, up_got, forward_weight, back_weight, scale, shift)
    )
    feat_got = exchange(feat_message, "narrow")
    up_rows, _ = hub_stage(place, live_slots, neighbours, up_got, 0.0)
    up_rows, feat_got = lax.optimization_barrier((up_rows, feat_got))
    up_rim = exchange(up_rows, "narrow")
    feat_rows, stats = hub_stage(place, live_slots, neighbours, feat_got, float("inf"), True)
    feat_rows, up_rim = lax.optimization_barrier((feat_rows, up_rim))
    feat_rim = exchange(feat_rows, "narrow")

    voxel_count = stats[2, 0] * group_width
    sums = group_sums(stats[:2], channels)
    mean = sums[0] / voxel_count
    rstd = lax.rsqrt(sums[1] / voxel_count - mean * mean + norm_eps)
    blank = jnp.zeros((channels,), f32)
    coef = jnp.stack([mean, rstd, scale, shift, blank + voxel_count, blank, blank, blank])

    grads, padded, shifted, hidden = weight_grad(occupancy, live, features, out_cotangent, up_rim, coef)
    bias = conv_bias[None, :]
    hat, grad_sums, mixed = convs(
        occupancy, live, features, padded, shifted, back_weight, coef, bias, hidden, feat_rim, forward_weight
    )
    weight_step, grad_sums, mixed = reduce_weights(grads, grad_sums, coef, mixed)
    mixed = forward_conv(1, occupancy, live, features, hidden, feat_rim, forward_weight, coef, bias, mixed)
    feature_grad = finish(occupancy, live, features, out_cotangent, hat, coef, grad_sums)
    return (mixed, feature_grad, weight_step)


def solution(mesh):
    return jax.shard_map(
        local,
        mesh=mesh,
        in_specs=(
            P(("wide", "narrow"), None, None, None),
            P(("wide", "narrow"), None, None, None),
            P(("wide", "narrow"), None, None),
            P("wide", None),
            P("wide", None),
            P(),
            P(),
            P(),
            P(),
            P(),
            P(),
        ),
        out_specs=(
            P(("wide", "narrow"), None, None, None),
            P(("wide", "narrow"), None, None, None),
            P(),
        ),
        check_vma=False,
    )
```

```python
import functools

import jax
import jax.numpy as jnp
from jax import lax
from jax.experimental import pallas as pl
from jax.experimental.pallas import tpu as pltpu
from jax.sharding import PartitionSpec as P

G = 32
norm_eps = 1e-05
step_eps = 1e-06
MIB = 1 << 20
f32 = jnp.float32
bf16 = jnp.bfloat16

SMEM = pl.BlockSpec(memory_space=pltpu.SMEM)
VMEM = pl.BlockSpec(memory_space=pltpu.VMEM)


def params(limit, semantics=None):
    return pltpu.CompilerParams(vmem_limit_bytes=limit * MIB, dimension_semantics=semantics)


def cost(flops, size):
    return pl.CostEstimate(flops=flops, bytes_accessed=size, transcendentals=0)


def film_terms(timestep, film_weight):
    half_width = film_weight.shape[0] // 2
    channels = film_weight.shape[1] // 2
    frequencies = jnp.exp(
        -jnp.log(10000.0) * jnp.arange(half_width).astype(jnp.float32) / half_width
    )
    angles = timestep.astype(jnp.float32)[0] * frequencies
    embedding = jax.nn.silu(jnp.concatenate([jnp.cos(angles), jnp.sin(angles)]))
    film_out = jnp.dot(embedding[None, :], film_weight, precision=lax.Precision.HIGHEST)[0]
    return (film_out[:channels], film_out[channels:])


def plane_mask(occ_ref, slot, z, edge, channels):
    bit = lax.broadcasted_iota(jnp.int32, (edge, channels), 0)
    rows = [
        jnp.bitwise_and(jnp.right_shift(jnp.full((edge, channels), occ_ref[slot, z, y], jnp.int32), bit), 1)
        for y in range(edge)
    ]
    return jnp.concatenate(rows, axis=0) != 0


def x_row(rows, edge, channels):
    return lax.rem(lax.broadcasted_iota(jnp.int32, (rows, channels), 0), edge)


def pieces(value, count):
    found = []
    for _ in range(count):
        part = value.astype(bf16).astype(f32)
        found.append(part)
        value = value - part
    return found


def surface_kernel(edge, with_stats, fill, occ_ref, v_ref, out_ref, plane_s, edge_s, stat_s):
    channels = v_ref.shape[-1]
    last = edge - 1
    slot = pl.program_id(0)

    @pl.when(slot == 0)
    def _():
        stat_s[...] = jnp.zeros_like(stat_s)
        edge_s[...] = jnp.zeros_like(edge_s)

    def coded(z):
        mask = plane_mask(occ_ref, slot, z, edge, channels)
        values = v_ref[0, z].astype(f32)
        return (mask, values, jnp.where(mask, values, fill))

    def step(z, carry):
        mask, values, shown = coded(z)
        plane_s[...] = shown
        for side in range(2):
            row = side * last
            out_ref[z, 4 + 2 * slot + side] = shown[row * edge : (row + 1) * edge].astype(bf16)
            out_ref[z, 8 + 2 * slot + side] = plane_s[pl.ds(row, edge, stride=edge), :].astype(bf16)
        if not with_stats:
            return carry
        total, squares, count = carry
        masked = jnp.where(mask, values, 0.0)
        total = total + jnp.sum(masked, axis=0, keepdims=True)
        squares = squares + jnp.sum(masked * values, axis=0, keepdims=True)
        count = count + jnp.sum(mask.astype(f32), axis=0, keepdims=True)
        return (total, squares, count)

    zero = jnp.zeros((1, channels), f32)
    found = lax.fori_loop(0, edge, step, (zero, zero, zero) if with_stats else 0)
    if with_stats:
        for index in range(3):
            stat_s[index : index + 1, :] = stat_s[index : index + 1, :] + found[index]
    for z_side in range(2):
        _, _, shown = coded(z_side * last)
        for hub in range(edge):
            out_ref[hub, 2 * slot + z_side] = shown[hub * edge : (hub + 1) * edge].astype(bf16)
        for y_side in range(2):
            for hub in range(edge):
                first = y_side * last * edge + hub
                for place in range(2):

                    @pl.when(slot == place)
                    def _():
                        row = 4 * place + 2 * z_side + y_side
                        edge_s[hub, row : row + 1, :] = shown[first : first + 1]

    @pl.when(slot == 1)
    def _():
        if with_stats:
            parts = pieces(stat_s[0:1, :], 3) + pieces(stat_s[1:2, :], 3) + pieces(stat_s[2:3, :], 2)
            for hub in range(edge):
                for row, part in enumerate(parts):
                    edge_s[hub, 8 + row : 9 + row, :] = part
        for hub in range(edge):
            for tile in range(16 // edge):
                out_ref[hub, 12 + tile] = edge_s[hub, tile * edge : (tile + 1) * edge].astype(bf16)


def surface(occupancy, values, fill, with_stats):
    edge, cells, channels = values.shape[1:]
    tiles = 12 + 16 // edge
    return pl.pallas_call(
        functools.partial(surface_kernel, edge, with_stats, fill),
        grid=(2,),
        out_shape=jax.ShapeDtypeStruct((edge, tiles, edge, channels), bf16),
        in_specs=[SMEM, pl.BlockSpec((1, edge, cells, channels), lambda s: (s, 0, 0, 0))],
        out_specs=pl.BlockSpec((edge, tiles, edge, channels), lambda s: (0, 0, 0, 0)),
        scratch_shapes=[
            pltpu.VMEM((cells, channels), f32),
            pltpu.VMEM((edge, 16, channels), f32),
            pltpu.VMEM((8, channels), f32),
        ],
        compiler_params=params(60, ("arbitrary",)),
        cost_estimate=cost(0, 3 * MIB),
        name="surface",
    )(occupancy, values)


def trade_kernel(edge, live_ref, got_ref, left_ref, right_ref, stat_ref, ends_s):
    live_count = live_ref.shape[1]
    for k in range(live_count):
        slot = live_ref[0, k]
        owner, local = slot // 2, lax.rem(slot, 2)
        for side, out in ((0, left_ref), (1, right_ref)):
            out[k] = got_ref[owner, 8 + 2 * local + side]
            for z_side in range(2):
                tile = got_ref[owner, 2 * local + z_side].astype(f32)
                row = 2 * k + z_side
                x = side * (edge - 1)
                ends_s[side, row : row + 1, :] = tile[x : x + 1]
    for side, out in ((0, left_ref), (1, right_ref)):
        for tile in range(2 * live_count // edge):
            out[live_count + tile] = ends_s[side, tile * edge : (tile + 1) * edge].astype(bf16)
    rows = []
    for tile in range(8 // edge if edge < 16 else 0, 16 // edge):
        total = got_ref[0, 12 + tile].astype(f32)
        for source in range(1, edge):
            total = total + got_ref[source, 12 + tile].astype(f32)
        rows.append(total)
    rows = jnp.concatenate(rows, axis=0)
    if edge == 16:
        rows = rows[8:]
    stat_ref[...] = jnp.zeros_like(stat_ref)
    stat_ref[0:1, :] = rows[0:1] + rows[1:2] + rows[2:3]
    stat_ref[1:2, :] = rows[3:4] + rows[4:5] + rows[5:6]
    stat_ref[2:3, :] = rows[6:7] + rows[7:8]


def trade(live_slots, got):
    edge, channels = got.shape[2], got.shape[-1]
    live_count = live_slots.shape[1]
    tiles = live_count + 2 * live_count // edge
    payload = jax.ShapeDtypeStruct((tiles, edge, channels), bf16)
    return pl.pallas_call(
        functools.partial(trade_kernel, edge),
        out_shape=(payload, payload, jax.ShapeDtypeStruct((8, channels), f32)),
        in_specs=[SMEM, VMEM],
        out_specs=(VMEM, VMEM, VMEM),
        scratch_shapes=[pltpu.VMEM((2, 2 * live_count, channels), f32)],
        compiler_params=params(16),
        cost_estimate=cost(0, 2 * MIB),
        name="trade",
    )(live_slots, got)


def hub_kernel(edge, fill, place_ref, live_ref, near_ref, got_ref, lower_ref, upper_ref, out_ref, wide_s, rows_s):
    live_count = live_ref.shape[1]
    last = edge - 1
    hub, group = place_ref[0], place_ref[1]
    x_refs = (lower_ref, upper_ref)
    for side in range(2):
        wide_s[side] = x_refs[side][...].astype(f32)

    def entry(k, dz, dy, dx):
        number = near_ref[k, 9 * (dz + 1) + 3 * (dy + 1) + (dx + 1)]
        index = jnp.clip(number - (group + dx) * live_count, 0, live_count - 1)
        return (number >= 0, index)

    def own(k, dz, dy):
        there, index = entry(k, dz, dy, 0)
        slot = live_ref[0, index]
        return (there, slot // 2, lax.rem(slot, 2))

    def step(k, carry):
        slot = live_ref[0, k]
        owner, local = slot // 2, lax.rem(slot, 2)

        def put(tile, there, values):
            out_ref[owner, local, tile] = jnp.where(there, values, fill).astype(bf16)

        def put_row(row, there, values):
            rows_s[row : row + 1, :] = jnp.where(there, values, fill)

        for side in range(2):
            step_to = 2 * side - 1
            there, source, place = own(k, step_to, 0)
            put(side, there, got_ref[source, 2 * place + 1 - side].astype(f32))
            there, source, place = own(k, 0, step_to)
            put(2 + side, there, got_ref[source, 4 + 2 * place + 1 - side].astype(f32))
            there, index = entry(k, 0, 0, step_to)
            put(4 + side, there, wide_s[side, index])
        dz_corner = jnp.where(hub == last, -1, 1)
        for a in range(2):
            for b in range(2):
                there, source, place = own(k, 2 * a - 1, 2 * b - 1)
                row = 4 * place + 2 * (1 - a) + (1 - b)
                tile = got_ref[source, 12 + row // edge].astype(f32)
                picked = lax.broadcasted_iota(jnp.int32, tile.shape, 0) == lax.rem(row, edge)
                put_row(2 * a + b, there, jnp.sum(jnp.where(picked, tile, 0.0), axis=0, keepdims=True))
                there, index = entry(k, 2 * a - 1, 0, 2 * b - 1)
                row = 2 * index + (1 - a)
                tile = wide_s[b, live_count + row // edge]
                picked = lax.broadcasted_iota(jnp.int32, tile.shape, 0) == lax.rem(row, edge)
                put_row(4 + 2 * a + b, there, jnp.sum(jnp.where(picked, tile, 0.0), axis=0, keepdims=True))
                row = last if a == 0 else 0
                there, index = entry(k, 0, 2 * a - 1, 2 * b - 1)
                put_row(8 + 2 * a + b, there, wide_s[b, index, row : row + 1, :])
                there, index = entry(k, dz_corner, 2 * a - 1, 2 * b - 1)
                put_row(12 + 2 * a + b, there, wide_s[b, index, row : row + 1, :])
        for tile in range(16 // edge):
            out_ref[owner, local, 6 + tile] = rows_s[tile * edge : (tile + 1) * edge].astype(bf16)
        return carry

    lax.fori_loop(0, live_count, step, 0)


def hub_rows(place, live_slots, neighbours, got, lower, upper, fill):
    edge, channels = got.shape[2], got.shape[-1]
    return pl.pallas_call(
        functools.partial(hub_kernel, edge, fill),
        out_shape=jax.ShapeDtypeStruct((edge, 2, 6 + 16 // edge, edge, channels), bf16),
        in_specs=[SMEM, SMEM, SMEM, VMEM, VMEM, VMEM],
        out_specs=VMEM,
        scratch_shapes=[
            pltpu.VMEM((2,) + lower.shape, f32),
            pltpu.VMEM((16, channels), f32),
        ],
        compiler_params=params(16),
        cost_estimate=cost(0, 8 * MIB),
        name="hub_rows",
    )(place, live_slots, neighbours, got, lower, upper)


def exchange(values, axis):
    return lax.all_to_all(values, axis, split_axis=0, concat_axis=0, tiled=True)


def hub_stage(place, live_slots, neighbours, got, fill, with_stats=False):
    to_left, to_right, stats = trade(live_slots, got)
    count = lax.axis_size("wide")
    lower = lax.ppermute(to_right, "wide", [(i, i + 1) for i in range(count - 1)])
    upper = lax.ppermute(to_left, "wide", [(i + 1, i) for i in range(count - 1)])
    if with_stats:
        stats, lower, upper = lax.optimization_barrier((wide_round(stats, 1), lower, upper))
        stats = wide_round(stats, 4)
    return (hub_rows(place, live_slots, neighbours, got, lower, upper, fill), stats)


def coefficients(coef_ref):
    return [coef_ref[i : i + 1, :] for i in range(5)]


def set_halo(edge, rim_ref, pad_ref, pad_lead, shift_ref, shift_lead, xh_s, edge_s, change):
    last = edge - 1
    for hub in range(edge):
        tiles = [change(rim_ref[hub, 0, tile].astype(f32)) for tile in range(6 + 16 // edge)]
        for side in range(2):
            pad_ref[pad_lead + (side * (edge + 1), hub + 1)] = tiles[side].astype(bf16)
            pad_ref[pad_lead + (hub + 1, side * (edge + 1))] = tiles[2 + side].astype(bf16)
            xh_s[side, hub + 1, 8 : 8 + edge, :] = tiles[4 + side]

        def row(index):
            tile = tiles[6 + index // edge]
            return tile[index % edge : index % edge + 1]

        for a in range(2):
            for b in range(2):
                edge_s[2 * a + b, hub : hub + 1, :] = row(2 * a + b)
                xh_s[b, a * (edge + 1), 8 + hub : 9 + hub, :] = row(4 + 2 * a + b)
                y = 8 + edge if a else 7
                xh_s[b, hub + 1, y : y + 1, :] = row(8 + 2 * a + b)
                if hub == last:
                    xh_s[b, 0, y : y + 1, :] = row(12 + 2 * a + b)
                if hub == 0:
                    xh_s[b, edge + 1, y : y + 1, :] = row(12 + 2 * a + b)
    for a in range(2):
        for b in range(2):
            pad_ref[pad_lead + (a * (edge + 1), b * (edge + 1))] = edge_s[2 * a + b].astype(bf16)
    for side in range(2):
        for z in range(edge + 2):
            for y in range(3):
                shift_ref[shift_lead + (side, y, z)] = xh_s[side, z, 7 + y : 7 + y + edge, :].astype(bf16)


def hidden_plane(feats, mask, coef):
    mean, rstd, scale, shift = coef[:4]
    pre = (feats - mean) * rstd * scale + shift
    return jnp.where(mask, pre * jax.nn.sigmoid(pre), 0.0)


def weight_kernel(edge, occ_ref, live_ref, f_ref, g_ref, rim_ref, coef_ref, grad_ref, pad_ref, shift_ref,
                  hid_ref, acc_s, even_s, odd_s, xh_s, edge_s, plane_s, face_s):
    channels = f_ref.shape[-1]
    cells = edge * edge
    slot = pl.program_id(0)
    coef = coefficients(coef_ref)
    depth = min(4, edge // 2)
    chunks = edge // depth

    @pl.when(slot == 0)
    def _():
        acc_s[...] = jnp.zeros_like(acc_s)

    @pl.when(live_ref[slot] != 0)
    def _():
        set_halo(edge, rim_ref, pad_ref, (0,), shift_ref, (0,), xh_s, edge_s, lambda v: v)
        lane_x = lax.rem(lax.broadcasted_iota(jnp.int32, (channels, cells), 1), edge)

        def fill(z, carry):
            mask = plane_mask(occ_ref, slot, z, edge, channels)
            ups = jnp.where(mask, g_ref[0, z].astype(f32), 0.0).astype(bf16)
            pad_ref[0, z + 1, 1 : edge + 1] = ups.reshape(edge, edge, channels)
            return carry

        lax.fori_loop(0, edge, fill, 0)

        def prepare(chunk, flip_s, part):
            if part < depth:
                z = chunk * depth + part
                mask = plane_mask(occ_ref, slot, z, edge, channels)
                hidden = hidden_plane(f_ref[0, z].astype(f32), mask, coef).astype(bf16)
                hid_ref[0, z] = hidden
                hidden = hidden.astype(f32)
                plane_s[part] = hidden
                for side in range(2):
                    face_s[side, pl.ds(z * edge, edge), :] = plane_s[
                        part, pl.ds(side * (edge - 1), edge, stride=edge), :
                    ]
                flat = hidden.T
                before = jnp.where(lane_x == edge - 1, 0.0, pltpu.roll(flat, cells - 1, 1))
                after = jnp.where(lane_x == 0, 0.0, pltpu.roll(flat, 1, 1))
                columns = slice(part * cells, (part + 1) * cells)
                flip_s[0:channels, columns] = before.astype(bf16)
                flip_s[channels : 2 * channels, columns] = flat.astype(bf16)
                flip_s[2 * channels : 3 * channels, columns] = after.astype(bf16)

        def add(tap, px, values):
            pz, py = tap // 3, tap % 3
            offset = 9 * (2 - pz) + 3 * (2 - py) + (2 - px)
            acc_s[offset] = acc_s[offset] + values

        pairs = [(0, 1), (2, 3), (4, 5), (6, 7), (8,)]

        def multiply(chunk, flip_s, beside):
            z0 = chunk * depth
            left = flip_s[...]
            for turn, pair in enumerate(pairs):
                right = [
                    pad_ref[0, pl.ds(z0 + tap // 3, depth), tap % 3 : tap % 3 + edge].reshape(
                        depth * cells, channels
                    )
                    for tap in pair
                ]
                right = right[0] if len(right) == 1 else jnp.concatenate(right, axis=1)
                found = jnp.dot(left, right, preferred_element_type=f32)
                for place, tap in enumerate(pair):
                    for px in range(3):
                        add(
                            tap,
                            px,
                            found[
                                px * channels : (px + 1) * channels,
                                place * channels : (place + 1) * channels,
                            ],
                        )
                beside(turn)

        def two(i, carry):
            multiply(2 * i, even_s, functools.partial(prepare, 2 * i + 1, odd_s))
            multiply(2 * i + 1, odd_s, functools.partial(prepare, 2 * i + 2, even_s))
            return carry

        for part in range(depth):
            prepare(0, even_s, part)
        lax.fori_loop(0, chunks // 2 - 1, two, 0)
        multiply(chunks - 2, even_s, functools.partial(prepare, chunks - 1, odd_s))
        multiply(chunks - 1, odd_s, lambda turn: None)
        for side in range(2):
            left = face_s[side].T.astype(bf16)
            for tap in range(9):
                right = shift_ref[0, side, tap % 3, tap // 3 : tap // 3 + edge].reshape(cells, channels)
                add(tap, 2 * side, jnp.dot(left, right, preferred_element_type=f32))

    @pl.when(slot == 1)
    def _():
        grad_ref[...] = acc_s[...]


def weight_grad(occupancy, live, features, cotangent, rim, coef):
    edge, channels = features.shape[1], features.shape[-1]
    cells = edge * edge
    wide = edge + 2
    whole = pl.BlockSpec((1, edge, cells, channels), lambda s: (s, 0, 0, 0))
    return pl.pallas_call(
        functools.partial(weight_kernel, edge),
        grid=(2,),
        out_shape=(
            jax.ShapeDtypeStruct((27, channels, channels), f32),
            jax.ShapeDtypeStruct((2, wide, wide, edge, channels), bf16),
            jax.ShapeDtypeStruct((2, 2, 3, wide, edge, channels), bf16),
            jax.ShapeDtypeStruct(features.shape, bf16),
        ),
        in_specs=[
            SMEM,
            SMEM,
            whole,
            whole,
            pl.BlockSpec((edge, 1) + rim.shape[2:], lambda s: (0, s, 0, 0, 0)),
            pl.BlockSpec((8, channels), lambda s: (0, 0)),
        ],
        out_specs=(
            pl.BlockSpec((27, channels, channels), lambda s: (0, 0, 0)),
            pl.BlockSpec((1, wide, wide, edge, channels), lambda s: (s, 0, 0, 0, 0)),
            pl.BlockSpec((1, 2, 3, wide, edge, channels), lambda s: (s, 0, 0, 0, 0, 0)),
            whole,
        ),
        scratch_shapes=[
            pltpu.VMEM((27, channels, channels), f32),
            pltpu.VMEM((3 * channels, min(4, edge // 2) * cells), bf16),
            pltpu.VMEM((3 * channels, min(4, edge // 2) * cells), bf16),
            pltpu.VMEM((2, wide, 8 * ((edge + 16) // 8), channels), f32),
            pltpu.VMEM((4, edge, channels), f32),
            pltpu.VMEM((min(4, edge // 2), cells, channels), f32),
            pltpu.VMEM((2, cells, channels), f32),
        ],
        compiler_params=params(60, ("arbitrary",)),
        cost_estimate=cost(10**8, MIB),
        name="weight_grad",
    )(occupancy, live, features, cotangent, rim, coef)


def side_rows(edge, shift_ref, shift_lead, w_ref, side_s):
    cells = edge * edge
    channels = w_ref.shape[0] // 9
    for side in range(2):
        rows = jnp.concatenate(
            [
                shift_ref[shift_lead + (side, tap % 3, slice(tap // 3, tap // 3 + edge))].reshape(cells, channels)
                for tap in range(9)
            ],
            axis=1,
        )
        first = 2 * side * channels
        side_s[side] = jnp.dot(rows, w_ref[:, first : first + channels], preferred_element_type=f32)


DEPTH = 4


def conv_pipeline(edge, pad_ref, pad_lead, w_ref, side_s, found_s, finish_plane, carry):
    cells = edge * edge
    rows = DEPTH * cells
    channels = w_ref.shape[0] // 9
    groups = edge // DEPTH
    x_at = x_row(cells, edge, channels)
    spans = [slice(0, 2 * channels), slice(2 * channels, 3 * channels)]

    def multiply(group, buffer, span):
        z = group * DEPTH
        lines = jnp.concatenate(
            [
                pad_ref[pad_lead + (pl.ds(z + tap // 3, DEPTH), slice(tap % 3, tap % 3 + edge))].reshape(
                    rows, channels
                )
                for tap in range(9)
            ],
            axis=1,
        )
        found_s[buffer, :, span] = jnp.dot(lines, w_ref[:, span], preferred_element_type=f32)

    def combine(group, buffer, part, carry):
        z = group * DEPTH + part
        found = found_s[buffer, part * cells : (part + 1) * cells]

        def beside(side):
            line = side_s[side, pl.ds(pl.multiple_of(z * edge, edge), edge), :]
            return jnp.broadcast_to(line[:, None, :], (edge, edge, channels)).reshape(cells, channels)

        before = jnp.where(x_at == 0, beside(0), pltpu.roll(found[:, :channels], 1, 0))
        after = jnp.where(x_at == edge - 1, beside(1), pltpu.roll(found[:, 2 * channels :], cells - 1, 0))
        return finish_plane(z, found[:, channels : 2 * channels] + before + after, carry)

    def advance(group, buffer, carry):
        for part in range(DEPTH):
            if part % (DEPTH // 2) == 0:
                multiply(group + 1, 1 - buffer, spans[2 * part // DEPTH])
            carry = combine(group, buffer, part, carry)
        return carry

    def step(i, carry):
        return advance(2 * i + 1, 1, advance(2 * i, 0, carry))

    for span in spans:
        multiply(0, 0, span)
    carry = lax.fori_loop(0, groups // 2 - 1, step, carry)
    carry = advance(groups - 2, 0, carry)
    for part in range(DEPTH):
        carry = combine(groups - 1, 1, part, carry)
    return carry


def forward_block(edge, slot, occ_ref, f_ref, hid_ref, rim_ref, w_ref, coef, bias_ref, out_ref,
                  pad_s, shift_s, xh_s, edge_s, side_s, found_s):
    channels = f_ref.shape[-1]

    def activate(coded):
        return hidden_plane(coded, coded < jnp.inf, coef)

    set_halo(edge, rim_ref, pad_s, (), shift_s, (), xh_s, edge_s, activate)
    for z in range(edge):
        pad_s[z + 1, 1 : edge + 1] = hid_ref[0, z].reshape(edge, edge, channels)
    side_rows(edge, shift_s, (), w_ref, side_s)

    def plane(z, conv, carry):
        mask = plane_mask(occ_ref, slot, z, edge, channels)
        feats = f_ref[0, z].astype(f32)
        out_ref[0, z] = (feats + jnp.where(mask, conv + bias_ref[...], 0.0)).astype(bf16)
        return carry

    conv_pipeline(edge, pad_s, (), w_ref, side_s, found_s, plane, 0)


def convs_kernel(edge, occ_ref, live_ref, f_ref, g_ref, pad_ref, shift_ref, back_ref, coef_ref, bias_ref,
                 hid_hbm, rim_hbm, forward_hbm, hat_hbm, sum_ref, out_ref,
                 side_s, found_s, hat_s, hid_s, rim_s, forward_s, pad_s, shift_s, xh_s, edge_s, sems):
    channels = f_ref.shape[-1]
    turn = pl.program_id(0)
    coef = coefficients(coef_ref)
    mean, rstd, scale, shift = coef[:4]
    fetches = [
        pltpu.make_async_copy(hid_hbm.at[pl.ds(0, 1)], hid_s, sems.at[0]),
        pltpu.make_async_copy(rim_hbm.at[:, pl.ds(0, 1)], rim_s, sems.at[1]),
        pltpu.make_async_copy(forward_hbm, forward_s, sems.at[2]),
    ]
    stores = [pltpu.make_async_copy(hat_s.at[slot], hat_hbm.at[slot], sems.at[3 + slot]) for slot in range(2)]

    @pl.when(turn == 0)
    def _():
        for fetch in fetches:
            fetch.start()
        sum_ref[...] = jnp.zeros_like(sum_ref)

    @pl.when(jnp.logical_and(turn < 2, live_ref[jnp.minimum(turn, 1)] != 0))
    def _():
        side_rows(edge, shift_ref, (0,), back_ref, side_s)

        def plane(z, back, carry):
            first, second = carry
            mask = plane_mask(occ_ref, turn, z, edge, channels)
            normed = (f_ref[0, z].astype(f32) - mean) * rstd
            pre = normed * scale + shift
            gate = jax.nn.sigmoid(pre)
            hat = jnp.where(mask, back * (gate * (1.0 + pre * (1.0 - gate))) * scale, 0.0)
            hat_s[turn, z] = g_ref[0, z].astype(f32) + rstd * hat
            first = first + jnp.sum(hat, axis=0, keepdims=True)
            second = second + jnp.sum(hat * normed, axis=0, keepdims=True)
            return (first, second)

        zero = jnp.zeros((1, channels), f32)
        first, second = conv_pipeline(edge, pad_ref, (0,), back_ref, side_s, found_s, plane, (zero, zero))
        sum_ref[0:1, :] = sum_ref[0:1, :] + first
        sum_ref[1:2, :] = sum_ref[1:2, :] + second

    for slot in range(2):

        @pl.when(jnp.logical_and(turn == slot, live_ref[slot] == 0))
        def _():
            def plane(z, carry):
                hat_s[slot, z] = g_ref[0, z].astype(f32)
                return carry

            lax.fori_loop(0, edge, plane, 0)

        @pl.when(turn == slot)
        def _():
            stores[slot].start()

    @pl.when(turn == 2)
    def _():
        for fetch in fetches:
            fetch.wait()

        @pl.when(live_ref[0] == 0)
        def _():
            out_ref[...] = f_ref[...]

        @pl.when(live_ref[0] != 0)
        def _():
            forward_block(edge, 0, occ_ref, f_ref, hid_s, rim_s, forward_s, coef, bias_ref, out_ref,
                          pad_s, shift_s, xh_s, edge_s, side_s, found_s)

        for store in stores:
            store.wait()


def forward_scratch(edge, channels):
    wide, cells = edge + 2, edge * edge
    return [
        pltpu.VMEM((wide, wide, edge, channels), bf16),
        pltpu.VMEM((2, 3, wide, edge, channels), bf16),
        pltpu.VMEM((2, wide, 8 * ((edge + 16) // 8), channels), f32),
        pltpu.VMEM((4, edge, channels), f32),
    ]


def conv_scratch(edge, channels):
    cells = edge * edge
    return [
        pltpu.VMEM((2, cells, channels), f32),
        pltpu.VMEM((2, DEPTH * cells, 3 * channels), f32),
    ]


def convs(occupancy, live, features, cotangent, padded, shifted, back_weight, coef, bias, hidden, rim, forward_weight):
    edge, channels = features.shape[1], features.shape[-1]
    cells = edge * edge
    block = (1, edge, cells, channels)
    any_space = pl.BlockSpec(memory_space=pl.ANY)

    def small(rows):
        return pl.BlockSpec((rows, channels), lambda t: (0, 0))

    return pl.pallas_call(
        functools.partial(convs_kernel, edge),
        grid=(3,),
        out_shape=(
            jax.ShapeDtypeStruct((2, edge, cells, channels), f32),
            jax.ShapeDtypeStruct((8, channels), f32),
            jax.ShapeDtypeStruct(features.shape, bf16),
        ),
        in_specs=[
            SMEM,
            SMEM,
            pl.BlockSpec(block, lambda t: (t % 2, 0, 0, 0)),
            pl.BlockSpec(block, lambda t: (jnp.minimum(t, 1), 0, 0, 0)),
            pl.BlockSpec((1,) + padded.shape[1:], lambda t: (jnp.minimum(t, 1), 0, 0, 0, 0)),
            pl.BlockSpec((1,) + shifted.shape[1:], lambda t: (jnp.minimum(t, 1), 0, 0, 0, 0, 0)),
            pl.BlockSpec(back_weight.shape, lambda t: (0, 0)),
            small(8),
            small(1),
            any_space,
            any_space,
            any_space,
        ],
        out_specs=(any_space, small(8), pl.BlockSpec(block, lambda t: (0, 0, 0, 0))),
        scratch_shapes=conv_scratch(edge, channels)
        + [
            pltpu.VMEM((2, edge, cells, channels), f32),
            pltpu.VMEM(block, bf16),
            pltpu.VMEM((edge, 1) + rim.shape[2:], bf16),
            pltpu.VMEM(forward_weight.shape, bf16),
        ]
        + forward_scratch(edge, channels)
        + [pltpu.SemaphoreType.DMA((5,))],
        compiler_params=params(60, ("arbitrary",)),
        cost_estimate=cost(30 * 10**9, 16 * MIB),
        name="convs",
    )(occupancy, live, features, cotangent, padded, shifted, back_weight, coef, bias, hidden, rim, forward_weight)


def forward_kernel(edge, slot, occ_ref, live_ref, f_ref, hid_ref, rim_ref, w_ref, coef_ref, bias_ref, base_ref,
                   out_ref, side_s, found_s, *scratch):
    @pl.when(live_ref[slot] == 0)
    def _():
        out_ref[...] = f_ref[...]

    @pl.when(live_ref[slot] != 0)
    def _():
        forward_block(edge, slot, occ_ref, f_ref, hid_ref, rim_ref, w_ref, coefficients(coef_ref), bias_ref,
                      out_ref, *scratch, side_s, found_s)


def forward_conv(slot, occupancy, live, features, hidden, rim, weight, coef, bias, base):
    edge, channels = features.shape[1], features.shape[-1]
    whole = pl.BlockSpec((1, edge, edge * edge, channels), lambda s: (slot, 0, 0, 0))
    return pl.pallas_call(
        functools.partial(forward_kernel, edge, slot),
        grid=(1,),
        out_shape=jax.ShapeDtypeStruct(features.shape, bf16),
        in_specs=[
            SMEM,
            SMEM,
            whole,
            whole,
            pl.BlockSpec((edge, 1) + rim.shape[2:], lambda s: (0, slot, 0, 0, 0)),
            pl.BlockSpec(weight.shape, lambda s: (0, 0)),
            pl.BlockSpec((8, channels), lambda s: (0, 0)),
            pl.BlockSpec((1, channels), lambda s: (0, 0)),
            pl.BlockSpec(memory_space=pl.ANY),
        ],
        out_specs=whole,
        scratch_shapes=conv_scratch(edge, channels) + forward_scratch(edge, channels),
        input_output_aliases={8: 0},
        compiler_params=params(60, ("arbitrary",)),
        cost_estimate=cost(10 * 10**9, 4 * MIB),
        name="forward_conv",
    )(occupancy, live, features, hidden, rim, weight, coef, bias, base)


def wide_round(values, step):
    count = lax.axis_size("wide")
    terms = [values]
    for turn in range(1, 4):
        route = [(i, i ^ (turn * step)) for i in range(count)]
        terms.append(lax.ppermute(values, "wide", route))
    return (terms[0] + terms[1]) + (terms[2] + terms[3])


def group_sums(rows, channels):
    width = channels // G
    which = jnp.arange(channels) // width
    same = (which[:, None] == which[None, :]).astype(f32)
    return jnp.dot(rows, same, precision=lax.Precision.HIGHEST)


def last_kernel(edge, rows, occ_ref, coef_ref, parts_hbm, f_hbm, hat_hbm, step_hbm, out_hbm,
                parts_s, f_s, hat_s, step_s, out_s, sems):
    channels = parts_s.shape[-1]
    few = edge // 2
    blocks = [(slot, pl.ds(half * few, few)) for slot in range(2) for half in range(2)]
    fetch = pltpu.make_async_copy(parts_hbm, parts_s, sems.at[0])
    fetches = [
        (
            pltpu.make_async_copy(f_hbm.at[block], f_s.at[block], sems.at[2 + 2 * i]),
            pltpu.make_async_copy(hat_hbm.at[block], hat_s.at[block], sems.at[3 + 2 * i]),
        )
        for i, block in enumerate(blocks)
    ]
    stores = [
        pltpu.make_async_copy(out_s.at[block], out_hbm.at[block], sems.at[10 + i]) for i, block in enumerate(blocks)
    ]
    store = pltpu.make_async_copy(step_s, step_hbm, sems.at[1])
    fetch.start()
    for pair in fetches:
        pair[0].start()
        pair[1].start()
    fetch.wait()
    tail = jnp.zeros((parts_s.shape[1] - rows, channels), f32)
    total = jnp.zeros((1, channels), f32)
    for part in range(parts_s.shape[0]):
        values = parts_s[part, 0:rows].astype(f32)
        total = total + jnp.sum(values * values, axis=0, keepdims=True)
        tail = tail + parts_s[part, rows:].astype(f32)
    mean = jnp.sum(total, axis=1, keepdims=True) / step_s.size
    factor = lax.rsqrt(mean + step_eps)
    for part in range(parts_s.shape[0]):
        step_s[part] = parts_s[part, 0:rows].astype(f32) * factor
    store.start()
    first = tail[0:1] + tail[1:2] + tail[2:3]
    second = tail[3:4] + tail[4:5] + tail[5:6]
    both = jnp.concatenate([first, second] + [jnp.zeros_like(first)] * 6, axis=0)
    row = lax.broadcasted_iota(jnp.int32, (channels, channels), 0) // (channels // G)
    column = lax.broadcasted_iota(jnp.int32, (channels, channels), 1) // (channels // G)
    same = (row == column).astype(f32)
    grouped = jnp.dot(both, same, precision=lax.Precision.HIGHEST, preferred_element_type=f32)
    mean, rstd = coef_ref[0:1, :], coef_ref[1:2, :]
    first = grouped[0:1] / coef_ref[4:5, :]
    second = grouped[1:2] / coef_ref[4:5, :]
    for i, (slot, _) in enumerate(blocks):
        fetches[i][0].wait()
        fetches[i][1].wait()

        def plane(z, carry):
            mask = plane_mask(occ_ref, slot, z, edge, channels)
            normed = (f_s[slot, z].astype(f32) - mean) * rstd
            change = jnp.where(mask, rstd * (first + normed * second), 0.0)
            out_s[slot, z] = (hat_s[slot, z] - change).astype(bf16)
            return carry

        lax.fori_loop(few * (i % 2), few * (i % 2) + few, plane, 0)
        stores[i].start()
    store.wait()
    for each in stores:
        each.wait()


def last_step(occupancy, coef, parts, features, hat, rows):
    wide, _, channels = parts.shape
    any_space = pl.BlockSpec(memory_space=pl.ANY)
    return pl.pallas_call(
        functools.partial(last_kernel, features.shape[1], rows),
        out_shape=(
            jax.ShapeDtypeStruct((wide, rows, channels), f32),
            jax.ShapeDtypeStruct(features.shape, bf16),
        ),
        in_specs=[SMEM, VMEM, any_space, any_space, any_space],
        out_specs=(any_space, any_space),
        scratch_shapes=[
            pltpu.VMEM(parts.shape, bf16),
            pltpu.VMEM(features.shape, bf16),
            pltpu.VMEM(features.shape, f32),
            pltpu.VMEM((wide, rows, channels), f32),
            pltpu.VMEM(features.shape, bf16),
            pltpu.SemaphoreType.DMA((14,)),
        ],
        compiler_params=params(60),
        cost_estimate=cost(0, 12 * MIB),
        name="last_step",
    )(occupancy, coef, parts, features, hat)


def reduce_weights(grads, sums, tie):
    shape = grads.shape
    channels = shape[2]
    wide, narrow = lax.axis_size("wide"), lax.axis_size("narrow")
    rows = shape[0] * shape[1] // wide
    mine = jnp.sum(exchange(grads.reshape(wide, rows, channels), "wide"), axis=0)
    deep = -(-rows // (8 * narrow)) * 8
    mine = jnp.pad(mine, ((0, deep * narrow - rows), (0, 0))).reshape(narrow, deep, channels)
    sums = jnp.broadcast_to(sums[None], (narrow,) + sums.shape)
    mine, tie = lax.optimization_barrier((mine, tie))
    mine = jnp.sum(exchange(jnp.concatenate([mine, sums], axis=1), "narrow"), axis=0)
    mine, sums = mine[:deep], mine[deep : deep + 2]
    mine = exchange(jnp.broadcast_to(mine.astype(bf16)[None], (narrow, deep, channels)), "narrow")
    high = lax.reduce_precision(sums, 8, 7)
    middle = lax.reduce_precision(sums - high, 8, 7)
    low = (sums - high) - middle
    tail = jnp.stack([high, middle, low], axis=1).reshape(6, channels).astype(bf16)
    mine = mine.reshape(narrow * deep, channels)[:rows]
    mine, tie = lax.optimization_barrier((mine, tie))
    mine = jnp.concatenate([mine, tail, jnp.zeros((2, channels), bf16)], axis=0)
    parts = exchange(jnp.broadcast_to(mine[None], (wide,) + mine.shape), "wide")
    return (parts, rows, tie)


def local(
    features,
    out_cotangent,
    occupancy,
    live_slots,
    neighbours,
    timestep,
    norm_gain,
    norm_bias,
    film_weight,
    conv_weight,
    conv_bias,
):
    channels = features.shape[-1]
    group_width = channels // G
    hub = lax.axis_index("narrow").astype(jnp.int32)
    place = jnp.stack([hub, lax.axis_index("wide").astype(jnp.int32)])
    mine = 2 * hub + jnp.arange(2, dtype=jnp.int32)
    live = jnp.any(live_slots[0][None, :] == mine[:, None], axis=1).astype(jnp.int32)

    taps = conv_weight.reshape(9, 3, channels, channels)
    forward_weight = taps.transpose(0, 2, 1, 3).reshape(9 * channels, 3 * channels)
    flipped = conv_weight[::-1].reshape(9, 3, channels, channels)
    back_weight = flipped.transpose(0, 3, 1, 2).reshape(9 * channels, 3 * channels)
    film_scale, film_shift = film_terms(timestep, film_weight)
    scale = norm_gain * (1.0 + film_scale)
    shift = norm_bias * (1.0 + film_scale) + film_shift

    up_got = exchange(surface(occupancy, out_cotangent, 0.0, False), "narrow")
    feat_message = surface(occupancy, features, float("inf"), True)
    feat_message, up_got, forward_weight, back_weight, scale, shift = lax.optimization_barrier(
        (feat_message, up_got, forward_weight, back_weight, scale, shift)
    )
    feat_got = exchange(feat_message, "narrow")
    up_rows, _ = hub_stage(place, live_slots, neighbours, up_got, 0.0)
    up_rows, feat_got = lax.optimization_barrier((up_rows, feat_got))
    up_rim = exchange(up_rows, "narrow")
    feat_rows, stats = hub_stage(place, live_slots, neighbours, feat_got, float("inf"), True)
    feat_rows, up_rim = lax.optimization_barrier((feat_rows, up_rim))
    feat_rim = exchange(feat_rows, "narrow")

    voxel_count = stats[2, 0] * group_width
    sums = group_sums(stats[:2], channels)
    mean = sums[0] / voxel_count
    rstd = lax.rsqrt(sums[1] / voxel_count - mean * mean + norm_eps)
    blank = jnp.zeros((channels,), f32)
    coef = jnp.stack([mean, rstd, scale, shift, blank + voxel_count, blank, blank, blank])

    grads, padded, shifted, hidden = weight_grad(occupancy, live, features, out_cotangent, up_rim, coef)
    grads, feat_rim = lax.optimization_barrier((grads, feat_rim))
    bias = conv_bias[None, :]
    hat, grad_sums, mixed = convs(
        occupancy, live, features, out_cotangent, padded, shifted, back_weight, coef, bias, hidden, feat_rim,
        forward_weight,
    )
    parts, rows, mixed = reduce_weights(grads, grad_sums, mixed)
    mixed = forward_conv(1, occupancy, live, features, hidden, feat_rim, forward_weight, coef, bias, mixed)
    weight_step, feature_grad = last_step(occupancy, coef, parts, features, hat, rows)
    return (mixed, feature_grad, weight_step.reshape(conv_weight.shape))


def solution(mesh):
    return jax.shard_map(
        local,
        mesh=mesh,
        in_specs=(
            P(("wide", "narrow"), None, None, None),
            P(("wide", "narrow"), None, None, None),
            P(("wide", "narrow"), None, None),
            P("wide", None),
            P("wide", None),
            P(),
            P(),
            P(),
            P(),
            P(),
            P(),
        ),
        out_specs=(
            P(("wide", "narrow"), None, None, None),
            P(("wide", "narrow"), None, None, None),
            P(),
        ),
        check_vma=False,
    )
```

```python
import functools

import jax
import jax.numpy as jnp
from jax import lax
from jax.experimental import pallas as pl
from jax.experimental.pallas import tpu as pltpu
from jax.sharding import PartitionSpec as P

G = 32
norm_eps = 1e-05
step_eps = 1e-06
MIB = 1 << 20
f32 = jnp.float32
bf16 = jnp.bfloat16

SMEM = pl.BlockSpec(memory_space=pltpu.SMEM)
VMEM = pl.BlockSpec(memory_space=pltpu.VMEM)


def params(limit, semantics=None):
    return pltpu.CompilerParams(vmem_limit_bytes=limit * MIB, dimension_semantics=semantics)


def cost(flops, size):
    return pl.CostEstimate(flops=flops, bytes_accessed=size, transcendentals=0)


def film_terms(timestep, film_weight):
    half_width = film_weight.shape[0] // 2
    channels = film_weight.shape[1] // 2
    frequencies = jnp.exp(
        -jnp.log(10000.0) * jnp.arange(half_width).astype(jnp.float32) / half_width
    )
    angles = timestep.astype(jnp.float32)[0] * frequencies
    embedding = jax.nn.silu(jnp.concatenate([jnp.cos(angles), jnp.sin(angles)]))
    film_out = jnp.dot(embedding[None, :], film_weight, precision=lax.Precision.HIGHEST)[0]
    return (film_out[:channels], film_out[channels:])


def plane_mask(occ_ref, slot, z, edge, channels):
    bit = lax.broadcasted_iota(jnp.int32, (edge, channels), 0)
    rows = [
        jnp.bitwise_and(jnp.right_shift(jnp.full((edge, channels), occ_ref[slot, z, y], jnp.int32), bit), 1)
        for y in range(edge)
    ]
    return jnp.concatenate(rows, axis=0) != 0


def x_row(rows, edge, channels):
    return lax.rem(lax.broadcasted_iota(jnp.int32, (rows, channels), 0), edge)


def pieces(value, count):
    found = []
    for _ in range(count):
        part = value.astype(bf16).astype(f32)
        found.append(part)
        value = value - part
    return found


def surface_kernel(edge, with_stats, fill, occ_ref, v_ref, out_ref, plane_s, edge_s, stat_s):
    channels = v_ref.shape[-1]
    last = edge - 1
    slot = pl.program_id(0)

    @pl.when(slot == 0)
    def _():
        stat_s[...] = jnp.zeros_like(stat_s)
        edge_s[...] = jnp.zeros_like(edge_s)

    def coded(z):
        mask = plane_mask(occ_ref, slot, z, edge, channels)
        values = v_ref[0, z].astype(f32)
        return (mask, values, jnp.where(mask, values, fill))

    def plane(z, place, carry):
        mask, values, shown = coded(z)
        plane_s[place] = shown
        for side in range(2):
            row = side * last
            out_ref[z, 4 + 2 * slot + side] = shown[row * edge : (row + 1) * edge].astype(bf16)
            out_ref[z, 8 + 2 * slot + side] = plane_s[place, pl.ds(row, edge, stride=edge), :].astype(bf16)
        if not with_stats:
            return carry
        total, squares, count = carry
        masked = jnp.where(mask, values, 0.0)
        total = total + jnp.sum(masked, axis=0, keepdims=True)
        squares = squares + jnp.sum(masked * values, axis=0, keepdims=True)
        count = count + jnp.sum(mask.astype(f32), axis=0, keepdims=True)
        return (total, squares, count)

    def step(i, carry):
        for place in range(4):
            carry = plane(4 * i + place, place, carry)
        return carry

    zero = jnp.zeros((1, channels), f32)
    found = lax.fori_loop(0, edge // 4, step, (zero, zero, zero) if with_stats else 0)
    if with_stats:
        for index in range(3):
            stat_s[index : index + 1, :] = stat_s[index : index + 1, :] + found[index]
    for z_side in range(2):
        _, _, shown = coded(z_side * last)
        for hub in range(edge):
            out_ref[hub, 2 * slot + z_side] = shown[hub * edge : (hub + 1) * edge].astype(bf16)
        for y_side in range(2):
            for hub in range(edge):
                first = y_side * last * edge + hub
                for place in range(2):

                    @pl.when(slot == place)
                    def _():
                        row = 4 * place + 2 * z_side + y_side
                        edge_s[hub, row : row + 1, :] = shown[first : first + 1]

    @pl.when(slot == 1)
    def _():
        if with_stats:
            parts = pieces(stat_s[0:1, :], 3) + pieces(stat_s[1:2, :], 3) + pieces(stat_s[2:3, :], 2)
            for hub in range(edge):
                for row, part in enumerate(parts):
                    edge_s[hub, 8 + row : 9 + row, :] = part
        for hub in range(edge):
            for tile in range(16 // edge):
                out_ref[hub, 12 + tile] = edge_s[hub, tile * edge : (tile + 1) * edge].astype(bf16)


def surface(occupancy, values, fill, with_stats):
    edge, cells, channels = values.shape[1:]
    tiles = 12 + 16 // edge
    return pl.pallas_call(
        functools.partial(surface_kernel, edge, with_stats, fill),
        grid=(2,),
        out_shape=jax.ShapeDtypeStruct((edge, tiles, edge, channels), bf16),
        in_specs=[SMEM, pl.BlockSpec((1, edge, cells, channels), lambda s: (s, 0, 0, 0))],
        out_specs=pl.BlockSpec((edge, tiles, edge, channels), lambda s: (0, 0, 0, 0)),
        scratch_shapes=[
            pltpu.VMEM((4, cells, channels), f32),
            pltpu.VMEM((edge, 16, channels), f32),
            pltpu.VMEM((8, channels), f32),
        ],
        compiler_params=params(60, ("arbitrary",)),
        cost_estimate=cost(0, 3 * MIB),
        name="surface",
    )(occupancy, values)


def trade_kernel(edge, live_ref, got_ref, left_ref, right_ref, stat_ref, ends_s):
    live_count = live_ref.shape[1]
    for k in range(live_count):
        slot = live_ref[0, k]
        owner, local = slot // 2, lax.rem(slot, 2)
        for side, out in ((0, left_ref), (1, right_ref)):
            out[k] = got_ref[owner, 8 + 2 * local + side]
            for z_side in range(2):
                tile = got_ref[owner, 2 * local + z_side].astype(f32)
                row = 2 * k + z_side
                x = side * (edge - 1)
                ends_s[side, row : row + 1, :] = tile[x : x + 1]
    for side, out in ((0, left_ref), (1, right_ref)):
        for tile in range(2 * live_count // edge):
            out[live_count + tile] = ends_s[side, tile * edge : (tile + 1) * edge].astype(bf16)
    rows = []
    for tile in range(8 // edge if edge < 16 else 0, 16 // edge):
        total = got_ref[0, 12 + tile].astype(f32)
        for source in range(1, edge):
            total = total + got_ref[source, 12 + tile].astype(f32)
        rows.append(total)
    rows = jnp.concatenate(rows, axis=0)
    if edge == 16:
        rows = rows[8:]
    stat_ref[...] = jnp.zeros_like(stat_ref)
    stat_ref[0:1, :] = rows[0:1] + rows[1:2] + rows[2:3]
    stat_ref[1:2, :] = rows[3:4] + rows[4:5] + rows[5:6]
    stat_ref[2:3, :] = rows[6:7] + rows[7:8]


def trade(live_slots, got):
    edge, channels = got.shape[2], got.shape[-1]
    live_count = live_slots.shape[1]
    tiles = live_count + 2 * live_count // edge
    payload = jax.ShapeDtypeStruct((tiles, edge, channels), bf16)
    return pl.pallas_call(
        functools.partial(trade_kernel, edge),
        out_shape=(payload, payload, jax.ShapeDtypeStruct((8, channels), f32)),
        in_specs=[SMEM, VMEM],
        out_specs=(VMEM, VMEM, VMEM),
        scratch_shapes=[pltpu.VMEM((2, 2 * live_count, channels), f32)],
        compiler_params=params(16),
        cost_estimate=cost(0, 2 * MIB),
        name="trade",
    )(live_slots, got)


def hub_kernel(edge, fill, place_ref, live_ref, near_ref, got_ref, lower_ref, upper_ref, out_ref, wide_s, rows_s):
    live_count = live_ref.shape[1]
    last = edge - 1
    hub, group = place_ref[0], place_ref[1]
    x_refs = (lower_ref, upper_ref)
    for side in range(2):
        wide_s[side] = x_refs[side][...].astype(f32)

    def entry(k, dz, dy, dx):
        number = near_ref[k, 9 * (dz + 1) + 3 * (dy + 1) + (dx + 1)]
        index = jnp.clip(number - (group + dx) * live_count, 0, live_count - 1)
        return (number >= 0, index)

    def own(k, dz, dy):
        there, index = entry(k, dz, dy, 0)
        slot = live_ref[0, index]
        return (there, slot // 2, lax.rem(slot, 2))

    def step(k, carry):
        slot = live_ref[0, k]
        owner, local = slot // 2, lax.rem(slot, 2)

        def put(tile, there, values):
            out_ref[owner, local, tile] = jnp.where(there, values, fill).astype(bf16)

        def put_row(row, there, values):
            rows_s[row : row + 1, :] = jnp.where(there, values, fill)

        for side in range(2):
            step_to = 2 * side - 1
            there, source, place = own(k, step_to, 0)
            put(side, there, got_ref[source, 2 * place + 1 - side].astype(f32))
            there, source, place = own(k, 0, step_to)
            put(2 + side, there, got_ref[source, 4 + 2 * place + 1 - side].astype(f32))
            there, index = entry(k, 0, 0, step_to)
            put(4 + side, there, wide_s[side, index])
        dz_corner = jnp.where(hub == last, -1, 1)
        for a in range(2):
            for b in range(2):
                there, source, place = own(k, 2 * a - 1, 2 * b - 1)
                row = 4 * place + 2 * (1 - a) + (1 - b)
                tile = got_ref[source, 12 + row // edge].astype(f32)
                picked = lax.broadcasted_iota(jnp.int32, tile.shape, 0) == lax.rem(row, edge)
                put_row(2 * a + b, there, jnp.sum(jnp.where(picked, tile, 0.0), axis=0, keepdims=True))
                there, index = entry(k, 2 * a - 1, 0, 2 * b - 1)
                row = 2 * index + (1 - a)
                tile = wide_s[b, live_count + row // edge]
                picked = lax.broadcasted_iota(jnp.int32, tile.shape, 0) == lax.rem(row, edge)
                put_row(4 + 2 * a + b, there, jnp.sum(jnp.where(picked, tile, 0.0), axis=0, keepdims=True))
                row = last if a == 0 else 0
                there, index = entry(k, 0, 2 * a - 1, 2 * b - 1)
                put_row(8 + 2 * a + b, there, wide_s[b, index, row : row + 1, :])
                there, index = entry(k, dz_corner, 2 * a - 1, 2 * b - 1)
                put_row(12 + 2 * a + b, there, wide_s[b, index, row : row + 1, :])
        for tile in range(16 // edge):
            out_ref[owner, local, 6 + tile] = rows_s[tile * edge : (tile + 1) * edge].astype(bf16)
        return carry

    lax.fori_loop(0, live_count, step, 0)


def hub_rows(place, live_slots, neighbours, got, lower, upper, fill):
    edge, channels = got.shape[2], got.shape[-1]
    return pl.pallas_call(
        functools.partial(hub_kernel, edge, fill),
        out_shape=jax.ShapeDtypeStruct((edge, 2, 6 + 16 // edge, edge, channels), bf16),
        in_specs=[SMEM, SMEM, SMEM, VMEM, VMEM, VMEM],
        out_specs=VMEM,
        scratch_shapes=[
            pltpu.VMEM((2,) + lower.shape, f32),
            pltpu.VMEM((16, channels), f32),
        ],
        compiler_params=params(16),
        cost_estimate=cost(0, 8 * MIB),
        name="hub_rows",
    )(place, live_slots, neighbours, got, lower, upper)


def exchange(values, axis):
    return lax.all_to_all(values, axis, split_axis=0, concat_axis=0, tiled=True)


def hub_stage(place, live_slots, neighbours, got, fill, with_stats=False):
    to_left, to_right, stats = trade(live_slots, got)
    count = lax.axis_size("wide")
    lower = lax.ppermute(to_right, "wide", [(i, i + 1) for i in range(count - 1)])
    upper = lax.ppermute(to_left, "wide", [(i + 1, i) for i in range(count - 1)])
    if with_stats:
        stats, lower, upper = lax.optimization_barrier((wide_round(stats, 1), lower, upper))
        stats = wide_round(stats, 4)
    return (hub_rows(place, live_slots, neighbours, got, lower, upper, fill), stats)


def coefficients(coef_ref):
    return [coef_ref[i : i + 1, :] for i in range(5)]


def set_halo(edge, rim_ref, pad_ref, pad_lead, shift_ref, shift_lead, xh_s, edge_s, change):
    last = edge - 1
    for hub in range(edge):
        tiles = [change(rim_ref[hub, 0, tile].astype(f32)) for tile in range(6 + 16 // edge)]
        for side in range(2):
            pad_ref[pad_lead + (side * (edge + 1), hub + 1)] = tiles[side].astype(bf16)
            pad_ref[pad_lead + (hub + 1, side * (edge + 1))] = tiles[2 + side].astype(bf16)
            xh_s[side, hub + 1, 8 : 8 + edge, :] = tiles[4 + side]

        def row(index):
            tile = tiles[6 + index // edge]
            return tile[index % edge : index % edge + 1]

        for a in range(2):
            for b in range(2):
                edge_s[2 * a + b, hub : hub + 1, :] = row(2 * a + b)
                xh_s[b, a * (edge + 1), 8 + hub : 9 + hub, :] = row(4 + 2 * a + b)
                y = 8 + edge if a else 7
                xh_s[b, hub + 1, y : y + 1, :] = row(8 + 2 * a + b)
                if hub == last:
                    xh_s[b, 0, y : y + 1, :] = row(12 + 2 * a + b)
                if hub == 0:
                    xh_s[b, edge + 1, y : y + 1, :] = row(12 + 2 * a + b)
    for a in range(2):
        for b in range(2):
            pad_ref[pad_lead + (a * (edge + 1), b * (edge + 1))] = edge_s[2 * a + b].astype(bf16)
    for side in range(2):
        for z in range(edge + 2):
            for y in range(3):
                shift_ref[shift_lead + (side, y, z)] = xh_s[side, z, 7 + y : 7 + y + edge, :].astype(bf16)


def hidden_plane(feats, mask, coef):
    mean, rstd, scale, shift = coef[:4]
    pre = (feats - mean) * rstd * scale + shift
    return jnp.where(mask, pre * jax.nn.sigmoid(pre), 0.0)


def weight_kernel(edge, occ_ref, live_ref, f_ref, g_ref, rim_ref, coef_ref, grad_ref, pad_ref, shift_ref,
                  hid_ref, acc_s, even_s, odd_s, xh_s, edge_s, plane_s, face_s):
    channels = f_ref.shape[-1]
    cells = edge * edge
    slot = pl.program_id(0)
    coef = coefficients(coef_ref)
    depth = min(4, edge // 2)
    chunks = edge // depth

    @pl.when(slot == 0)
    def _():
        acc_s[...] = jnp.zeros_like(acc_s)

    @pl.when(live_ref[slot] != 0)
    def _():
        set_halo(edge, rim_ref, pad_ref, (0,), shift_ref, (0,), xh_s, edge_s, lambda v: v)
        lane_x = lax.rem(lax.broadcasted_iota(jnp.int32, (channels, cells), 1), edge)

        def fill(z, carry):
            mask = plane_mask(occ_ref, slot, z, edge, channels)
            ups = jnp.where(mask, g_ref[0, z].astype(f32), 0.0).astype(bf16)
            pad_ref[0, z + 1, 1 : edge + 1] = ups.reshape(edge, edge, channels)
            return carry

        lax.fori_loop(0, edge, fill, 0)

        def prepare(chunk, flip_s, part):
            if part < depth:
                z = chunk * depth + part
                mask = plane_mask(occ_ref, slot, z, edge, channels)
                hidden = hidden_plane(f_ref[0, z].astype(f32), mask, coef).astype(bf16)
                hid_ref[0, z] = hidden
                hidden = hidden.astype(f32)
                plane_s[part] = hidden
                for side in range(2):
                    face_s[side, pl.ds(z * edge, edge), :] = plane_s[
                        part, pl.ds(side * (edge - 1), edge, stride=edge), :
                    ]
                flat = hidden.T
                before = jnp.where(lane_x == edge - 1, 0.0, pltpu.roll(flat, cells - 1, 1))
                after = jnp.where(lane_x == 0, 0.0, pltpu.roll(flat, 1, 1))
                columns = slice(part * cells, (part + 1) * cells)
                flip_s[0:channels, columns] = before.astype(bf16)
                flip_s[channels : 2 * channels, columns] = flat.astype(bf16)
                flip_s[2 * channels : 3 * channels, columns] = after.astype(bf16)

        def add(tap, px, values):
            pz, py = tap // 3, tap % 3
            offset = 9 * (2 - pz) + 3 * (2 - py) + (2 - px)
            acc_s[offset] = acc_s[offset] + values

        pairs = [(0, 1), (2, 3), (4, 5), (6, 7), (8,)]

        def multiply(chunk, flip_s, beside):
            z0 = chunk * depth
            left = flip_s[...]
            for turn, pair in enumerate(pairs):
                right = [
                    pad_ref[0, pl.ds(z0 + tap // 3, depth), tap % 3 : tap % 3 + edge].reshape(
                        depth * cells, channels
                    )
                    for tap in pair
                ]
                right = right[0] if len(right) == 1 else jnp.concatenate(right, axis=1)
                found = jnp.dot(left, right, preferred_element_type=f32)
                for place, tap in enumerate(pair):
                    for px in range(3):
                        add(
                            tap,
                            px,
                            found[
                                px * channels : (px + 1) * channels,
                                place * channels : (place + 1) * channels,
                            ],
                        )
                beside(turn)

        def two(i, carry):
            multiply(2 * i, even_s, functools.partial(prepare, 2 * i + 1, odd_s))
            multiply(2 * i + 1, odd_s, functools.partial(prepare, 2 * i + 2, even_s))
            return carry

        for part in range(depth):
            prepare(0, even_s, part)
        lax.fori_loop(0, chunks // 2 - 1, two, 0)
        multiply(chunks - 2, even_s, functools.partial(prepare, chunks - 1, odd_s))
        multiply(chunks - 1, odd_s, lambda turn: None)
        for side in range(2):
            left = face_s[side].T.astype(bf16)
            for tap in range(9):
                right = shift_ref[0, side, tap % 3, tap // 3 : tap // 3 + edge].reshape(cells, channels)
                add(tap, 2 * side, jnp.dot(left, right, preferred_element_type=f32))

    @pl.when(slot == 1)
    def _():
        grad_ref[...] = acc_s[...]


def weight_grad(occupancy, live, features, cotangent, rim, coef):
    edge, channels = features.shape[1], features.shape[-1]
    cells = edge * edge
    wide = edge + 2
    whole = pl.BlockSpec((1, edge, cells, channels), lambda s: (s, 0, 0, 0))
    return pl.pallas_call(
        functools.partial(weight_kernel, edge),
        grid=(2,),
        out_shape=(
            jax.ShapeDtypeStruct((27, channels, channels), f32),
            jax.ShapeDtypeStruct((2, wide, wide, edge, channels), bf16),
            jax.ShapeDtypeStruct((2, 2, 3, wide, edge, channels), bf16),
            jax.ShapeDtypeStruct(features.shape, bf16),
        ),
        in_specs=[
            SMEM,
            SMEM,
            whole,
            whole,
            pl.BlockSpec((edge, 1) + rim.shape[2:], lambda s: (0, s, 0, 0, 0)),
            pl.BlockSpec((8, channels), lambda s: (0, 0)),
        ],
        out_specs=(
            pl.BlockSpec((27, channels, channels), lambda s: (0, 0, 0)),
            pl.BlockSpec((1, wide, wide, edge, channels), lambda s: (s, 0, 0, 0, 0)),
            pl.BlockSpec((1, 2, 3, wide, edge, channels), lambda s: (s, 0, 0, 0, 0, 0)),
            whole,
        ),
        scratch_shapes=[
            pltpu.VMEM((27, channels, channels), f32),
            pltpu.VMEM((3 * channels, min(4, edge // 2) * cells), bf16),
            pltpu.VMEM((3 * channels, min(4, edge // 2) * cells), bf16),
            pltpu.VMEM((2, wide, 8 * ((edge + 16) // 8), channels), f32),
            pltpu.VMEM((4, edge, channels), f32),
            pltpu.VMEM((min(4, edge // 2), cells, channels), f32),
            pltpu.VMEM((2, cells, channels), f32),
        ],
        compiler_params=params(60, ("arbitrary",)),
        cost_estimate=cost(10**8, MIB),
        name="weight_grad",
    )(occupancy, live, features, cotangent, rim, coef)


def side_rows(edge, shift_ref, shift_lead, w_ref, side_s):
    cells = edge * edge
    channels = w_ref.shape[0] // 9
    for side in range(2):
        rows = jnp.concatenate(
            [
                shift_ref[shift_lead + (side, tap % 3, slice(tap // 3, tap // 3 + edge))].reshape(cells, channels)
                for tap in range(9)
            ],
            axis=1,
        )
        first = 2 * side * channels
        side_s[side] = jnp.dot(rows, w_ref[:, first : first + channels], preferred_element_type=f32)


DEPTH = 4


def conv_pipeline(edge, pad_ref, pad_lead, w_ref, side_s, found_s, finish_plane, carry):
    cells = edge * edge
    rows = DEPTH * cells
    channels = w_ref.shape[0] // 9
    groups = edge // DEPTH
    x_at = x_row(cells, edge, channels)
    spans = [slice(0, 2 * channels), slice(2 * channels, 3 * channels)]

    def multiply(group, buffer, span):
        z = group * DEPTH
        lines = jnp.concatenate(
            [
                pad_ref[pad_lead + (pl.ds(z + tap // 3, DEPTH), slice(tap % 3, tap % 3 + edge))].reshape(
                    rows, channels
                )
                for tap in range(9)
            ],
            axis=1,
        )
        found_s[buffer, :, span] = jnp.dot(lines, w_ref[:, span], preferred_element_type=f32)

    def combine(group, buffer, part, carry):
        z = group * DEPTH + part
        found = found_s[buffer, part * cells : (part + 1) * cells]

        def beside(side):
            line = side_s[side, pl.ds(pl.multiple_of(z * edge, edge), edge), :]
            return jnp.broadcast_to(line[:, None, :], (edge, edge, channels)).reshape(cells, channels)

        before = jnp.where(x_at == 0, beside(0), pltpu.roll(found[:, :channels], 1, 0))
        after = jnp.where(x_at == edge - 1, beside(1), pltpu.roll(found[:, 2 * channels :], cells - 1, 0))
        return finish_plane(z, found[:, channels : 2 * channels] + before + after, carry)

    def advance(group, buffer, carry):
        for part in range(DEPTH):
            if part % (DEPTH // 2) == 0:
                multiply(group + 1, 1 - buffer, spans[2 * part // DEPTH])
            carry = combine(group, buffer, part, carry)
        return carry

    def step(i, carry):
        return advance(2 * i + 1, 1, advance(2 * i, 0, carry))

    for span in spans:
        multiply(0, 0, span)
    carry = lax.fori_loop(0, groups // 2 - 1, step, carry)
    carry = advance(groups - 2, 0, carry)
    for part in range(DEPTH):
        carry = combine(groups - 1, 1, part, carry)
    return carry


def forward_block(edge, slot, occ_ref, f_ref, hid_ref, rim_ref, w_ref, coef, bias_ref, out_ref,
                  pad_s, shift_s, xh_s, edge_s, side_s, found_s):
    channels = f_ref.shape[-1]

    def activate(coded):
        return hidden_plane(coded, coded < jnp.inf, coef)

    set_halo(edge, rim_ref, pad_s, (), shift_s, (), xh_s, edge_s, activate)
    for z in range(edge):
        pad_s[z + 1, 1 : edge + 1] = hid_ref[0, z].reshape(edge, edge, channels)
    side_rows(edge, shift_s, (), w_ref, side_s)

    def plane(z, conv, carry):
        mask = plane_mask(occ_ref, slot, z, edge, channels)
        feats = f_ref[0, z].astype(f32)
        out_ref[0, z] = (feats + jnp.where(mask, conv + bias_ref[...], 0.0)).astype(bf16)
        return carry

    conv_pipeline(edge, pad_s, (), w_ref, side_s, found_s, plane, 0)


def convs_kernel(edge, occ_ref, live_ref, f_ref, g_ref, pad_ref, shift_ref, back_ref, coef_ref, bias_ref,
                 hid_hbm, rim_hbm, forward_hbm, hat_hbm, sum_ref, out_ref,
                 side_s, found_s, hat_s, hid_s, rim_s, forward_s, pad_s, shift_s, xh_s, edge_s, sems):
    channels = f_ref.shape[-1]
    turn = pl.program_id(0)
    coef = coefficients(coef_ref)
    mean, rstd, scale, shift = coef[:4]
    fetches = [
        pltpu.make_async_copy(hid_hbm.at[pl.ds(0, 1)], hid_s, sems.at[0]),
        pltpu.make_async_copy(rim_hbm.at[:, pl.ds(0, 1)], rim_s, sems.at[1]),
        pltpu.make_async_copy(forward_hbm, forward_s, sems.at[2]),
    ]
    stores = [pltpu.make_async_copy(hat_s.at[slot], hat_hbm.at[slot], sems.at[3 + slot]) for slot in range(2)]

    @pl.when(turn == 0)
    def _():
        for fetch in fetches:
            fetch.start()
        sum_ref[...] = jnp.zeros_like(sum_ref)

    @pl.when(jnp.logical_and(turn < 2, live_ref[jnp.minimum(turn, 1)] != 0))
    def _():
        side_rows(edge, shift_ref, (0,), back_ref, side_s)

        def plane(z, back, carry):
            first, second = carry
            mask = plane_mask(occ_ref, turn, z, edge, channels)
            normed = (f_ref[0, z].astype(f32) - mean) * rstd
            pre = normed * scale + shift
            gate = jax.nn.sigmoid(pre)
            hat = jnp.where(mask, back * (gate * (1.0 + pre * (1.0 - gate))) * scale, 0.0)
            hat_s[turn, z] = g_ref[0, z].astype(f32) + rstd * hat
            first = first + jnp.sum(hat, axis=0, keepdims=True)
            second = second + jnp.sum(hat * normed, axis=0, keepdims=True)
            return (first, second)

        zero = jnp.zeros((1, channels), f32)
        first, second = conv_pipeline(edge, pad_ref, (0,), back_ref, side_s, found_s, plane, (zero, zero))
        sum_ref[0:1, :] = sum_ref[0:1, :] + first
        sum_ref[1:2, :] = sum_ref[1:2, :] + second

    for slot in range(2):

        @pl.when(jnp.logical_and(turn == slot, live_ref[slot] == 0))
        def _():
            def plane(z, carry):
                hat_s[slot, z] = g_ref[0, z].astype(f32)
                return carry

            lax.fori_loop(0, edge, plane, 0)

        @pl.when(turn == slot)
        def _():
            stores[slot].start()

    @pl.when(turn == 2)
    def _():
        for fetch in fetches:
            fetch.wait()

        @pl.when(live_ref[0] == 0)
        def _():
            out_ref[...] = f_ref[...]

        @pl.when(live_ref[0] != 0)
        def _():
            forward_block(edge, 0, occ_ref, f_ref, hid_s, rim_s, forward_s, coef, bias_ref, out_ref,
                          pad_s, shift_s, xh_s, edge_s, side_s, found_s)

        for store in stores:
            store.wait()


def forward_scratch(edge, channels):
    wide, cells = edge + 2, edge * edge
    return [
        pltpu.VMEM((wide, wide, edge, channels), bf16),
        pltpu.VMEM((2, 3, wide, edge, channels), bf16),
        pltpu.VMEM((2, wide, 8 * ((edge + 16) // 8), channels), f32),
        pltpu.VMEM((4, edge, channels), f32),
    ]


def conv_scratch(edge, channels):
    cells = edge * edge
    return [
        pltpu.VMEM((2, cells, channels), f32),
        pltpu.VMEM((2, DEPTH * cells, 3 * channels), f32),
    ]


def convs(occupancy, live, features, cotangent, padded, shifted, back_weight, coef, bias, hidden, rim, forward_weight):
    edge, channels = features.shape[1], features.shape[-1]
    cells = edge * edge
    block = (1, edge, cells, channels)
    any_space = pl.BlockSpec(memory_space=pl.ANY)

    def small(rows):
        return pl.BlockSpec((rows, channels), lambda t: (0, 0))

    return pl.pallas_call(
        functools.partial(convs_kernel, edge),
        grid=(3,),
        out_shape=(
            jax.ShapeDtypeStruct((2, edge, cells, channels), f32),
            jax.ShapeDtypeStruct((8, channels), f32),
            jax.ShapeDtypeStruct(features.shape, bf16),
        ),
        in_specs=[
            SMEM,
            SMEM,
            pl.BlockSpec(block, lambda t: (t % 2, 0, 0, 0)),
            pl.BlockSpec(block, lambda t: (jnp.minimum(t, 1), 0, 0, 0)),
            pl.BlockSpec((1,) + padded.shape[1:], lambda t: (jnp.minimum(t, 1), 0, 0, 0, 0)),
            pl.BlockSpec((1,) + shifted.shape[1:], lambda t: (jnp.minimum(t, 1), 0, 0, 0, 0, 0)),
            pl.BlockSpec(back_weight.shape, lambda t: (0, 0)),
            small(8),
            small(1),
            any_space,
            any_space,
            any_space,
        ],
        out_specs=(any_space, small(8), pl.BlockSpec(block, lambda t: (0, 0, 0, 0))),
        scratch_shapes=conv_scratch(edge, channels)
        + [
            pltpu.VMEM((2, edge, cells, channels), f32),
            pltpu.VMEM(block, bf16),
            pltpu.VMEM((edge, 1) + rim.shape[2:], bf16),
            pltpu.VMEM(forward_weight.shape, bf16),
        ]
        + forward_scratch(edge, channels)
        + [pltpu.SemaphoreType.DMA((5,))],
        compiler_params=params(60, ("arbitrary",)),
        cost_estimate=cost(30 * 10**9, 16 * MIB),
        name="convs",
    )(occupancy, live, features, cotangent, padded, shifted, back_weight, coef, bias, hidden, rim, forward_weight)


def forward_kernel(edge, slot, occ_ref, live_ref, f_ref, hid_ref, rim_ref, w_ref, coef_ref, bias_ref, base_ref,
                   out_ref, side_s, found_s, *scratch):
    @pl.when(live_ref[slot] == 0)
    def _():
        out_ref[...] = f_ref[...]

    @pl.when(live_ref[slot] != 0)
    def _():
        forward_block(edge, slot, occ_ref, f_ref, hid_ref, rim_ref, w_ref, coefficients(coef_ref), bias_ref,
                      out_ref, *scratch, side_s, found_s)


def forward_conv(slot, occupancy, live, features, hidden, rim, weight, coef, bias, base):
    edge, channels = features.shape[1], features.shape[-1]
    whole = pl.BlockSpec((1, edge, edge * edge, channels), lambda s: (slot, 0, 0, 0))
    return pl.pallas_call(
        functools.partial(forward_kernel, edge, slot),
        grid=(1,),
        out_shape=jax.ShapeDtypeStruct(features.shape, bf16),
        in_specs=[
            SMEM,
            SMEM,
            whole,
            whole,
            pl.BlockSpec((edge, 1) + rim.shape[2:], lambda s: (0, slot, 0, 0, 0)),
            pl.BlockSpec(weight.shape, lambda s: (0, 0)),
            pl.BlockSpec((8, channels), lambda s: (0, 0)),
            pl.BlockSpec((1, channels), lambda s: (0, 0)),
            pl.BlockSpec(memory_space=pl.ANY),
        ],
        out_specs=whole,
        scratch_shapes=conv_scratch(edge, channels) + forward_scratch(edge, channels),
        input_output_aliases={8: 0},
        compiler_params=params(60, ("arbitrary",)),
        cost_estimate=cost(10 * 10**9, 4 * MIB),
        name="forward_conv",
    )(occupancy, live, features, hidden, rim, weight, coef, bias, base)


def wide_round(values, step):
    count = lax.axis_size("wide")
    terms = [values]
    for turn in range(1, 4):
        route = [(i, i ^ (turn * step)) for i in range(count)]
        terms.append(lax.ppermute(values, "wide", route))
    return (terms[0] + terms[1]) + (terms[2] + terms[3])


def group_sums(rows, channels):
    width = channels // G
    which = jnp.arange(channels) // width
    same = (which[:, None] == which[None, :]).astype(f32)
    return jnp.dot(rows, same, precision=lax.Precision.HIGHEST)


def last_kernel(edge, rows, occ_ref, coef_ref, parts_hbm, f_hbm, hat_hbm, step_hbm, out_hbm,
                parts_s, f_s, hat_s, step_s, out_s, sems):
    channels = parts_s.shape[-1]
    few = edge // 2
    blocks = [(slot, pl.ds(half * few, few)) for slot in range(2) for half in range(2)]
    fetch = pltpu.make_async_copy(parts_hbm, parts_s, sems.at[0])
    fetches = [
        (
            pltpu.make_async_copy(f_hbm.at[block], f_s.at[block], sems.at[2 + 2 * i]),
            pltpu.make_async_copy(hat_hbm.at[block], hat_s.at[block], sems.at[3 + 2 * i]),
        )
        for i, block in enumerate(blocks)
    ]
    stores = [
        pltpu.make_async_copy(out_s.at[block], out_hbm.at[block], sems.at[10 + i]) for i, block in enumerate(blocks)
    ]
    store = pltpu.make_async_copy(step_s, step_hbm, sems.at[1])
    fetch.start()
    for pair in fetches:
        pair[0].start()
        pair[1].start()
    fetch.wait()
    tail = jnp.zeros((parts_s.shape[1] - rows, channels), f32)
    total = jnp.zeros((1, channels), f32)
    for part in range(parts_s.shape[0]):
        values = parts_s[part, 0:rows].astype(f32)
        total = total + jnp.sum(values * values, axis=0, keepdims=True)
        tail = tail + parts_s[part, rows:].astype(f32)
    mean = jnp.sum(total, axis=1, keepdims=True) / step_s.size
    factor = lax.rsqrt(mean + step_eps)
    for part in range(parts_s.shape[0]):
        step_s[part] = parts_s[part, 0:rows].astype(f32) * factor
    store.start()
    first = tail[0:1] + tail[1:2] + tail[2:3]
    second = tail[3:4] + tail[4:5] + tail[5:6]
    both = jnp.concatenate([first, second] + [jnp.zeros_like(first)] * 6, axis=0)
    row = lax.broadcasted_iota(jnp.int32, (channels, channels), 0) // (channels // G)
    column = lax.broadcasted_iota(jnp.int32, (channels, channels), 1) // (channels // G)
    same = (row == column).astype(f32)
    grouped = jnp.dot(both, same, precision=lax.Precision.HIGHEST, preferred_element_type=f32)
    mean, rstd = coef_ref[0:1, :], coef_ref[1:2, :]
    first = grouped[0:1] / coef_ref[4:5, :]
    second = grouped[1:2] / coef_ref[4:5, :]
    for i, (slot, _) in enumerate(blocks):
        fetches[i][0].wait()
        fetches[i][1].wait()

        def plane(z, carry):
            mask = plane_mask(occ_ref, slot, z, edge, channels)
            normed = (f_s[slot, z].astype(f32) - mean) * rstd
            change = jnp.where(mask, rstd * (first + normed * second), 0.0)
            out_s[slot, z] = (hat_s[slot, z] - change).astype(bf16)
            return carry

        lax.fori_loop(few * (i % 2), few * (i % 2) + few, plane, 0)
        stores[i].start()
    store.wait()
    for each in stores:
        each.wait()


def last_step(occupancy, coef, parts, features, hat, rows):
    wide, _, channels = parts.shape
    any_space = pl.BlockSpec(memory_space=pl.ANY)
    return pl.pallas_call(
        functools.partial(last_kernel, features.shape[1], rows),
        out_shape=(
            jax.ShapeDtypeStruct((wide, rows, channels), f32),
            jax.ShapeDtypeStruct(features.shape, bf16),
        ),
        in_specs=[SMEM, VMEM, any_space, any_space, any_space],
        out_specs=(any_space, any_space),
        scratch_shapes=[
            pltpu.VMEM(parts.shape, bf16),
            pltpu.VMEM(features.shape, bf16),
            pltpu.VMEM(features.shape, f32),
            pltpu.VMEM((wide, rows, channels), f32),
            pltpu.VMEM(features.shape, bf16),
            pltpu.SemaphoreType.DMA((14,)),
        ],
        compiler_params=params(60),
        cost_estimate=cost(0, 12 * MIB),
        name="last_step",
    )(occupancy, coef, parts, features, hat)


def reduce_weights(grads, sums, tie):
    shape = grads.shape
    channels = shape[2]
    wide, narrow = lax.axis_size("wide"), lax.axis_size("narrow")
    rows = shape[0] * shape[1] // wide
    mine = jnp.sum(exchange(grads.reshape(wide, rows, channels), "wide"), axis=0)
    deep = -(-rows // (8 * narrow)) * 8
    mine = jnp.pad(mine, ((0, deep * narrow - rows), (0, 0))).reshape(narrow, deep, channels)
    sums = jnp.broadcast_to(sums[None], (narrow,) + sums.shape)
    mine, tie = lax.optimization_barrier((mine, tie))
    mine = jnp.sum(exchange(jnp.concatenate([mine, sums], axis=1), "narrow"), axis=0)
    mine, sums = mine[:deep], mine[deep : deep + 2]
    mine = exchange(jnp.broadcast_to(mine.astype(bf16)[None], (narrow, deep, channels)), "narrow")
    high = lax.reduce_precision(sums, 8, 7)
    middle = lax.reduce_precision(sums - high, 8, 7)
    low = (sums - high) - middle
    tail = jnp.stack([high, middle, low], axis=1).reshape(6, channels).astype(bf16)
    mine = mine.reshape(narrow * deep, channels)[:rows]
    mine, tie = lax.optimization_barrier((mine, tie))
    mine = jnp.concatenate([mine, tail, jnp.zeros((2, channels), bf16)], axis=0)
    parts = exchange(jnp.broadcast_to(mine[None], (wide,) + mine.shape), "wide")
    return (parts, rows, tie)


def local(
    features,
    out_cotangent,
    occupancy,
    live_slots,
    neighbours,
    timestep,
    norm_gain,
    norm_bias,
    film_weight,
    conv_weight,
    conv_bias,
):
    channels = features.shape[-1]
    group_width = channels // G
    hub = lax.axis_index("narrow").astype(jnp.int32)
    place = jnp.stack([hub, lax.axis_index("wide").astype(jnp.int32)])
    mine = 2 * hub + jnp.arange(2, dtype=jnp.int32)
    live = jnp.any(live_slots[0][None, :] == mine[:, None], axis=1).astype(jnp.int32)

    taps = conv_weight.reshape(9, 3, channels, channels)
    forward_weight = taps.transpose(0, 2, 1, 3).reshape(9 * channels, 3 * channels)
    flipped = conv_weight[::-1].reshape(9, 3, channels, channels)
    back_weight = flipped.transpose(0, 3, 1, 2).reshape(9 * channels, 3 * channels)
    film_scale, film_shift = film_terms(timestep, film_weight)
    scale = norm_gain * (1.0 + film_scale)
    shift = norm_bias * (1.0 + film_scale) + film_shift

    up_got = exchange(surface(occupancy, out_cotangent, 0.0, False), "narrow")
    feat_message = surface(occupancy, features, float("inf"), True)
    feat_message, up_got, forward_weight, back_weight, scale, shift = lax.optimization_barrier(
        (feat_message, up_got, forward_weight, back_weight, scale, shift)
    )
    feat_got = exchange(feat_message, "narrow")
    up_rows, _ = hub_stage(place, live_slots, neighbours, up_got, 0.0)
    up_rows, feat_got = lax.optimization_barrier((up_rows, feat_got))
    up_rim = exchange(up_rows, "narrow")
    feat_rows, stats = hub_stage(place, live_slots, neighbours, feat_got, float("inf"), True)
    feat_rows, up_rim, stats = lax.optimization_barrier((feat_rows, up_rim, stats))
    feat_rim = exchange(feat_rows, "narrow")

    voxel_count = stats[2, 0] * group_width
    sums = group_sums(stats[:2], channels)
    mean = sums[0] / voxel_count
    rstd = lax.rsqrt(sums[1] / voxel_count - mean * mean + norm_eps)
    blank = jnp.zeros((channels,), f32)
    coef = jnp.stack([mean, rstd, scale, shift, blank + voxel_count, blank, blank, blank])

    grads, padded, shifted, hidden = weight_grad(occupancy, live, features, out_cotangent, up_rim, coef)
    grads, feat_rim = lax.optimization_barrier((grads, feat_rim))
    bias = conv_bias[None, :]
    hat, grad_sums, mixed = convs(
        occupancy, live, features, out_cotangent, padded, shifted, back_weight, coef, bias, hidden, feat_rim,
        forward_weight,
    )
    parts, rows, mixed = reduce_weights(grads, grad_sums, mixed)
    mixed = forward_conv(1, occupancy, live, features, hidden, feat_rim, forward_weight, coef, bias, mixed)
    weight_step, feature_grad = last_step(occupancy, coef, parts, features, hat, rows)
    return (mixed, feature_grad, weight_step.reshape(conv_weight.shape))


def solution(mesh):
    return jax.shard_map(
        local,
        mesh=mesh,
        in_specs=(
            P(("wide", "narrow"), None, None, None),
            P(("wide", "narrow"), None, None, None),
            P(("wide", "narrow"), None, None),
            P("wide", None),
            P("wide", None),
            P(),
            P(),
            P(),
            P(),
            P(),
            P(),
        ),
        out_specs=(
            P(("wide", "narrow"), None, None, None),
            P(("wide", "narrow"), None, None, None),
            P(),
        ),
        check_vma=False,
    )
```
